128 devices in a mesh: lat: 8 (over z, x_lo), lon: 16 (over x_hi, y, core).
Axes of the slice: x: 4 (x_hi: 2, x_lo: 2; x = x_hi * 2 + x_lo), y: 4, z: 4, core: 2. Of those that a mesh axis runs over, the one named last changes fastest.
Arguments:
- tracer_cot: float32 [50, 512, 2048], P(None, 'lat', 'lon'), may hold values from -6 to 6
- east_cot: float32 [50, 512, 2048], P(None, 'lat', 'lon'), may hold values from -3 to 3
- north_cot: float32 [50, 512, 2048], P(None, 'lat', 'lon'), may hold values from -3 to 3
- surface_cot: float32 [512, 2048], P('lat', 'lon'), may hold values from -60 to 60
- depth_levels: int32 [512, 2048], P('lat', 'lon'), may hold values from 0 to 50
- diffusivity: float32 [512, 2048], P('lat', 'lon'), may hold values from 0.03 to 0.2
- coriolis: float32 [512, 2048], P('lat', 'lon'), may hold values from -1 to 1
- storage: float32 [512, 2048], P('lat', 'lon'), may hold values from 0.5 to 5
- thickness: float32 [50], replicated, may hold values from 0.1 to 0.5
Outputs:
- tracer_adj: float32 [50, 512, 2048], P(None, 'lat', 'lon')
- east_adj: float32 [50, 512, 2048], P(None, 'lat', 'lon')
- north_adj: float32 [50, 512, 2048], P(None, 'lat', 'lon')
- surface_adj: float32 [512, 2048], P('lat', 'lon')
The draws below stay inside these ranges and needn't reach their ends.
All inputs are finite; a program needn't handle non-finite values.
Results may differ from the reference program's by a relative error of at most 0.0003.
Values sent between devices are 32-bit elements; how exact they have to be, the bound alone decides.
No kernel may reach another device: no remote copies, remote signals or barrier semaphores. Data moves between devices by JAX's collectives and lax.ppermute only.
A program may use at most 128 MiB of HBM per device.

```python
import math
import jax
import jax.numpy as jnp
from jax import lax

LEVELS = 50
ITERS = 4
NLAT = 512
NLON = 2048


def draw_surface_cot(key, part):
    key = jax.random.fold_in(key, 11)
    key_base, key_rows, key_cols = jax.random.split(key, 3)
    row_scale = jnp.exp(jax.random.uniform(key_rows, (NLAT, 1), jnp.float32, 0.0, math.log(10.0))) / 3.2
    col_scale = jnp.exp(jax.random.uniform(key_cols, (1, NLON), jnp.float32, 0.0, math.log(10.0))) / 3.2
    lat_share = jnp.arange(NLAT, dtype=jnp.float32)[:, None] / max(NLAT - 1, 1)
    rising = 1.0 + 2.0 * lat_share
    base_values = jnp.clip(jax.random.normal(key_base, (NLAT, NLON), jnp.float32), -4.0, 4.0)
    return base_values * row_scale * col_scale * rising / 3.0


def set_ends(values, key, low, top_value):
    dims = values.shape
    place = [jax.random.randint(jax.random.fold_in(key, axis), (), 0, dims[axis]) for axis in range(len(dims))]
    values = values.at[tuple(place)].set(low)
    longest = dims.index(max(dims))
    place[longest] = (place[longest] + 1) % dims[longest]
    return values.at[tuple(place)].set(top_value)


def block_levels(rng, shape, cuts, smallest, top_value):
    def one(position, shards_of):
        steps = jax.random.uniform(jax.random.fold_in(jax.random.fold_in(rng, 6), position), (shards_of,), jnp.float32, smallest / len(cuts), top_value / len(cuts))
        return jnp.repeat(jnp.exp(steps), shape[position] // shards_of).reshape((-1,) + (1,) * (len(shape) - position - 1))

    loudness = one(*cuts[0])
    for cut in cuts[1:]:
        loudness = loudness * one(*cut)
    return loudness


def normal_values(key, dims, deviation, most, cuts=(), kind=jnp.bfloat16):
    gain = block_levels(key, dims, cuts, -0.22, 0.18) if cuts else 1.0
    result = jax.random.normal(key, dims, jnp.float32) * deviation * gain
    return jnp.minimum(jnp.maximum(result, -most), most).astype(kind)


def setup_inputs(seed: int = 0) -> dict:
    arg_keys = jax.random.split(jax.random.key(seed), 10)
    return {
        "tracer_cot": normal_values(arg_keys[0], (LEVELS, NLAT, NLON), 1.0, 6.0, ((1, 8), (2, 16)), jnp.float32),
        "east_cot": normal_values(arg_keys[1], (LEVELS, NLAT, NLON), 0.5, 3.0, ((1, 8), (2, 16)), jnp.float32),
        "north_cot": normal_values(arg_keys[2], (LEVELS, NLAT, NLON), 0.5, 3.0, ((1, 8), (2, 16)), jnp.float32),
        "surface_cot": draw_surface_cot(jax.random.fold_in(arg_keys[9], 71), 0),
        "depth_levels": set_ends(jax.random.randint(arg_keys[4], (NLAT, NLON), 0, LEVELS + 1), jax.random.fold_in(arg_keys[4], 1), 0, LEVELS).astype(jnp.int32),
        "diffusivity": jnp.clip(jnp.exp(math.log(0.2) - 1.89712 * jax.random.uniform(arg_keys[5], (NLAT, NLON), jnp.float32) ** block_levels(arg_keys[5], (NLAT, NLON), ((0, 8), (1, 16)), -0.2, 0.2)), 0.03, 0.2),
        "coriolis": jnp.clip(jax.random.uniform(arg_keys[6], (NLAT, NLON), jnp.float32, -1.0, 1.0) * block_levels(arg_keys[6], (NLAT, NLON), ((0, 8), (1, 16)), -0.4, 0.0), -1.0, 1.0),
        "storage": jnp.clip(jnp.exp(math.log(5.0) - 2.3025851 * jax.random.uniform(arg_keys[7], (NLAT, NLON), jnp.float32) ** block_levels(arg_keys[7], (NLAT, NLON), ((0, 8), (1, 16)), -0.2, 0.2)), 0.5, 5.0),
        "thickness": jnp.clip(jnp.exp(jax.random.uniform(arg_keys[8], (LEVELS,), jnp.float32, math.log(0.1), math.log(0.5))), 0.1, 0.5),
    }


def east_of(values):
    return jnp.roll(values, -1, axis=-1)


def west_of(values):
    return jnp.roll(values, 1, axis=-1)


def north_of(values):
    return jnp.concatenate([values[..., 1:, :], values[..., -1:, ::-1]], axis=-2)


def south_of(values):
    return jnp.concatenate([jnp.zeros_like(values[..., :1, :]), values[..., :-1, :]], axis=-2)


def level_faces(level, depth_levels, diffusivity, top_rows):
    wet_mask = (depth_levels > level).astype(jnp.float32)
    wet_east = east_of(wet_mask)
    wet_north = north_of(wet_mask)
    face_east = diffusivity * wet_mask * wet_east
    face_west = west_of(face_east)
    face_north = (diffusivity + top_rows * north_of(diffusivity)) * wet_mask * wet_north
    face_south = south_of(diffusivity * wet_mask * wet_north)
    return wet_mask, wet_east, wet_north, (face_east, face_west, face_north, face_south)


def diffuse(values, wet_mask, coeffs):
    face_east, face_west, face_north, face_south = coeffs
    flows = face_east * (values - east_of(values)) + face_west * (values - west_of(values))
    flows = flows + face_north * (values - north_of(values)) + face_south * (values - south_of(values))
    return wet_mask * values - flows


def reference(tracer_cot, east_cot, north_cot, surface_cot, depth_levels, diffusivity, coriolis, storage, thickness):
    row_index = jnp.arange(surface_cot.shape[0], dtype=jnp.int32)[:, None]
    top_rows = jnp.broadcast_to((row_index == surface_cot.shape[0] - 1).astype(jnp.float32), surface_cot.shape)
    levels = jnp.arange(LEVELS, dtype=jnp.int32)
    zero_plane = jnp.zeros(surface_cot.shape, jnp.float32)

    def first_pass(carry, inputs):
        level, tracer_level, east_level, north_level, level_thickness = inputs
        east_sum, north_sum, east_depth, north_depth = carry
        wet_mask, wet_east, wet_north, coeffs = level_faces(level, depth_levels, diffusivity, top_rows)
        tracer_level_adj = diffuse(tracer_level, wet_mask, coeffs)
        east_face = wet_mask * wet_east
        north_face = wet_mask * wet_north
        carry = (east_sum + east_face * east_level, north_sum + north_face * north_level,
                 east_depth + level_thickness * east_face, north_depth + level_thickness * north_face)
        return carry, tracer_level_adj

    sums, tracer_adj = lax.scan(first_pass, (zero_plane, zero_plane, zero_plane, zero_plane),
                                (levels, tracer_cot, east_cot, north_cot, thickness))
    east_sum, north_sum, east_depth, north_plain = sums
    source = surface_cot + east_sum - west_of(east_sum) + north_sum - south_of(north_sum) - top_rows * north_of(north_sum)
    north_depth = north_plain * (1.0 + top_rows)
    east_depth_w = west_of(east_depth)
    north_depth_s = south_of(north_plain)
    inverse = 1.0 / (storage + east_depth + east_depth_w + north_depth + north_depth_s)

    def operate(values):
        total = storage * values + east_depth * (values - east_of(values)) + east_depth_w * (values - west_of(values))
        return total + north_depth * (values - north_of(values)) + north_depth_s * (values - south_of(values))

    solution = zero_plane
    residual = source
    precond = residual * inverse
    direction = precond
    scaled_norm = jnp.sum(residual * precond)
    for iteration in range(ITERS):
        applied = operate(direction)
        alpha_step = scaled_norm / jnp.sum(direction * applied)
        solution = solution + alpha_step * direction
        residual = residual - alpha_step * applied
        precond = residual * inverse
        next_norm = jnp.sum(residual * precond)
        direction = precond + (next_norm / scaled_norm) * direction
        scaled_norm = next_norm

    surface_adj = storage * solution
    east_flux = east_of(solution) - solution
    north_flux = north_of(solution) - solution

    def second_pass(carry, inputs):
        level, east_level, north_level, level_thickness = inputs
        wet_mask, wet_east, wet_north, coeffs = level_faces(level, depth_levels, diffusivity, top_rows)
        east_total = east_level + level_thickness * east_flux
        north_total = north_level + level_thickness * north_flux
        east_level_adj = diffuse(east_total, wet_mask, coeffs) - coriolis * wet_mask * north_total
        north_level_adj = diffuse(north_total, wet_mask, coeffs) + coriolis * wet_mask * east_total
        return carry, (east_level_adj, north_level_adj)

    unused, pair = lax.scan(second_pass, jnp.zeros((), jnp.float32), (levels, east_cot, north_cot, thickness))
    return tracer_adj, pair[0], pair[1], surface_adj
```

```python
import jax
import jax.numpy as jnp
from jax import lax
from jax.experimental import pallas as pl
from jax.experimental.pallas import tpu as pltpu
from jax.sharding import PartitionSpec as P

WIDE = 6
PAD = 8
SHIFTS = (1.0, 0.3, 1.7)
PARTS = 5
LANES = 128
BOTH = ("lat", "lon")
VMEM_BYTES = 24 * 1024 * 1024

DEPTH_AT, STORE_AT, SOURCE_AT, STRIP_AT, DIFF_AT = 64, 70, 76, 82, 88
LEVEL_ROWS = 56
RAW_AT = 3 * PAD
PAIR_AT = RAW_AT + LEVEL_ROWS
MESSAGE_ROWS = PAIR_AT + LEVEL_ROWS


def iota(shape, dim):
    return lax.broadcasted_iota(jnp.int32, shape, dim)


def turn(values, shift, dim):
    return pltpu.roll(values, shift % values.shape[dim], dim)


def pack_kernel(
    east, north, tracer, depth, storage, surf, diff,
    to_east, to_west, source, rows_out,
    px, py, m_east, m_north, first_east, first_west, second_east, second_west,
):
    step = pl.program_id(0)
    size, rows, lanes = east.shape
    lane = iota((rows, lanes), 1)
    row = iota((rows, lanes), 0)

    @pl.when(step == 0)
    def _():
        deep = depth[...].astype(jnp.float32)
        m_east[...] = jnp.where(lane == lanes - 1, 0.0, jnp.minimum(deep, turn(deep, -1, 1)))
        m_north[...] = jnp.where(row == rows - 1, 0.0, jnp.minimum(deep, turn(deep, -1, 0)))
        for ref in (px, py, first_east, first_west, second_east, second_west):
            ref[...] = jnp.zeros((rows, lanes), jnp.float32)
        rows_out[...] = jnp.zeros(rows_out.shape, jnp.float32)

    levels = [step * size + t for t in range(size)]
    for number, ref in enumerate((east, north, tracer)):
        for t, level in enumerate(levels):
            rows_out[number, pl.ds(level, 1), :] = ref[t, rows - 1 : rows, :]
            rows_out[3 + number, pl.ds(level, 1), :] = ref[t, 0:1, :]
    for ref, limit, total in ((east, m_east, px), (north, m_north, py)):
        bound = limit[...]
        acc = total[...]
        for t, level in enumerate(levels):
            acc = acc + jnp.where(level.astype(jnp.float32) < bound, ref[t], 0.0)
        total[...] = acc
    for ref, start, low, high in (
        (east, 0, first_west, first_east),
        (north, 50, first_west, first_east),
        (tracer, 0, second_west, second_east),
    ):
        left, right = low[...], high[...]
        for t, level in enumerate(levels):
            here = lane == level + start
            values = ref[t]
            left = jnp.where(here, values[:, 0:1], left)
            right = jnp.where(here, values[:, lanes - 1 :], right)
        low[...] = left
        high[...] = right

    @pl.when(step == pl.num_programs(0) - 1)
    def _():
        plane = surf[...] + px[...] - turn(px[...], 1, 1) + py[...] - turn(py[...], 1, 0)
        source[...] = plane
        deep = depth[...].astype(jnp.float32)
        planes = (
            (deep, DEPTH_AT), (storage[...], STORE_AT), (plane, SOURCE_AT), (rows_out[1], STRIP_AT)
        )

        def put(target, values, start, place, count):
            moved = turn(values, place - start, 1)
            return jnp.where((lane >= place) & (lane < place + count), moved, target)

        for ref, first, second, start in (
            (to_east, first_east, second_east, lanes - WIDE), (to_west, first_west, second_west, 0)
        ):
            tile = second[...]
            for values, place in planes:
                tile = put(tile, values, start, place, WIDE)
            tile = put(tile, diff[...], lanes - 1, DIFF_AT, 1)
            ref[:, :lanes] = first[...]
            ref[:, lanes:] = tile


def stitch_kernel(
    from_west, from_east, to_east, depth, storage, source, diff, rows_in,
    wide, face_west, message_a, message_b,
):
    rows, lanes = depth.shape
    lane = iota((rows, lanes), 1)
    left_tile, right_tile = from_west[:, lanes:], from_east[:, lanes:]

    def side(place):
        right = turn(right_tile, -place, 1)
        left = turn(left_tile, lanes - WIDE - place, 1)
        return jnp.where(lane < WIDE, right, jnp.where(lane >= lanes - WIDE, left, 0.0))

    deep, deep_side = depth[...].astype(jnp.float32), side(DEPTH_AT)
    store, store_side = storage[...], side(STORE_AT)
    plane, plane_side = source[...], side(SOURCE_AT)
    strip = side(STRIP_AT)
    level = lane.astype(jnp.float32)
    bound = jnp.minimum(deep[:, lanes - 1 :], deep_side[:, 0:1])
    flux_east = jnp.sum(
        jnp.where(level < bound, to_east[:, :lanes], 0.0), axis=1, keepdims=True
    )
    bound = jnp.minimum(deep_side[:, lanes - 1 :], deep[:, 0:1])
    flux_west = jnp.sum(
        jnp.where(level < bound, from_west[:, :lanes], 0.0), axis=1, keepdims=True
    )
    first, last = lane == 0, lane == lanes - 1
    plane = plane + jnp.where(last, flux_east, 0.0) - jnp.where(first, flux_west, 0.0)
    plane_side = plane_side - jnp.where(first, flux_east, 0.0) + jnp.where(last, flux_west, 0.0)
    top_rows = rows_in[1]
    both = ((deep, deep_side), (store, store_side), (plane, plane_side), (top_rows, strip))
    for number, (one, two) in enumerate(both):
        wide[number, :, :lanes] = one
        wide[number, :, lanes:] = two
    faces = diff[...]
    face_west[...] = jnp.where(first, turn(left_tile, -DIFF_AT, 1), turn(faces, 1, 1))

    def fill(ref, up):
        start = rows - PAD if up else 0
        for number, (one, two) in enumerate(both[:3]):
            ref[number * PAD : (number + 1) * PAD, :lanes] = one[start : start + PAD]
            ref[number * PAD : (number + 1) * PAD, lanes:] = two[start : start + PAD]
        base = 0 if up else 3
        ref[RAW_AT:PAIR_AT, :lanes] = rows_in[base + 1, :LEVEL_ROWS]
        ref[RAW_AT:PAIR_AT, lanes:] = strip[:LEVEL_ROWS]
        ref[PAIR_AT:, :lanes] = rows_in[base, :LEVEL_ROWS]
        ref[PAIR_AT:, lanes:] = rows_in[base + 2, :LEVEL_ROWS]
        if up:
            ref[PAIR_AT - 1 : PAIR_AT, :lanes] = faces[rows - 1 :]

    even = lax.rem(lax.axis_index("lat"), 2) == 0

    @pl.when(even)
    def _():
        fill(message_a, True)
        fill(message_b, False)

    @pl.when(jnp.logical_not(even))
    def _():
        fill(message_a, False)
        fill(message_b, True)


def level_kernel(
    from_west, from_east, wide, diff, face_west, coriolis, east, north, tracer,
    east_out, north_out, tracer_out,
    m_east, m_west, m_north, m_south,
):
    step = pl.program_id(0)
    size, rows, lanes = east.shape
    lane = iota((rows, lanes), 1)
    row = iota((rows, lanes), 0)
    first, last = lane == 0, lane == lanes - 1

    @pl.when(step == 0)
    def _():
        deep, beside = wide[0, :, :lanes], wide[0, :, lanes:]
        m_east[...] = jnp.minimum(deep, jnp.where(last, beside[:, 0:1], turn(deep, -1, 1)))
        m_west[...] = jnp.minimum(deep, jnp.where(first, beside[:, lanes - 1 :], turn(deep, 1, 1)))
        m_north[...] = jnp.where(row == rows - 1, 0.0, jnp.minimum(deep, turn(deep, -1, 0)))
        m_south[...] = jnp.where(row == 0, 0.0, jnp.minimum(deep, turn(deep, 1, 0)))

    for t in range(size):
        level = step * size + t
        height = level.astype(jnp.float32)
        deep = wide[0, :, :lanes]
        wet = height < deep
        has_east, has_west = height < m_east[...], height < m_west[...]
        has_north, has_south = height < m_north[...], height < m_south[...]
        face = diff[...]
        left_face = face_west[...]
        south_face = turn(face, 1, 0)

        def smooth(values, tile, start):
            cols_east = from_east[:, tile * lanes : (tile + 1) * lanes]
            cols_west = from_west[:, tile * lanes : (tile + 1) * lanes]
            east_halo = pltpu.roll(cols_east, lanes - 1 - start - level, 1)
            west_halo = pltpu.roll(cols_west, lanes - start - level, 1)
            east_side = jnp.where(last, east_halo, turn(values, -1, 1))
            west_side = jnp.where(first, west_halo, turn(values, 1, 1))
            ahead = jnp.where(has_east, values - east_side, 0.0)
            ahead = ahead + jnp.where(has_north, values - turn(values, -1, 0), 0.0)
            flows = face * ahead + jnp.where(has_west, left_face * (values - west_side), 0.0)
            flows = flows + jnp.where(has_south, south_face * (values - turn(values, 1, 0)), 0.0)
            return jnp.where(wet, values, 0.0) - flows

        spin = jnp.where(wet, coriolis[...], 0.0)
        east_out[t] = smooth(east[t], 0, 0) - spin * north[t]
        north_out[t] = smooth(north[t], 0, 50) + spin * east[t]
        tracer_out[t] = smooth(tracer[t], 1, 0)


def shifted(values):
    return turn(values, -1, 1), turn(values, 1, 1), turn(values, -1, 0), turn(values, 1, 0)


def basis_kernel(thickness, got_a, got_b, wide, gram, basis, depth_wide, halo):
    rows, lanes = wide.shape[1], wide.shape[2] // 2
    lat = lax.axis_index("lat")
    even = lax.rem(lat, 2) == 0
    at_top = lat == lax.axis_size("lat") - 1
    at_bottom = lat == 0

    @pl.when(at_top)
    def _():
        back = lanes - 1 - iota((PAD, lanes), 1)
        for number in range(MESSAGE_ROWS // PAD):
            for tile in range(2):
                values = got_b[number * PAD : (number + 1) * PAD, tile * lanes : (tile + 1) * lanes]
                values = jnp.take_along_axis(values, back, axis=1)
                if number < 3:
                    values = jnp.concatenate(
                        [values[i : i + 1] for i in range(PAD - 1, -1, -1)], axis=0
                    )
                halo[0, number * PAD : (number + 1) * PAD, tile * lanes : (tile + 1) * lanes] = values

    @pl.when(jnp.logical_not(at_top))
    def _():
        halo[0] = jnp.where(even, got_a[...], got_b[...])

    halo[1] = jnp.where(at_bottom, 0.0, jnp.where(even, got_b[...], got_a[...]))

    def whole(number):
        place = slice(number * PAD, (number + 1) * PAD)
        return jnp.concatenate([halo[1, place], wide[number], halo[0, place]], axis=0)

    deep, store, plane = whole(0), whole(1), whole(2)
    depth_wide[...] = deep
    full = deep.shape
    row = iota(full, 0)
    core_end = PAD + rows
    level = iota((LEVEL_ROWS, full[1]), 0).astype(jnp.float32)
    bound = jnp.minimum(deep[core_end - 1 : core_end], deep[core_end : core_end + 1])
    edge = wide[3, :LEVEL_ROWS] - jnp.where(at_top, halo[0, RAW_AT:PAIR_AT], 0.0)
    flux = jnp.sum(jnp.where(level < bound, edge, 0.0), axis=0, keepdims=True)
    plane = plane + jnp.where(row == core_end - 1, flux, 0.0) - jnp.where(row == core_end, flux, 0.0)
    bound = jnp.minimum(deep[PAD - 1 : PAD], deep[PAD : PAD + 1])
    flux = jnp.sum(jnp.where(level < bound, halo[1, RAW_AT:PAIR_AT], 0.0), axis=0, keepdims=True)
    plane = plane + jnp.where(row == PAD - 1, flux, 0.0) - jnp.where(row == PAD, flux, 0.0)

    place = iota((PAD, lanes), 1)
    table = jnp.zeros((PAD, lanes), jnp.float32)
    for number in range(thickness.shape[0]):
        table = table + jnp.where(place > number, thickness[number], 0.0)

    def column(bound):
        index = bound.astype(jnp.int32)
        return jnp.concatenate(
            [
                jnp.concatenate(
                    [
                        jnp.take_along_axis(
                            table, index[i : i + PAD, j : j + lanes], axis=1
                        )
                        for j in range(0, full[1], lanes)
                    ],
                    axis=1,
                )
                for i in range(0, full[0], PAD)
            ],
            axis=0,
        )

    beside, _, above, _ = shifted(deep)
    to_east = column(jnp.minimum(deep, beside))
    to_north = column(jnp.minimum(deep, above))
    to_north = jnp.where(at_top & (row == core_end - 1), 2.0, 1.0) * to_north
    to_west, to_south = turn(to_east, 1, 1), turn(to_north, 1, 0)
    diag = store + to_east + to_west + to_north + to_south
    there = diag > 0.0
    inverse = jnp.where(there, 1.0 / jnp.where(there, diag, 1.0), 0.0)

    def operate(values):
        east_side, west_side, north_side, south_side = shifted(values)
        total = (
            store * values + to_east * (values - east_side) + to_west * (values - west_side)
        )
        return total + to_north * (values - north_side) + to_south * (values - south_side)

    vectors, images = [plane * inverse], []
    for number in range(4):
        images.append(operate(vectors[-1]))
        if number < 3:
            vectors.append(images[-1] * inverse - SHIFTS[number] * vectors[-1])
    for number in range(4):
        basis[number] = vectors[number]

    def core(values):
        return values[PAD:core_end, :lanes]

    sums = []
    for i in range(4):
        for j in range(i, 4):
            sums.append(core(vectors[i]) * core(images[j]))
    for i in range(4):
        sums.append(core(vectors[i]) * core(plane))
    sums = [jnp.sum(item, axis=0, keepdims=True) for item in sums]
    sums = sums + [jnp.zeros((1, lanes), jnp.float32)] * (16 - len(sums))
    sums = jnp.sum(jnp.concatenate(sums, axis=0), axis=1, keepdims=True)
    same = iota((16, lanes), 0) == iota((16, lanes), 1)
    line = jnp.sum(jnp.where(same, sums, 0.0), axis=0, keepdims=True)
    gram[...] = jnp.broadcast_to(line, gram.shape)


def solve(line):
    entry = [line[:, i : i + 1] for i in range(14)]
    system = [[None] * 5 for _ in range(4)]
    for i in range(4):
        for j in range(i, 4):
            system[i][j] = entry.pop(0)
    for i in range(4):
        system[i][4] = entry.pop(0)
    factor, part = {}, []
    for k in range(4):
        pivot = system[k][k]
        usable = pivot > 0.0
        scale = jnp.where(usable, 1.0 / jnp.where(usable, pivot, 1.0), 0.0)
        part.append(system[k][4] * scale)
        for i in range(k + 1, 4):
            factor[i, k] = system[k][i] * scale
            for j in range(i, 5):
                system[i][j] = system[i][j] - factor[i, k] * system[k][j]
    for k in range(2, -1, -1):
        for i in range(k + 1, 4):
            part[k] = part[k] - factor[i, k] * part[i]
    return part


def final_kernel(
    thickness, totals, basis, depth_wide, storage, diff, face_west, coriolis, halo, rows_in,
    east, north, tracer_in,
    tracer, east_out, north_out, surface,
    planes, fixes, edges, load_sems, store_sems,
):
    step = pl.program_id(0)
    size, rows, lanes = east.shape
    levels_count = edges.shape[1]
    core_end = PAD + rows

    def edge_copy(number, back):
        inside = tracer.at[:, pl.ds(number * (rows - PAD), PAD), :]
        if back:
            return pltpu.make_async_copy(edges.at[number], inside, store_sems.at[number])
        return pltpu.make_async_copy(inside, edges.at[number], load_sems.at[number])

    @pl.when(step == 0)
    def _():
        edge_copy(0, False).start()
        edge_copy(1, False).start()
        at_top = lax.axis_index("lat") == lax.axis_size("lat") - 1
        row = iota((rows, lanes), 0)
        deep = depth_wide[...]
        bounds = [jnp.minimum(deep, item)[PAD:core_end, :lanes] for item in shifted(deep)]
        face = diff[...]
        north_face = face + jnp.where(
            at_top & (row == rows - 1), halo[0, PAIR_AT - 1 : PAIR_AT, :lanes], 0.0
        )
        south_face = jnp.where(row == 0, halo[1, PAIR_AT - 1 : PAIR_AT, :lanes], turn(face, 1, 0))
        faces = (face, face_west[...], north_face, south_face)
        planes[0] = deep[PAD:core_end, :lanes]
        for number in range(4):
            planes[1 + number] = bounds[number]
        level = iota((LEVEL_ROWS, lanes), 0).astype(jnp.float32)
        for side, line in ((0, rows - 1), (1, 0)):
            bound = bounds[2 + side][line : line + 1]
            weight = faces[2 + side][line : line + 1]
            outer = (
                halo[side, PAIR_AT:, :lanes],
                halo[side, RAW_AT:PAIR_AT, :lanes],
                halo[side, PAIR_AT:, lanes:],
            )
            for number in range(3):
                inner = rows_in[3 * side + number, :LEVEL_ROWS]
                fixes[3 * side + number] = jnp.where(
                    level < bound, weight * (outer[number] - inner), 0.0
                )
        parts = solve(jnp.sum(totals[...], axis=0, keepdims=True))
        height = parts[0] * basis[0]
        for number in range(1, 4):
            height = height + parts[number] * basis[number]
        surface[...] = storage[...] * height[PAD:core_end, :lanes]
        full_row = iota(height.shape, 0)
        folded = at_top & (full_row == core_end)
        to_east, to_west, to_north, to_south = shifted(height)
        slope_x = jnp.where(folded, to_west, to_east) - height
        slope_y = jnp.where(folded, to_south, to_north) - height
        inner_x, inner_y = slope_x[PAD:core_end, :lanes], slope_y[PAD:core_end, :lanes]
        spin = coriolis[...]
        planes[5] = inner_x - spin * inner_y
        planes[6] = inner_y + spin * inner_x
        for start, slope, inner in ((7, slope_x, inner_x), (11, slope_y, inner_y)):
            for number, item in enumerate(shifted(slope)):
                planes[start + number] = faces[number] * (inner - item[PAD:core_end, :lanes])
        for number, line in ((0, 0), (1, PAD - 1)):
            edge_copy(number, False).wait()
            fix = fixes[3 * (1 - number) + 2]
            edges[number, :, line, :] = edges[number, :, line, :] + fix[:levels_count]
            edge_copy(number, True).start()

    line = iota((PAD, lanes), 0)
    for tile in range(rows // PAD):
        place = slice(tile * PAD, (tile + 1) * PAD)
        own = [planes[number, place] for number in range(15)]
        for t in range(size):
            level = step * size + t
            height = level.astype(jnp.float32)
            open_sides = [height < own[number] for number in range(5)]
            for out, values, base, start, number in (
                (east_out, east, 5, 7, 0), (north_out, north, 6, 11, 1)
            ):
                change = jnp.where(open_sides[0], own[base], 0.0)
                for side in range(4):
                    change = change - jnp.where(open_sides[1 + side], own[start + side], 0.0)
                result = values[t, place] + thickness[level] * change
                if tile == 0:
                    fix = fixes[3 + number, pl.ds(level, 1), :]
                    result = result + jnp.where(line == 0, fix, 0.0)
                if tile == rows // PAD - 1:
                    fix = fixes[number, pl.ds(level, 1), :]
                    result = result + jnp.where(line == PAD - 1, fix, 0.0)
                out[t, place] = result

    @pl.when(step == pl.num_programs(0) - 1)
    def _():
        edge_copy(0, True).wait()
        edge_copy(1, True).wait()


def swaps(lats, lons, odd):
    pairs = []
    for lat in range(lats):
        for lon in range(lons):
            other = lat + 1 if lat % 2 == odd else lat - 1
            if other < 0:
                continue
            if other == lats:
                pairs.append((lat * lons + lon, lat * lons + lons - 1 - lon))
            else:
                pairs.append((lat * lons + lon, other * lons + lon))
    return pairs


def local(
    tracer_cot, east_cot, north_cot, surface_cot, depth_levels, diffusivity, coriolis, storage,
    thickness,
):
    levels, rows, lanes = tracer_cot.shape
    size = levels // PARTS
    lats, lons = lax.axis_size("lat"), lax.axis_size("lon")
    floats = lambda *shape: jax.ShapeDtypeStruct(shape, jnp.float32)
    scratch = lambda *shape: pltpu.VMEM(shape, jnp.float32)
    whole = lambda *shape: pl.BlockSpec(shape, lambda *_: (0,) * len(shape))
    block = pl.BlockSpec((size, rows, lanes), lambda i: (i, 0, 0))
    plane = whole(rows, lanes)
    pair = whole(rows, 2 * lanes)
    scalars = pl.BlockSpec(memory_space=pltpu.SMEM)
    anywhere = pl.BlockSpec(memory_space=pl.ANY)
    params = pltpu.CompilerParams(vmem_limit_bytes=VMEM_BYTES)
    full = (rows + 2 * PAD, 2 * lanes)
    message = (MESSAGE_ROWS, 2 * lanes)

    to_east, to_west, source, edge_rows = pl.pallas_call(
        pack_kernel,
        grid=(PARTS,),
        in_specs=[block] * 3 + [plane] * 4,
        out_specs=[pair, pair, plane, whole(6, rows, lanes)],
        out_shape=[floats(rows, 2 * lanes)] * 2 + [floats(rows, lanes), floats(6, rows, lanes)],
        scratch_shapes=[scratch(rows, lanes)] * 8,
        compiler_params=params,
        name="pack",
    )(east_cot, north_cot, tracer_cot, depth_levels, storage, surface_cot, diffusivity)

    from_west = lax.ppermute(to_east, "lon", [(i, (i + 1) % lons) for i in range(lons)])
    from_east = lax.ppermute(to_west, "lon", [(i, (i - 1) % lons) for i in range(lons)])

    wide, face_west, message_a, message_b = pl.pallas_call(
        stitch_kernel,
        grid=(1,),
        in_specs=[pair] * 3 + [plane] * 4 + [whole(6, rows, lanes)],
        out_specs=[whole(4, rows, 2 * lanes), plane, whole(*message), whole(*message)],
        out_shape=[
            floats(4, rows, 2 * lanes), floats(rows, lanes), floats(*message), floats(*message)
        ],
        compiler_params=params,
        name="stitch",
    )(from_west, from_east, to_east, depth_levels, storage, source, diffusivity, edge_rows)

    got_a = lax.ppermute(message_a, BOTH, swaps(lats, lons, 0))
    got_b = lax.ppermute(message_b, BOTH, swaps(lats, lons, 1))

    east_part, north_part, tracer_part = pl.pallas_call(
        level_kernel,
        grid=(PARTS,),
        in_specs=[pair, pair, whole(4, rows, 2 * lanes)] + [plane] * 3 + [block] * 3,
        out_specs=[block] * 3,
        out_shape=[floats(levels, rows, lanes)] * 3,
        scratch_shapes=[scratch(rows, lanes)] * 4,
        compiler_params=params,
        cost_estimate=pl.CostEstimate(
            flops=60 * levels * rows * lanes, bytes_accessed=24 * levels * rows * lanes,
            transcendentals=0,
        ),
        name="level",
    )(from_west, from_east, wide, diffusivity, face_west, coriolis, east_cot, north_cot, tracer_cot)

    gram, basis, depth_wide, halo = pl.pallas_call(
        basis_kernel,
        grid=(1,),
        in_specs=[scalars, whole(*message), whole(*message), whole(4, rows, 2 * lanes)],
        out_specs=[
            whole(lats * lons, lanes), whole(4, *full), whole(*full), whole(2, *message)
        ],
        out_shape=[
            floats(lats * lons, lanes), floats(4, *full), floats(*full), floats(2, *message)
        ],
        compiler_params=params,
        name="basis",
    )(thickness, got_a, got_b, wide)

    totals = lax.all_to_all(gram, BOTH, 0, 0, tiled=True)

    tracer_adj, east_adj, north_adj, surface_adj = pl.pallas_call(
        final_kernel,
        grid=(PARTS,),
        in_specs=[scalars, whole(lats * lons, lanes), whole(4, *full), whole(*full)]
        + [plane] * 4
        + [whole(2, *message), whole(6, rows, lanes), block, block, anywhere],
        out_specs=[anywhere, block, block, plane],
        out_shape=[floats(levels, rows, lanes)] * 3 + [floats(rows, lanes)],
        scratch_shapes=[
            scratch(15, rows, lanes),
            scratch(6, LEVEL_ROWS, lanes),
            scratch(2, levels, PAD, lanes),
            pltpu.SemaphoreType.DMA((2,)),
            pltpu.SemaphoreType.DMA((2,)),
        ],
        input_output_aliases={12: 0},
        compiler_params=params,
        name="final",
    )(
        thickness, totals, basis, depth_wide, storage, diffusivity, face_west, coriolis, halo,
        edge_rows, east_part, north_part, tracer_part,
    )
    return tracer_adj, east_adj, north_adj, surface_adj


def solution(mesh):
    field, plane = P(None, "lat", "lon"), P("lat", "lon")
    return jax.shard_map(
        local,
        mesh=mesh,
        in_specs=(field, field, field, plane, plane, plane, plane, plane, P()),
        out_specs=(field, field, field, plane),
        check_vma=False,
    )
```

```python
import jax
import jax.numpy as jnp
from jax import lax
from jax.experimental import pallas as pl
from jax.experimental.pallas import tpu as pltpu
from jax.sharding import PartitionSpec as P

WIDE = 6
PAD = 8
SHIFTS = (1.0, 0.3, 1.7)
PARTS = 5
LANES = 128
BOTH = ("lat", "lon")
VMEM_BYTES = 32 * 1024 * 1024

DEPTH_AT, STORE_AT, SOURCE_AT, STRIP_AT, DIFF_AT = 100, 106, 112, 118, 124
LEVEL_ROWS = 56
RAW_AT = 3 * PAD
PAIR_AT = RAW_AT + LEVEL_ROWS
MESSAGE_ROWS = PAIR_AT + LEVEL_ROWS


def iota(shape, dim):
    return lax.broadcasted_iota(jnp.int32, shape, dim)


def turn(values, shift, dim):
    return pltpu.roll(values, shift % values.shape[dim], dim)


def pack_kernel(
    east_in, north_in, tracer_in, depth_in, storage_in, surf_in, diff_in, spin_in,
    message_0, message_1, planes, rows_out, edges, east, north, tracer,
    depth, surf, px, py, bounds, field_sems, plane_sems,
):
    levels, rows, lanes = east.shape
    size = levels // PARTS
    sources, fields = (east_in, north_in, tracer_in), (east, north, tracer)

    def part_copy(number, part):
        place = pl.ds(part * size, size)
        return pltpu.make_async_copy(
            sources[number].at[place], fields[number].at[place], field_sems.at[number, part]
        )

    moves = [
        pltpu.make_async_copy(source, target, plane_sems.at[number])
        for number, (source, target) in enumerate(
            (
                (depth_in, depth), (storage_in, planes.at[1]), (surf_in, surf),
                (diff_in, planes.at[2]), (spin_in, planes.at[4]),
            )
        )
    ]
    for move in moves:
        move.start()
    for part in range(PARTS):
        for number in range(3):
            part_copy(number, part).start()
    rows_out[:, levels - levels % PAD :] = jnp.zeros((6, rows - levels + levels % PAD, lanes), jnp.float32)
    px[...] = jnp.zeros((rows, lanes), jnp.float32)
    py[...] = jnp.zeros((rows, lanes), jnp.float32)
    edges[...] = jnp.zeros((3, rows, lanes), jnp.float32)
    for move in moves:
        move.wait()
    lane = iota((rows, lanes), 1)
    row = iota((rows, lanes), 0)
    deep = depth[...].astype(jnp.float32)
    planes[0] = deep
    bounds[0] = jnp.where(lane == lanes - 1, 0.0, jnp.minimum(deep, turn(deep, -1, 1)))
    bounds[1] = jnp.where(row == rows - 1, 0.0, jnp.minimum(deep, turn(deep, -1, 0)))
    pair_lane = lax.shift_right_logical(iota((PAD, lanes), 1), 1)

    def part_step(part, carry):
        for number in range(3):
            part_copy(number, part).wait()
        for t in range(size):
            level = part * size + t
            for number, ref in enumerate(fields):
                rows_out[number, pl.ds(level, 1), :] = ref[level, rows - 1 : rows, :]
                rows_out[3 + number, pl.ds(level, 1), :] = ref[level, 0:1, :]
        for tile in range(rows // PAD):
            place = slice(tile * PAD, (tile + 1) * PAD)
            sum_x, sum_y = px[place], py[place]
            limit_x, limit_y = bounds[0, place], bounds[1, place]
            ends = [edges[number, place] for number in range(3)]
            for t in range(size):
                level = part * size + t
                height = level.astype(jnp.float32)
                here = pair_lane == level
                values = [ref[level, place] for ref in fields]
                for number in range(3):
                    moved = pltpu.roll(values[number], 2 * level + 1, 1)
                    ends[number] = jnp.where(here, moved, ends[number])
                sum_x = sum_x + jnp.where(height < limit_x, values[0], 0.0)
                sum_y = sum_y + jnp.where(height < limit_y, values[1], 0.0)
            px[place], py[place] = sum_x, sum_y
            for number in range(3):
                edges[number, place] = ends[number]
        return carry

    lax.fori_loop(0, PARTS, part_step, 0)
    plane = surf[...] + px[...] - turn(px[...], 1, 1) + py[...] - turn(py[...], 1, 0)
    planes[3] = plane
    odd_lane = lax.rem(lane, 2) == 1

    def put(target, values, start, place, count):
        moved = turn(values, place - start, 1)
        return jnp.where((lane >= place) & (lane < place + count), moved, target)

    def fill(ref, eastward):
        if eastward:
            ref[:, :lanes] = jnp.where(odd_lane, turn(edges[1], 1, 1), edges[0])
        else:
            ref[:, :lanes] = jnp.where(odd_lane, edges[0], turn(edges[1], -1, 1))
        start = lanes - WIDE if eastward else 0
        tile = edges[2]
        for values, place in (
            (deep, DEPTH_AT), (planes[1], STORE_AT), (plane, SOURCE_AT), (rows_out[1], STRIP_AT)
        ):
            tile = put(tile, values, start, place, WIDE)
        ref[:, lanes:] = put(tile, planes[2], lanes - 1, DIFF_AT, 1)

    even = lax.rem(lax.axis_index("lon"), 2) == 0

    @pl.when(even)
    def _():
        fill(message_0, True)
        fill(message_1, False)

    @pl.when(jnp.logical_not(even))
    def _():
        fill(message_0, False)
        fill(message_1, True)


def received(got_0, got_1):
    even = lax.rem(lax.axis_index("lon"), 2) == 0
    one, two = got_0[...], got_1[...]
    return jnp.where(even, two, one), jnp.where(even, one, two)


def stitch_kernel(
    got_0, got_1, planes, rows_in, edges,
    wide, face_west, message_a, message_b,
):
    rows, lanes = planes.shape[1:]
    from_west, from_east = received(got_0, got_1)
    lane = iota((rows, lanes), 1)
    left_tile, right_tile = from_west[:, lanes:], from_east[:, lanes:]

    def side(place):
        right = turn(right_tile, -place, 1)
        left = turn(left_tile, lanes - WIDE - place, 1)
        return jnp.where(lane < WIDE, right, jnp.where(lane >= lanes - WIDE, left, 0.0))

    deep, deep_side = planes[0], side(DEPTH_AT)
    store, store_side = planes[1], side(STORE_AT)
    plane, plane_side = planes[3], side(SOURCE_AT)
    strip = side(STRIP_AT)
    level = lax.shift_right_logical(lane, 1).astype(jnp.float32)
    even_lane = lax.rem(lane, 2) == 0

    def flux(values, bound):
        used = even_lane & (level < bound)
        return jnp.sum(jnp.where(used, values, 0.0), axis=1, keepdims=True)

    flux_east = flux(edges[0], jnp.minimum(deep[:, lanes - 1 :], deep_side[:, 0:1]))
    flux_west = flux(from_west[:, :lanes], jnp.minimum(deep_side[:, lanes - 1 :], deep[:, 0:1]))
    first, last = lane == 0, lane == lanes - 1
    plane = plane + jnp.where(last, flux_east, 0.0) - jnp.where(first, flux_west, 0.0)
    plane_side = plane_side - jnp.where(first, flux_east, 0.0) + jnp.where(last, flux_west, 0.0)
    both = ((deep, deep_side), (store, store_side), (plane, plane_side), (rows_in[1], strip))
    for number, (one, two) in enumerate(both):
        wide[number, :, :lanes] = one
        wide[number, :, lanes:] = two
    faces = planes[2]
    face_west[...] = jnp.where(first, turn(left_tile, -DIFF_AT, 1), turn(faces, 1, 1))

    def fill(ref, up):
        start = rows - PAD if up else 0
        for number, (one, two) in enumerate(both[:3]):
            ref[number * PAD : (number + 1) * PAD, :lanes] = one[start : start + PAD]
            ref[number * PAD : (number + 1) * PAD, lanes:] = two[start : start + PAD]
        base = 0 if up else 3
        ref[RAW_AT:PAIR_AT, :lanes] = rows_in[base + 1, :LEVEL_ROWS]
        ref[RAW_AT:PAIR_AT, lanes:] = strip[:LEVEL_ROWS]
        ref[PAIR_AT:, :lanes] = rows_in[base, :LEVEL_ROWS]
        ref[PAIR_AT:, lanes:] = rows_in[base + 2, :LEVEL_ROWS]
        if up:
            ref[PAIR_AT - 1 : PAIR_AT, :lanes] = faces[rows - 1 :]

    even = lax.rem(lax.axis_index("lat"), 2) == 0

    @pl.when(even)
    def _():
        fill(message_a, True)
        fill(message_b, False)

    @pl.when(jnp.logical_not(even))
    def _():
        fill(message_a, False)
        fill(message_b, True)


def level_kernel(
    got_0, got_1, wide, planes, face_west, edges, east, north, tracer,
    east_out, north_out, tracer_out,
    bounds, sides,
):
    levels, rows, lanes = east.shape
    from_west, from_east = received(got_0, got_1)
    lane = iota((rows, lanes), 1)
    row = iota((rows, lanes), 0)
    deep, beside = wide[0, :, :lanes], wide[0, :, lanes:]
    bounds[0] = jnp.where(lane == lanes - 1, 0.0, jnp.minimum(deep, turn(deep, -1, 1)))
    bounds[1] = jnp.where(row == rows - 1, 0.0, jnp.minimum(deep, turn(deep, -1, 0)))
    level = lax.shift_right_logical(lane, 1).astype(jnp.float32)
    odd_lane = lax.rem(lane, 2) == 1
    bound_east = jnp.minimum(deep[:, lanes - 1 :], beside[:, 0:1])
    bound_west = jnp.minimum(deep[:, 0:1], beside[:, lanes - 1 :])
    weight_east, weight_west = planes[2, :, lanes - 1 :], face_west[:, 0:1]
    weight = jnp.where(odd_lane, weight_west, weight_east)
    weight = jnp.where(level < jnp.where(odd_lane, bound_west, bound_east), weight, 0.0)
    halos = (
        jnp.where(odd_lane, turn(from_west[:, :lanes], 1, 1), turn(from_east[:, :lanes], -1, 1)),
        jnp.where(odd_lane, from_west[:, :lanes], from_east[:, :lanes]),
        jnp.where(odd_lane, turn(from_west[:, lanes:], 1, 1), turn(from_east[:, lanes:], -1, 1)),
    )
    for number in range(3):
        sides[number] = weight * (halos[number] - edges[number])
    small_lane, line = iota((PAD, lanes), 1), iota((PAD, lanes), 0)
    rim = (small_lane == 0) | (small_lane == lanes - 1)
    first_line, last_line = line == 0, line == PAD - 1
    fields, outs = (east, north, tracer), (east_out, north_out, tracer_out)
    tiles = rows // PAD

    def level_step(level, carry):
        height = level.astype(jnp.float32)
        values = [ref[level, :PAD] for ref in fields]
        lifted = [turn(item, -1, 0) for item in values]
        below = [jnp.zeros((PAD, lanes), jnp.float32)] * 3
        for tile in range(tiles):
            place = slice(tile * PAD, (tile + 1) * PAD)
            wet = height < planes[0, place]
            face = planes[2, place]
            face_east = jnp.where(height < bounds[0, place], face, 0.0)
            face_north = jnp.where(height < bounds[1, place], face, 0.0)
            results = []
            for number in range(3):
                item = values[number]
                flux = face_east * (item - turn(item, -1, 1))
                if tile + 1 < tiles:
                    upper = fields[number][level, (tile + 1) * PAD : (tile + 2) * PAD]
                    upper_lifted = turn(upper, -1, 0)
                    above = jnp.where(last_line, upper_lifted, lifted[number])
                else:
                    upper, upper_lifted, above = item, lifted[number], lifted[number]
                rise = face_north * (item - above)
                moved = turn(rise, 1, 0)
                fall = jnp.where(first_line, below[number], moved)
                rim_part = pltpu.roll(sides[number, place], lanes - 1 - 2 * level + lanes, 1)
                result = jnp.where(wet, item, 0.0) + jnp.where(rim, rim_part, 0.0)
                results.append(result + (turn(flux, 1, 1) - flux) + (fall - rise))
                below[number] = moved
                values[number], lifted[number] = upper, upper_lifted
                if number < 2:
                    results.append(item)
            spin = jnp.where(wet, planes[4, place], 0.0)
            east_out[level, place] = results[0] - spin * results[3]
            north_out[level, place] = results[2] + spin * results[1]
            tracer_out[level, place] = results[4]
        return carry

    lax.fori_loop(0, levels, level_step, 0, unroll=2)


def shifted(values):
    return turn(values, -1, 1), turn(values, 1, 1), turn(values, -1, 0), turn(values, 1, 0)


def basis_kernel(thickness, got_a, got_b, wide, gram, basis, depth_wide, halo):
    rows, lanes = wide.shape[1], wide.shape[2] // 2
    lat = lax.axis_index("lat")
    even = lax.rem(lat, 2) == 0
    at_top = lat == lax.axis_size("lat") - 1
    at_bottom = lat == 0

    @pl.when(at_top)
    def _():
        back = lanes - 1 - iota((PAD, lanes), 1)
        for number in range(MESSAGE_ROWS // PAD):
            for tile in range(2):
                values = got_b[number * PAD : (number + 1) * PAD, tile * lanes : (tile + 1) * lanes]
                values = jnp.take_along_axis(values, back, axis=1)
                if number < 3:
                    values = jnp.concatenate(
                        [values[i : i + 1] for i in range(PAD - 1, -1, -1)], axis=0
                    )
                halo[0, number * PAD : (number + 1) * PAD, tile * lanes : (tile + 1) * lanes] = values

    @pl.when(jnp.logical_not(at_top))
    def _():
        halo[0] = jnp.where(even, got_a[...], got_b[...])

    halo[1] = jnp.where(at_bottom, 0.0, jnp.where(even, got_b[...], got_a[...]))

    def whole(number):
        place = slice(number * PAD, (number + 1) * PAD)
        return jnp.concatenate([halo[1, place], wide[number], halo[0, place]], axis=0)

    deep, store, plane = whole(0), whole(1), whole(2)
    depth_wide[...] = deep
    full = deep.shape
    row = iota(full, 0)
    core_end = PAD + rows
    level = iota((LEVEL_ROWS, full[1]), 0).astype(jnp.float32)
    bound = jnp.minimum(deep[core_end - 1 : core_end], deep[core_end : core_end + 1])
    edge = wide[3, :LEVEL_ROWS] - jnp.where(at_top, halo[0, RAW_AT:PAIR_AT], 0.0)
    flux = jnp.sum(jnp.where(level < bound, edge, 0.0), axis=0, keepdims=True)
    plane = plane + jnp.where(row == core_end - 1, flux, 0.0) - jnp.where(row == core_end, flux, 0.0)
    bound = jnp.minimum(deep[PAD - 1 : PAD], deep[PAD : PAD + 1])
    flux = jnp.sum(jnp.where(level < bound, halo[1, RAW_AT:PAIR_AT], 0.0), axis=0, keepdims=True)
    plane = plane + jnp.where(row == PAD - 1, flux, 0.0) - jnp.where(row == PAD, flux, 0.0)

    place = iota((PAD, lanes), 1)
    table = jnp.zeros((PAD, lanes), jnp.float32)
    for number in range(thickness.shape[0]):
        table = table + jnp.where(place > number, thickness[number], 0.0)

    def column(bound):
        index = bound.astype(jnp.int32)
        return jnp.concatenate(
            [
                jnp.concatenate(
                    [
                        jnp.take_along_axis(
                            table, index[i : i + PAD, j : j + lanes], axis=1
                        )
                        for j in range(0, full[1], lanes)
                    ],
                    axis=1,
                )
                for i in range(0, full[0], PAD)
            ],
            axis=0,
        )

    beside, _, above, _ = shifted(deep)
    to_east = column(jnp.minimum(deep, beside))
    to_north = column(jnp.minimum(deep, above))
    to_north = jnp.where(at_top & (row == core_end - 1), 2.0, 1.0) * to_north
    to_west, to_south = turn(to_east, 1, 1), turn(to_north, 1, 0)
    diag = store + to_east + to_west + to_north + to_south
    there = diag > 0.0
    inverse = jnp.where(there, 1.0 / jnp.where(there, diag, 1.0), 0.0)

    def operate(values):
        east_side, west_side, north_side, south_side = shifted(values)
        total = (
            store * values + to_east * (values - east_side) + to_west * (values - west_side)
        )
        return total + to_north * (values - north_side) + to_south * (values - south_side)

    vectors, images = [plane * inverse], []
    for number in range(4):
        images.append(operate(vectors[-1]))
        if number < 3:
            vectors.append(images[-1] * inverse - SHIFTS[number] * vectors[-1])
    for number in range(4):
        basis[number] = vectors[number]

    def core(values):
        return values[PAD:core_end, :lanes]

    sums = []
    for i in range(4):
        for j in range(i, 4):
            sums.append(core(vectors[i]) * core(images[j]))
    for i in range(4):
        sums.append(core(vectors[i]) * core(plane))
    sums = [jnp.sum(item, axis=0, keepdims=True) for item in sums]
    sums = sums + [jnp.zeros((1, lanes), jnp.float32)] * (16 - len(sums))
    sums = jnp.sum(jnp.concatenate(sums, axis=0), axis=1, keepdims=True)
    same = iota((16, lanes), 0) == iota((16, lanes), 1)
    line = jnp.sum(jnp.where(same, sums, 0.0), axis=0, keepdims=True)
    gram[...] = jnp.broadcast_to(line, gram.shape)


def solve(line):
    entry = [line[:, i : i + 1] for i in range(14)]
    system = [[None] * 5 for _ in range(4)]
    for i in range(4):
        for j in range(i, 4):
            system[i][j] = entry.pop(0)
    for i in range(4):
        system[i][4] = entry.pop(0)
    factor, part = {}, []
    for k in range(4):
        pivot = system[k][k]
        usable = pivot > 0.0
        scale = jnp.where(usable, 1.0 / jnp.where(usable, pivot, 1.0), 0.0)
        part.append(system[k][4] * scale)
        for i in range(k + 1, 4):
            factor[i, k] = system[k][i] * scale
            for j in range(i, 5):
                system[i][j] = system[i][j] - factor[i, k] * system[k][j]
    for k in range(2, -1, -1):
        for i in range(k + 1, 4):
            part[k] = part[k] - factor[i, k] * part[i]
    return part


def final_kernel(
    thickness, totals, basis, depth_wide, planes_in, face_west, halo, rows_in,
    east, north, tracer_in,
    tracer_hbm, east_hbm, north_hbm, surface,
    planes, fixes, tracer, east_out, north_out, sems, tracer_sem,
):
    levels, rows, lanes = east.shape
    size = levels // PARTS
    core_end = PAD + rows
    outs = ((east_out, east_hbm), (north_out, north_hbm))

    def part_copy(number, part):
        place = pl.ds(part * size, size)
        source, target = outs[number]
        return pltpu.make_async_copy(source.at[place], target.at[place], sems.at[number, part])

    tracer_copy = pltpu.make_async_copy(tracer, tracer_hbm, tracer_sem)
    at_top = lax.axis_index("lat") == lax.axis_size("lat") - 1
    row = iota((rows, lanes), 0)
    deep = depth_wide[...]
    bounds = [jnp.minimum(deep, item)[PAD:core_end, :lanes] for item in shifted(deep)]
    face = planes_in[2]
    north_face = face + jnp.where(
        at_top & (row == rows - 1), halo[0, PAIR_AT - 1 : PAIR_AT, :lanes], 0.0
    )
    south_face = jnp.where(row == 0, halo[1, PAIR_AT - 1 : PAIR_AT, :lanes], turn(face, 1, 0))
    faces = (face, face_west[...], north_face, south_face)
    planes[0] = deep[PAD:core_end, :lanes]
    for number in range(4):
        planes[1 + number] = bounds[number]
    level = iota((LEVEL_ROWS, lanes), 0).astype(jnp.float32)
    for side, line in ((0, rows - 1), (1, 0)):
        bound = bounds[2 + side][line : line + 1]
        weight = faces[2 + side][line : line + 1]
        outer = (
            halo[side, PAIR_AT:, :lanes],
            halo[side, RAW_AT:PAIR_AT, :lanes],
            halo[side, PAIR_AT:, lanes:],
        )
        for number in range(3):
            inner = rows_in[3 * side + number, :LEVEL_ROWS]
            fixes[3 * side + number] = jnp.where(
                level < bound, weight * (outer[number] - inner), 0.0
            )
    parts = solve(jnp.sum(totals[...], axis=0, keepdims=True))
    height = parts[0] * basis[0]
    for number in range(1, 4):
        height = height + parts[number] * basis[number]
    surface[...] = planes_in[1] * height[PAD:core_end, :lanes]
    full_row = iota(height.shape, 0)
    folded = at_top & (full_row == core_end)
    to_east, to_west, to_north, to_south = shifted(height)
    slope_x = jnp.where(folded, to_west, to_east) - height
    slope_y = jnp.where(folded, to_south, to_north) - height
    inner_x, inner_y = slope_x[PAD:core_end, :lanes], slope_y[PAD:core_end, :lanes]
    spin = planes_in[4]
    planes[5] = inner_x - spin * inner_y
    planes[6] = inner_y + spin * inner_x
    for start, slope, inner in ((7, slope_x, inner_x), (11, slope_y, inner_y)):
        for number, item in enumerate(shifted(slope)):
            planes[start + number] = faces[number] * (inner - item[PAD:core_end, :lanes])

    line = iota((PAD, lanes), 0)
    first_line, last_line = line == 0, line == PAD - 1

    def part_step(part, carry):
        for tile in range(rows // PAD):
            place = slice(tile * PAD, (tile + 1) * PAD)
            own = [planes[number, place] for number in range(15)]
            for t in range(size):
                level = part * size + t
                height = level.astype(jnp.float32)
                open_sides = [height < own[number] for number in range(5)]
                for out, values, base, start, number in (
                    (east_out, east, 5, 7, 0), (north_out, north, 6, 11, 1)
                ):
                    change = jnp.where(open_sides[0], own[base], 0.0)
                    for side in range(4):
                        change = change - jnp.where(open_sides[1 + side], own[start + side], 0.0)
                    result = values[level, place] + thickness[level] * change
                    if tile == 0:
                        fix = fixes[3 + number, pl.ds(level, 1), :]
                        result = result + jnp.where(first_line, fix, 0.0)
                    if tile == rows // PAD - 1:
                        fix = fixes[number, pl.ds(level, 1), :]
                        result = result + jnp.where(last_line, fix, 0.0)
                    out[level, place] = result
        part_copy(0, part).start()
        part_copy(1, part).start()
        return carry

    def tracer_step(level, carry):
        for tile in range(rows // PAD):
            place = slice(tile * PAD, (tile + 1) * PAD)
            result = tracer_in[level, place]
            if tile == 0:
                result = result + jnp.where(first_line, fixes[5, pl.ds(level, 1), :], 0.0)
            if tile == rows // PAD - 1:
                result = result + jnp.where(last_line, fixes[2, pl.ds(level, 1), :], 0.0)
            tracer[level, place] = result
        return carry

    lax.fori_loop(0, levels, tracer_step, 0, unroll=5)
    tracer_copy.start()
    lax.fori_loop(0, PARTS, part_step, 0)
    tracer_copy.wait()
    for part in range(PARTS):
        part_copy(0, part).wait()
        part_copy(1, part).wait()


def swaps(lats, lons, odd):
    pairs = []
    for lat in range(lats):
        for lon in range(lons):
            other = lat + 1 if lat % 2 == odd else lat - 1
            if other < 0:
                continue
            if other == lats:
                pairs.append((lat * lons + lon, lat * lons + lons - 1 - lon))
            else:
                pairs.append((lat * lons + lon, other * lons + lon))
    return pairs


def lon_swaps(lons, odd):
    return [(lon, (lon + (1 if lon % 2 == odd else -1)) % lons) for lon in range(lons)]


def local(
    tracer_cot, east_cot, north_cot, surface_cot, depth_levels, diffusivity, coriolis, storage,
    thickness,
):
    levels, rows, lanes = tracer_cot.shape
    lats, lons = lax.axis_size("lat"), lax.axis_size("lon")
    far = lambda value: pltpu.with_memory_space_constraint(value, pltpu.HBM)
    near = lambda value: pltpu.with_memory_space_constraint(value, pltpu.VMEM)
    floats = lambda *shape: pltpu.HBM(shape, jnp.float32)
    scratch = lambda *shape: pltpu.VMEM(shape, jnp.float32)
    scalars = pl.BlockSpec(memory_space=pltpu.SMEM)
    in_hbm = pl.BlockSpec(memory_space=pltpu.HBM)
    in_vmem = pl.BlockSpec(memory_space=pltpu.VMEM)
    params = pltpu.CompilerParams(vmem_limit_bytes=VMEM_BYTES)
    plane, pair, field = (rows, lanes), (rows, 2 * lanes), (levels, rows, lanes)
    full = (rows + 2 * PAD, 2 * lanes)
    message = (MESSAGE_ROWS, 2 * lanes)

    message_0, message_1, planes, edge_rows, edges, east, north, tracer = pl.pallas_call(
        pack_kernel,
        in_specs=[in_hbm] * 8,
        out_specs=[in_vmem] * 8,
        out_shape=[
            scratch(*pair), scratch(*pair), scratch(5, *plane), scratch(6, *plane),
            scratch(3, *plane), scratch(*field), scratch(*field), scratch(*field),
        ],
        scratch_shapes=[
            pltpu.VMEM(plane, jnp.int32), scratch(*plane), scratch(*plane), scratch(*plane),
            scratch(2, *plane), pltpu.SemaphoreType.DMA((3, PARTS)), pltpu.SemaphoreType.DMA((5,)),
        ],
        compiler_params=params,
        name="pack",
    )(
        *[
            far(item)
            for item in (
                east_cot, north_cot, tracer_cot, depth_levels, storage, surface_cot, diffusivity,
                coriolis,
            )
        ]
    )

    got_1 = near(lax.ppermute(message_1, "lon", lon_swaps(lons, 1)))
    got_0 = near(lax.ppermute(message_0, "lon", lon_swaps(lons, 0)))

    wide, face_west, message_a, message_b = pl.pallas_call(
        stitch_kernel,
        in_specs=[in_vmem] * 5,
        out_specs=[in_vmem] * 4,
        out_shape=[scratch(4, *pair), scratch(*plane), scratch(*message), scratch(*message)],
        compiler_params=params,
        name="stitch",
    )(got_0, got_1, near(planes), near(edge_rows), near(edges))

    got_b = lax.ppermute(message_b, BOTH, swaps(lats, lons, 1))
    got_a = lax.ppermute(message_a, BOTH, swaps(lats, lons, 0))

    east_part, north_part, tracer_part = pl.pallas_call(
        level_kernel,
        in_specs=[in_vmem] * 9,
        out_specs=[in_vmem] * 3,
        out_shape=[scratch(*field)] * 3,
        scratch_shapes=[scratch(2, *plane), scratch(3, *plane)],
        compiler_params=params,
        cost_estimate=pl.CostEstimate(
            flops=60 * levels * rows * lanes, bytes_accessed=24 * levels * rows * lanes,
            transcendentals=0,
        ),
        name="level",
    )(
        got_0, got_1, near(wide), near(planes), near(face_west), near(edges), near(east),
        near(north), near(tracer),
    )

    wide, east_part = lax.optimization_barrier((wide, east_part))
    gram, basis, depth_wide, halo = pl.pallas_call(
        basis_kernel,
        in_specs=[scalars] + [in_vmem] * 3,
        out_specs=[in_vmem] * 4,
        out_shape=[
            scratch(lats * lons, lanes), scratch(4, *full), scratch(*full), scratch(2, *message)
        ],
        compiler_params=params,
        name="basis",
    )(thickness, near(got_a), near(got_b), near(wide))

    totals = lax.all_to_all(gram, BOTH, 0, 0, tiled=True)

    tracer_adj, east_adj, north_adj, surface_adj = pl.pallas_call(
        final_kernel,
        in_specs=[scalars] + [in_vmem] * 10,
        out_specs=[in_hbm] * 3 + [in_vmem],
        out_shape=[floats(*field)] * 3 + [jax.ShapeDtypeStruct(plane, jnp.float32)],
        scratch_shapes=[
            scratch(15, *plane), scratch(6, LEVEL_ROWS, lanes), scratch(*field), scratch(*field),
            scratch(*field), pltpu.SemaphoreType.DMA((2, PARTS)), pltpu.SemaphoreType.DMA,
        ],
        compiler_params=params,
        name="final",
    )(
        thickness, near(totals), near(basis), near(depth_wide), near(planes), near(face_west),
        near(halo), near(edge_rows), near(east_part), near(north_part), near(tracer_part),
    )
    return tracer_adj, east_adj, north_adj, surface_adj


def solution(mesh):
    field, plane = P(None, "lat", "lon"), P("lat", "lon")
    return jax.shard_map(
        local,
        mesh=mesh,
        in_specs=(field, field, field, plane, plane, plane, plane, plane, P()),
        out_specs=(field, field, field, plane),
        check_vma=False,
    )
```

```python
import jax
import jax.numpy as jnp
from jax import lax
from jax.experimental import pallas as pl
from jax.experimental.pallas import tpu as pltpu
from jax.sharding import PartitionSpec as P

WIDE = 6
PAD = 8
SHIFTS = (1.0, 0.3, 1.7)
PARTS = 5
OUT_PARTS = 10
LANES = 128
GROUP = 5
TILES = 4
BOTH = ("lat", "lon")
VMEM_BYTES = 32 * 1024 * 1024

DEPTH_AT, STORE_AT, SOURCE_AT, STRIP_AT, DIFF_AT = 100, 106, 112, 118, 124
LEVEL_ROWS = 56
RAW_AT = 3 * PAD
PAIR_AT = RAW_AT + LEVEL_ROWS
HALO_ROWS = PAIR_AT + LEVEL_ROWS
SIDES_AT = HALO_ROWS + LEVEL_ROWS
MESSAGE_ROWS = SIDES_AT + PAD
SIDE_GROUPS = PAIR_AT // PAD


def iota(shape, dim):
    return lax.broadcasted_iota(jnp.int32, shape, dim)


def turn(values, shift, dim):
    return pltpu.roll(values, shift % values.shape[dim], dim)


def pack_kernel(
    east_in, north_in, tracer_in, depth_in, storage_in, surf_in, diff_in, spin_in,
    message_0, message_1, planes, rows_out, edges, east, north, tracer,
    depth, surf, px, py, bounds, field_sems, plane_sems,
):
    levels, rows, lanes = east.shape
    size = levels // PARTS
    sources, fields = (east_in, north_in, tracer_in), (east, north, tracer)

    def part_copy(number, part):
        place = pl.ds(part * size, size)
        return pltpu.make_async_copy(
            sources[number].at[place], fields[number].at[place], field_sems.at[number, part]
        )

    moves = [
        pltpu.make_async_copy(source, target, plane_sems.at[number])
        for number, (source, target) in enumerate(
            (
                (depth_in, depth), (storage_in, planes.at[1]), (surf_in, surf),
                (diff_in, planes.at[2]), (spin_in, planes.at[4]),
            )
        )
    ]
    for move in moves:
        move.start()
    for part in range(PARTS):
        for number in range(3):
            part_copy(number, part).start()
    rows_out[:, levels - levels % PAD :] = jnp.zeros((6, rows - levels + levels % PAD, lanes), jnp.float32)
    px[...] = jnp.zeros((rows, lanes), jnp.float32)
    py[...] = jnp.zeros((rows, lanes), jnp.float32)
    edges[...] = jnp.zeros((3, rows, lanes), jnp.float32)
    for move in moves:
        move.wait()
    lane = iota((rows, lanes), 1)
    row = iota((rows, lanes), 0)
    deep = depth[...].astype(jnp.float32)
    planes[0] = deep
    bounds[0] = jnp.where(lane == lanes - 1, 0.0, jnp.minimum(deep, turn(deep, -1, 1)))
    bounds[1] = jnp.where(row == rows - 1, 0.0, jnp.minimum(deep, turn(deep, -1, 0)))
    pair_lane = lax.shift_right_logical(iota((PAD, lanes), 1), 1)

    for part in range(PARTS):
        for number in range(3):
            part_copy(number, part).wait()
        for t in range(size):
            level = part * size + t
            for number, ref in enumerate(fields):
                rows_out[number, level : level + 1, :] = ref[level, rows - 1 : rows, :]
                rows_out[3 + number, level : level + 1, :] = ref[level, 0:1, :]
        for tile in range(rows // PAD):
            place = slice(tile * PAD, (tile + 1) * PAD)
            sum_x, sum_y = px[place], py[place]
            limit_x, limit_y = bounds[0, place], bounds[1, place]
            ends = [edges[number, place] for number in range(3)]
            for t in range(size):
                level = part * size + t
                here = pair_lane == level
                values = [ref[level, place] for ref in fields]
                for number in range(3):
                    moved = turn(values[number], 2 * level + 1, 1)
                    ends[number] = jnp.where(here, moved, ends[number])
                sum_x = sum_x + jnp.where(limit_x > level, values[0], 0.0)
                sum_y = sum_y + jnp.where(limit_y > level, values[1], 0.0)
            px[place], py[place] = sum_x, sum_y
            for number in range(3):
                edges[number, place] = ends[number]

    plane = surf[...] + px[...] - turn(px[...], 1, 1) + py[...] - turn(py[...], 1, 0)
    planes[3] = plane
    odd_lane = lax.rem(lane, 2) == 1

    def put(target, values, start, place, count):
        moved = turn(values, place - start, 1)
        return jnp.where((lane >= place) & (lane < place + count), moved, target)

    def fill(ref, eastward):
        if eastward:
            ref[:, :lanes] = jnp.where(odd_lane, turn(edges[1], 1, 1), edges[0])
        else:
            ref[:, :lanes] = jnp.where(odd_lane, edges[0], turn(edges[1], -1, 1))
        start = lanes - WIDE if eastward else 0
        tile = edges[2]
        for values, place in (
            (deep, DEPTH_AT), (planes[1], STORE_AT), (plane, SOURCE_AT), (rows_out[1], STRIP_AT)
        ):
            tile = put(tile, values, start, place, WIDE)
        ref[:, lanes:] = put(tile, planes[2], lanes - 1, DIFF_AT, 1)

    even = lax.rem(lax.axis_index("lon"), 2) == 0

    @pl.when(even)
    def _():
        fill(message_0, True)
        fill(message_1, False)

    @pl.when(jnp.logical_not(even))
    def _():
        fill(message_0, False)
        fill(message_1, True)


def received(got_0, got_1):
    even = lax.rem(lax.axis_index("lon"), 2) == 0
    one, two = got_0[...], got_1[...]
    return jnp.where(even, two, one), jnp.where(even, one, two)


def stitch_kernel(
    got_0, got_1, planes, rows_in, edges,
    wide, face_west, message_a, message_b,
):
    rows, lanes = planes.shape[1:]
    from_west, from_east = received(got_0, got_1)
    lane = iota((rows, lanes), 1)
    left_tile, right_tile = from_west[:, lanes:], from_east[:, lanes:]

    def side(place):
        right = turn(right_tile, -place, 1)
        left = turn(left_tile, lanes - WIDE - place, 1)
        return jnp.where(lane < WIDE, right, jnp.where(lane >= lanes - WIDE, left, 0.0))

    deep, deep_side = planes[0], side(DEPTH_AT)
    store, store_side = planes[1], side(STORE_AT)
    plane, plane_side = planes[3], side(SOURCE_AT)
    strip = side(STRIP_AT)
    level = lax.shift_right_logical(lane, 1).astype(jnp.float32)
    even_lane = lax.rem(lane, 2) == 0

    def flux(values, bound):
        used = even_lane & (level < bound)
        return jnp.sum(jnp.where(used, values, 0.0), axis=1, keepdims=True)

    flux_east = flux(edges[0], jnp.minimum(deep[:, lanes - 1 :], deep_side[:, 0:1]))
    flux_west = flux(from_west[:, :lanes], jnp.minimum(deep_side[:, lanes - 1 :], deep[:, 0:1]))
    first, last = lane == 0, lane == lanes - 1
    plane = plane + jnp.where(last, flux_east, 0.0) - jnp.where(first, flux_west, 0.0)
    plane_side = plane_side - jnp.where(first, flux_east, 0.0) + jnp.where(last, flux_west, 0.0)
    both = ((deep, deep_side), (store, store_side), (plane, plane_side), (rows_in[1], strip))
    for number, (one, two) in enumerate(both):
        wide[number, :, :lanes] = one
        wide[number, :, lanes:] = two
    faces = planes[2]
    face_west[...] = jnp.where(first, turn(left_tile, -DIFF_AT, 1), turn(faces, 1, 1))

    small_lane = iota((PAD, lanes), 1)

    def fill(ref, up):
        start = rows - PAD if up else 0
        base = 0 if up else 3
        groups = [two[start : start + PAD] for _, two in both[:3]]
        groups = groups + [strip[i : i + PAD] for i in range(0, LEVEL_ROWS, PAD)]
        packed = jnp.zeros((PAD, lanes), jnp.float32)
        for number, item in enumerate(groups):
            place = 2 * WIDE * number
            here = (small_lane >= place) & (small_lane < place + 2 * WIDE)
            packed = jnp.where(here, turn(item, place + WIDE, 1), packed)
        for number, (one, _) in enumerate(both[:3]):
            ref[number * PAD : (number + 1) * PAD] = one[start : start + PAD]
        ref[RAW_AT:PAIR_AT] = rows_in[base + 1, :LEVEL_ROWS]
        ref[PAIR_AT:HALO_ROWS] = rows_in[base, :LEVEL_ROWS]
        ref[HALO_ROWS:SIDES_AT] = rows_in[base + 2, :LEVEL_ROWS]
        ref[SIDES_AT:] = packed
        if up:
            ref[PAIR_AT - 1 : PAIR_AT] = faces[rows - 1 :]

    even = lax.rem(lax.axis_index("lat"), 2) == 0

    @pl.when(even)
    def _():
        fill(message_a, True)
        fill(message_b, False)

    @pl.when(jnp.logical_not(even))
    def _():
        fill(message_a, False)
        fill(message_b, True)


def shifted(values):
    return turn(values, -1, 1), turn(values, 1, 1), turn(values, -1, 0), turn(values, 1, 0)


def face_planes(planes, limits, weights):
    deep, face = planes[0], planes[2]
    lane, row = iota(deep.shape, 1), iota(deep.shape, 0)
    rows, lanes = deep.shape
    edges = (lane == lanes - 1, lane == 0, row == rows - 1, row == 0)
    for number, (edge, values) in enumerate(zip(edges, shifted(deep))):
        limits[number] = jnp.where(edge, 0.0, jnp.minimum(deep, values))
    weights[0] = turn(face, 1, 1)
    weights[1] = turn(face, 1, 0)


def level_faces(level, place, planes, limits, weights):
    height = level.astype(jnp.float32)
    face = planes[2, place]
    return (
        height < planes[0, place],
        jnp.where(height < limits[0, place], face, 0.0),
        jnp.where(height < limits[1, place], weights[0, place], 0.0),
        jnp.where(height < limits[2, place], face, 0.0),
        jnp.where(height < limits[3, place], weights[1, place], 0.0),
    )


def smooth(ref, level, tile, tiles, faces):
    wet, face_east, face_west, face_north, face_south = faces
    start = tile * PAD
    item = ref[level, start : start + PAD]
    if tile + 1 < tiles:
        above = ref[level, start + 1 : start + 1 + PAD]
    else:
        above = turn(item, -1, 0)
    below = ref[level, start - 1 : start - 1 + PAD] if tile else turn(item, 1, 0)
    change = face_north * (above - item) + face_south * (below - item)
    change = change + face_east * (turn(item, -1, 1) - item)
    change = change + face_west * (turn(item, 1, 1) - item)
    return item, jnp.where(wet, item, 0.0) + change


def inner_kernel(
    planes, east, north, tracer, east_out, north_out, tracer_out, limits, weights
):
    levels, rows, lanes = tracer.shape
    tiles = rows // PAD
    face_planes(planes, limits, weights)
    for first in range(0, tiles, TILES):

        def step(group, carry):
            for t in range(GROUP):
                level = group * GROUP + t
                for tile in range(first, first + TILES):
                    place = slice(tile * PAD, (tile + 1) * PAD)
                    faces = level_faces(level, place, planes, limits, weights)
                    one, new_one = smooth(east, level, tile, tiles, faces)
                    two, new_two = smooth(north, level, tile, tiles, faces)
                    spin = jnp.where(faces[0], planes[4, place], 0.0)
                    east_out[level, place] = new_one - spin * two
                    north_out[level, place] = new_two + spin * one
                    tracer_out[level, place] = smooth(tracer, level, tile, tiles, faces)[1]
            return carry

        lax.fori_loop(0, levels // GROUP, step, 0)


def rim_kernel(
    got_0, got_1, wide, planes, face_west, edges, east, north, tracer,
    east_out, north_out, tracer_out,
    sides,
):
    levels, rows, lanes = east.shape
    from_west, from_east = received(got_0, got_1)
    lane = iota((rows, lanes), 1)
    deep, beside = wide[0, :, :lanes], wide[0, :, lanes:]
    level_of = lax.shift_right_logical(lane, 1).astype(jnp.float32)
    odd_lane = lax.rem(lane, 2) == 1
    bound_east = jnp.minimum(deep[:, lanes - 1 :], beside[:, 0:1])
    bound_west = jnp.minimum(deep[:, 0:1], beside[:, lanes - 1 :])
    weight = jnp.where(odd_lane, face_west[:, 0:1], planes[2, :, lanes - 1 :])
    weight = jnp.where(level_of < jnp.where(odd_lane, bound_west, bound_east), weight, 0.0)
    halos = (
        jnp.where(odd_lane, turn(from_west[:, :lanes], 1, 1), turn(from_east[:, :lanes], -1, 1)),
        jnp.where(odd_lane, from_west[:, :lanes], from_east[:, :lanes]),
        jnp.where(odd_lane, turn(from_west[:, lanes:], 1, 1), turn(from_east[:, lanes:], -1, 1)),
    )
    for number in range(3):
        sides[number] = turn(weight * (halos[number] - edges[number]), -1, 1)
    small_lane = iota((PAD, lanes), 1)
    rim = (small_lane == 0) | (small_lane == lanes - 1)
    tiles = rows // PAD
    pairs = ((east, east_out), (north, north_out), (tracer, tracer_out))
    for first in range(0, tiles, TILES):
        chunk = range(first, first + TILES)

        def step(group, rims):
            for t in range(GROUP):
                level = group * GROUP + t
                for number, tile in enumerate(chunk):
                    place = slice(tile * PAD, (tile + 1) * PAD)
                    for index, (source, target) in enumerate(pairs):
                        part = turn(rims[3 * number + index], -2 * t, 1)
                        target[level, place] = source[level, place] + jnp.where(rim, part, 0.0)
            return tuple(turn(item, -2 * GROUP, 1) for item in rims)

        lax.fori_loop(
            0, levels // GROUP, step,
            tuple(
                sides[number, tile * PAD : (tile + 1) * PAD] for tile in chunk for number in range(3)
            ),
        )


def basis_kernel(
    thickness, got_a, got_b, wide, planes, rows_in, tracer_in,
    gram, basis, depth_wide, halo, fixes, tracer,
):
    rows, lanes = wide.shape[1], wide.shape[2] // 2
    lat = lax.axis_index("lat")
    even = lax.rem(lat, 2) == 0
    at_top = lat == lax.axis_size("lat") - 1
    at_bottom = lat == 0

    one, two = got_a[...], got_b[...]
    small_lane = iota((PAD, lanes), 1)
    near_side = (small_lane < WIDE) | (small_lane >= lanes - WIDE)

    def tiles_of(values, number):
        start = number * PAD
        first = values[start : start + PAD]
        if number < SIDE_GROUPS:
            second = turn(values[SIDES_AT:], -2 * WIDE * number - WIDE, 1)
            second = jnp.where(near_side, second, 0.0)
        else:
            start = start + LEVEL_ROWS
            second = values[start : start + PAD]
        return first, second

    groups = range(HALO_ROWS // PAD)
    above = jnp.where(even, one, two)

    @pl.when(at_top)
    def _():
        back = lanes - 1 - small_lane
        for number in groups:
            for tile, values in enumerate(tiles_of(above, number)):
                values = jnp.take_along_axis(values, back, axis=1)
                if number < 3:
                    values = jnp.concatenate(
                        [values[i : i + 1] for i in range(PAD - 1, -1, -1)], axis=0
                    )
                halo[0, number * PAD : (number + 1) * PAD, tile * lanes : (tile + 1) * lanes] = values

    @pl.when(jnp.logical_not(at_top))
    def _():
        for number in groups:
            for tile, values in enumerate(tiles_of(above, number)):
                halo[0, number * PAD : (number + 1) * PAD, tile * lanes : (tile + 1) * lanes] = values

    below = jnp.where(at_bottom, 0.0, jnp.where(even, two, one))
    for number in groups:
        for tile, values in enumerate(tiles_of(below, number)):
            halo[1, number * PAD : (number + 1) * PAD, tile * lanes : (tile + 1) * lanes] = values

    def whole(number):
        place = slice(number * PAD, (number + 1) * PAD)
        return jnp.concatenate([halo[1, place], wide[number], halo[0, place]], axis=0)

    deep, store, plane = whole(0), whole(1), whole(2)
    depth_wide[...] = deep
    full = deep.shape
    row = iota(full, 0)
    core_end = PAD + rows
    level = iota((LEVEL_ROWS, full[1]), 0).astype(jnp.float32)
    bound = jnp.minimum(deep[core_end - 1 : core_end], deep[core_end : core_end + 1])
    edge = wide[3, :LEVEL_ROWS] - jnp.where(at_top, halo[0, RAW_AT:PAIR_AT], 0.0)
    flux = jnp.sum(jnp.where(level < bound, edge, 0.0), axis=0, keepdims=True)
    plane = plane + jnp.where(row == core_end - 1, flux, 0.0) - jnp.where(row == core_end, flux, 0.0)
    bound = jnp.minimum(deep[PAD - 1 : PAD], deep[PAD : PAD + 1])
    flux = jnp.sum(jnp.where(level < bound, halo[1, RAW_AT:PAIR_AT], 0.0), axis=0, keepdims=True)
    plane = plane + jnp.where(row == PAD - 1, flux, 0.0) - jnp.where(row == PAD, flux, 0.0)

    place = iota((PAD, lanes), 1)
    table = jnp.zeros((PAD, lanes), jnp.float32)
    for number in range(thickness.shape[0]):
        table = table + jnp.where(place > number, thickness[number], 0.0)

    def column(bound):
        index = bound.astype(jnp.int32)
        return jnp.concatenate(
            [
                jnp.concatenate(
                    [
                        jnp.take_along_axis(
                            table, index[i : i + PAD, j : j + lanes], axis=1
                        )
                        for j in range(0, full[1], lanes)
                    ],
                    axis=1,
                )
                for i in range(0, full[0], PAD)
            ],
            axis=0,
        )

    beside, _, above, _ = shifted(deep)
    to_east = column(jnp.minimum(deep, beside))
    to_north = column(jnp.minimum(deep, above))
    to_north = jnp.where(at_top & (row == core_end - 1), 2.0, 1.0) * to_north
    to_west, to_south = turn(to_east, 1, 1), turn(to_north, 1, 0)
    diag = store + to_east + to_west + to_north + to_south
    there = diag > 0.0
    inverse = jnp.where(there, 1.0 / jnp.where(there, diag, 1.0), 0.0)

    def operate(values):
        east_side, west_side, north_side, south_side = shifted(values)
        total = (
            store * values + to_east * (values - east_side) + to_west * (values - west_side)
        )
        return total + to_north * (values - north_side) + to_south * (values - south_side)

    vectors, images = [plane * inverse], []
    for number in range(4):
        images.append(operate(vectors[-1]))
        if number < 3:
            vectors.append(images[-1] * inverse - SHIFTS[number] * vectors[-1])
    for number in range(4):
        basis[number] = vectors[number]

    def core(values):
        return values[PAD:core_end, :lanes]

    sums = []
    for i in range(4):
        for j in range(i, 4):
            sums.append(core(vectors[i]) * core(images[j]))
    for i in range(4):
        sums.append(core(vectors[i]) * core(plane))
    sums = [jnp.sum(item, axis=0, keepdims=True) for item in sums]
    sums = sums + [jnp.zeros((1, lanes), jnp.float32)] * (16 - len(sums))
    sums = jnp.sum(jnp.concatenate(sums, axis=0), axis=1, keepdims=True)
    same = iota((16, lanes), 0) == iota((16, lanes), 1)
    line = jnp.sum(jnp.where(same, sums, 0.0), axis=0, keepdims=True)
    gram[...] = jnp.broadcast_to(line, gram.shape)

    face = planes[2]
    level = level[:, :lanes]
    top_face = face[rows - 1 :] + jnp.where(at_top, halo[0, PAIR_AT - 1 : PAIR_AT, :lanes], 0.0)
    low_face = halo[1, PAIR_AT - 1 : PAIR_AT, :lanes]
    for side, line, weight in ((0, core_end - 1, top_face), (1, PAD, low_face)):
        other = line + 1 - 2 * side
        bound = jnp.minimum(deep[line : line + 1], deep[other : other + 1])[:, :lanes]
        outer = (
            halo[side, PAIR_AT:, :lanes],
            halo[side, RAW_AT:PAIR_AT, :lanes],
            halo[side, PAIR_AT:, lanes:],
        )
        for number in range(3):
            inner = rows_in[3 * side + number, :LEVEL_ROWS]
            fixes[3 * side + number] = jnp.where(
                level < bound, weight * (outer[number] - inner), 0.0
            )
    for number in range(tracer.shape[0]):
        last = tracer_in[number, rows - 1 : rows] + fixes[2, number : number + 1]
        first = tracer_in[number, 0:1] + fixes[5, number : number + 1]
        tracer[number, rows - 1 : rows] = last
        tracer[number, 0:1] = first


def solve(line):
    entry = [line[:, i : i + 1] for i in range(14)]
    system = [[None] * 5 for _ in range(4)]
    for i in range(4):
        for j in range(i, 4):
            system[i][j] = entry.pop(0)
    for i in range(4):
        system[i][4] = entry.pop(0)
    factor, part = {}, []
    for k in range(4):
        pivot = system[k][k]
        usable = pivot > 0.0
        scale = jnp.where(usable, 1.0 / jnp.where(usable, pivot, 1.0), 0.0)
        part.append(system[k][4] * scale)
        for i in range(k + 1, 4):
            factor[i, k] = system[k][i] * scale
            for j in range(i, 5):
                system[i][j] = system[i][j] - factor[i, k] * system[k][j]
    for k in range(2, -1, -1):
        for i in range(k + 1, 4):
            part[k] = part[k] - factor[i, k] * part[i]
    return part


def final_kernel(
    thickness, totals, basis, depth_wide, planes_in, face_west, halo, fixes, east, north, tracer,
    tracer_hbm, east_hbm, north_hbm, surface,
    planes, east_out, north_out, sems, tracer_sem,
):
    levels, rows, lanes = east.shape
    size = levels // OUT_PARTS
    core_end = PAD + rows
    outs = ((east_out, east_hbm), (north_out, north_hbm))

    def part_copy(number, part):
        place = pl.ds(part * size, size)
        source, target = outs[number]
        return pltpu.make_async_copy(source.at[place], target.at[place], sems.at[number, part])

    tracer_copy = pltpu.make_async_copy(tracer, tracer_hbm, tracer_sem)
    tracer_copy.start()
    at_top = lax.axis_index("lat") == lax.axis_size("lat") - 1
    row = iota((rows, lanes), 0)
    deep = depth_wide[...]
    bounds = [jnp.minimum(deep, item)[PAD:core_end, :lanes] for item in shifted(deep)]
    face = planes_in[2]
    north_face = face + jnp.where(
        at_top & (row == rows - 1), halo[0, PAIR_AT - 1 : PAIR_AT, :lanes], 0.0
    )
    south_face = jnp.where(row == 0, halo[1, PAIR_AT - 1 : PAIR_AT, :lanes], turn(face, 1, 0))
    faces = (face, face_west[...], north_face, south_face)
    planes[0] = deep[PAD:core_end, :lanes]
    for number in range(4):
        planes[1 + number] = bounds[number]
    parts = solve(jnp.sum(totals[...], axis=0, keepdims=True))
    height = parts[0] * basis[0]
    for number in range(1, 4):
        height = height + parts[number] * basis[number]
    surface[...] = planes_in[1] * height[PAD:core_end, :lanes]
    full_row = iota(height.shape, 0)
    folded = at_top & (full_row == core_end)
    to_east, to_west, to_north, to_south = shifted(height)
    slope_x = jnp.where(folded, to_west, to_east) - height
    slope_y = jnp.where(folded, to_south, to_north) - height
    inner_x, inner_y = slope_x[PAD:core_end, :lanes], slope_y[PAD:core_end, :lanes]
    spin = planes_in[4]
    planes[5] = inner_x - spin * inner_y
    planes[6] = inner_y + spin * inner_x
    for start, slope, inner in ((7, slope_x, inner_x), (11, slope_y, inner_y)):
        for number, item in enumerate(shifted(slope)):
            planes[start + number] = faces[number] * (inner - item[PAD:core_end, :lanes])

    line = iota((PAD, lanes), 0)
    first_line, last_line = line == 0, line == PAD - 1

    def part_step(part, carry):
        for tile in range(rows // PAD):
            place = slice(tile * PAD, (tile + 1) * PAD)
            own = [planes[number, place] for number in range(15)]
            for t in range(size):
                level = part * size + t
                height = level.astype(jnp.float32)
                open_sides = [height < own[number] for number in range(5)]
                for out, values, base, start, number in (
                    (east_out, east, 5, 7, 0), (north_out, north, 6, 11, 1)
                ):
                    change = jnp.where(open_sides[0], own[base], 0.0)
                    for side in range(4):
                        change = change - jnp.where(open_sides[1 + side], own[start + side], 0.0)
                    result = values[level, place] + thickness[level] * change
                    if tile == 0:
                        fix = fixes[3 + number, pl.ds(level, 1), :]
                        result = result + jnp.where(first_line, fix, 0.0)
                    if tile == rows // PAD - 1:
                        fix = fixes[number, pl.ds(level, 1), :]
                        result = result + jnp.where(last_line, fix, 0.0)
                    out[level, place] = result
        part_copy(0, part).start()
        part_copy(1, part).start()
        return carry

    lax.fori_loop(0, OUT_PARTS, part_step, 0)
    tracer_copy.wait()
    for part in range(OUT_PARTS):
        part_copy(0, part).wait()
        part_copy(1, part).wait()


def swaps(lats, lons, odd):
    pairs = []
    for lat in range(lats):
        for lon in range(lons):
            other = lat + 1 if lat % 2 == odd else lat - 1
            if other < 0:
                pairs.append((lon, (lon ^ 1) % lons))
            elif other == lats:
                pairs.append((lat * lons + lon, lat * lons + lons - 1 - lon))
            else:
                pairs.append((lat * lons + lon, other * lons + lon))
    return pairs


def lon_swaps(lons, odd):
    return [(lon, (lon + (1 if lon % 2 == odd else -1)) % lons) for lon in range(lons)]


def local(
    tracer_cot, east_cot, north_cot, surface_cot, depth_levels, diffusivity, coriolis, storage,
    thickness,
):
    levels, rows, lanes = tracer_cot.shape
    lats, lons = lax.axis_size("lat"), lax.axis_size("lon")
    far = lambda value: pltpu.with_memory_space_constraint(value, pltpu.HBM)
    near = lambda value: pltpu.with_memory_space_constraint(value, pltpu.VMEM)
    floats = lambda *shape: pltpu.HBM(shape, jnp.float32)
    scratch = lambda *shape: pltpu.VMEM(shape, jnp.float32)
    scalars = pl.BlockSpec(memory_space=pltpu.SMEM)
    in_hbm = pl.BlockSpec(memory_space=pltpu.HBM)
    in_vmem = pl.BlockSpec(memory_space=pltpu.VMEM)
    params = pltpu.CompilerParams(vmem_limit_bytes=VMEM_BYTES)
    cost = lambda work: pl.CostEstimate(
        flops=work * levels * rows * lanes, bytes_accessed=8 * levels * rows * lanes,
        transcendentals=0,
    )
    plane, pair, field = (rows, lanes), (rows, 2 * lanes), (levels, rows, lanes)
    full = (rows + 2 * PAD, 2 * lanes)
    message, strips = (MESSAGE_ROWS, lanes), (2, HALO_ROWS, 2 * lanes)

    message_0, message_1, planes, edge_rows, edges, east, north, tracer = pl.pallas_call(
        pack_kernel,
        in_specs=[in_hbm] * 8,
        out_specs=[in_vmem] * 8,
        out_shape=[
            scratch(*pair), scratch(*pair), scratch(5, *plane), scratch(6, *plane),
            scratch(3, *plane), scratch(*field), scratch(*field), scratch(*field),
        ],
        scratch_shapes=[
            pltpu.VMEM(plane, jnp.int32), scratch(*plane), scratch(*plane), scratch(*plane),
            scratch(2, *plane), pltpu.SemaphoreType.DMA((3, PARTS)), pltpu.SemaphoreType.DMA((5,)),
        ],
        compiler_params=params,
        name="pack",
    )(
        *[
            far(item)
            for item in (
                east_cot, north_cot, tracer_cot, depth_levels, storage, surface_cot, diffusivity,
                coriolis,
            )
        ]
    )

    got_1 = lax.ppermute(message_1, "lon", lon_swaps(lons, 1))
    got_0 = lax.ppermute(message_0, "lon", lon_swaps(lons, 0))

    east_part, north_part, tracer_part = pl.pallas_call(
        inner_kernel,
        in_specs=[in_vmem] * 4,
        out_specs=[in_vmem] * 3,
        out_shape=[scratch(*field)] * 3,
        scratch_shapes=[scratch(4, *plane), scratch(2, *plane)],
        compiler_params=params,
        cost_estimate=cost(60),
        name="inner",
    )(near(planes), near(east), near(north), near(tracer))

    edges, east_part = lax.optimization_barrier((edges, east_part))
    got_0, got_1 = near(got_0), near(got_1)
    wide, face_west, message_a, message_b = pl.pallas_call(
        stitch_kernel,
        in_specs=[in_vmem] * 5,
        out_specs=[in_vmem] * 4,
        out_shape=[scratch(4, *pair), scratch(*plane), scratch(*message), scratch(*message)],
        compiler_params=params,
        name="stitch",
    )(got_0, got_1, near(planes), near(edge_rows), near(edges))

    got_b = lax.ppermute(message_b, BOTH, swaps(lats, lons, 1))
    got_a = lax.ppermute(message_a, BOTH, swaps(lats, lons, 0))

    east_part, north_part, tracer_part = pl.pallas_call(
        rim_kernel,
        in_specs=[in_vmem] * 9,
        out_specs=[in_vmem] * 3,
        out_shape=[scratch(*field)] * 3,
        scratch_shapes=[scratch(3, *plane)],
        input_output_aliases={6: 0, 7: 1, 8: 2},
        compiler_params=params,
        cost_estimate=cost(10),
        name="rim",
    )(
        got_0, got_1, near(wide), near(planes), near(face_west), near(edges), near(east_part),
        near(north_part), near(tracer_part),
    )

    wide, east_part = lax.optimization_barrier((wide, east_part))
    gram, basis, depth_wide, halo, fixes, tracer_part = pl.pallas_call(
        basis_kernel,
        in_specs=[scalars] + [in_vmem] * 6,
        out_specs=[in_vmem] * 6,
        out_shape=[
            scratch(lats * lons, lanes), scratch(4, *full), scratch(*full), scratch(*strips),
            scratch(6, LEVEL_ROWS, lanes), scratch(*field),
        ],
        input_output_aliases={6: 5},
        compiler_params=params,
        name="basis",
    )(
        thickness, near(got_a), near(got_b), near(wide), near(planes), near(edge_rows),
        near(tracer_part),
    )

    totals = lax.all_to_all(gram, BOTH, 0, 0, tiled=True)

    tracer_adj, east_adj, north_adj, surface_adj = pl.pallas_call(
        final_kernel,
        in_specs=[scalars] + [in_vmem] * 10,
        out_specs=[in_hbm] * 3 + [in_vmem],
        out_shape=[floats(*field)] * 3 + [jax.ShapeDtypeStruct(plane, jnp.float32)],
        scratch_shapes=[
            scratch(15, *plane), scratch(*field), scratch(*field),
            pltpu.SemaphoreType.DMA((2, OUT_PARTS)), pltpu.SemaphoreType.DMA,
        ],
        compiler_params=params,
        name="final",
    )(
        thickness, near(totals), near(basis), near(depth_wide), near(planes), near(face_west),
        near(halo), near(fixes), near(east_part), near(north_part), near(tracer_part),
    )
    return tracer_adj, east_adj, north_adj, surface_adj


def solution(mesh):
    field, plane = P(None, "lat", "lon"), P("lat", "lon")
    return jax.shard_map(
        local,
        mesh=mesh,
        in_specs=(field, field, field, plane, plane, plane, plane, plane, P()),
        out_specs=(field, field, field, plane),
        check_vma=False,
    )
```

```python
import jax
import jax.numpy as jnp
from jax import lax
from jax.experimental import pallas as pl
from jax.experimental.pallas import tpu as pltpu
from jax.sharding import PartitionSpec as P

WIDE = 6
PAD = 8
SHIFTS = (1.0, 0.3, 1.7)
PARTS = 5
OUT_PARTS = 10
LANES = 128
GROUP = 5
TILES = 4
BOTH = ("lat", "lon")
VMEM_BYTES = 32 * 1024 * 1024

DEPTH_AT, STORE_AT, SOURCE_AT, STRIP_AT, DIFF_AT = 100, 106, 112, 118, 124
LEVEL_ROWS = 56
RAW_AT = 3 * PAD
PAIR_AT = RAW_AT + LEVEL_ROWS
HALO_ROWS = PAIR_AT + LEVEL_ROWS
SIDES_AT = HALO_ROWS + LEVEL_ROWS
MESSAGE_ROWS = SIDES_AT + PAD
SIDE_GROUPS = PAIR_AT // PAD


def iota(shape, dim):
    return lax.broadcasted_iota(jnp.int32, shape, dim)


def turn(values, shift, dim):
    return pltpu.roll(values, shift % values.shape[dim], dim)


def pack_kernel(
    east_in, north_in, tracer_in, depth_in, storage_in, surf_in, diff_in, spin_in,
    message_0, message_1, planes, rows_out, edges, east, north, tracer,
    depth, surf, px, py, bounds, field_sems, plane_sems,
):
    levels, rows, lanes = east.shape
    size = levels // PARTS
    sources, fields = (east_in, north_in, tracer_in), (east, north, tracer)

    def part_copy(number, part):
        place = pl.ds(part * size, size)
        return pltpu.make_async_copy(
            sources[number].at[place], fields[number].at[place], field_sems.at[number, part]
        )

    moves = [
        pltpu.make_async_copy(source, target, plane_sems.at[number])
        for number, (source, target) in enumerate(
            (
                (depth_in, depth), (storage_in, planes.at[1]), (surf_in, surf),
                (diff_in, planes.at[2]), (spin_in, planes.at[4]),
            )
        )
    ]
    for move in moves:
        move.start()
    for part in range(PARTS):
        for number in range(3):
            part_copy(number, part).start(priority=min(part, 1))
    rows_out[:, levels - levels % PAD :] = jnp.zeros((6, rows - levels + levels % PAD, lanes), jnp.float32)
    px[...] = jnp.zeros((rows, lanes), jnp.float32)
    py[...] = jnp.zeros((rows, lanes), jnp.float32)
    edges[...] = jnp.zeros((3, rows, lanes), jnp.float32)
    for move in moves:
        move.wait()
    lane = iota((rows, lanes), 1)
    row = iota((rows, lanes), 0)
    deep = depth[...].astype(jnp.float32)
    planes[0] = deep
    bounds[0] = jnp.where(lane == lanes - 1, 0.0, jnp.minimum(deep, turn(deep, -1, 1)))
    bounds[1] = jnp.where(row == rows - 1, 0.0, jnp.minimum(deep, turn(deep, -1, 0)))
    pair_lane = lax.shift_right_logical(iota((PAD, lanes), 1), 1)

    for part in range(PARTS):
        for number in range(3):
            part_copy(number, part).wait()
        for t in range(size):
            level = part * size + t
            for number, ref in enumerate(fields):
                rows_out[number, level : level + 1, :] = ref[level, rows - 1 : rows, :]
                rows_out[3 + number, level : level + 1, :] = ref[level, 0:1, :]
        for tile in range(rows // PAD):
            place = slice(tile * PAD, (tile + 1) * PAD)
            sum_x, sum_y = px[place], py[place]
            limit_x, limit_y = bounds[0, place], bounds[1, place]
            ends = [edges[number, place] for number in range(3)]
            for t in range(size):
                level = part * size + t
                here = pair_lane == level
                values = [ref[level, place] for ref in fields]
                for number in range(3):
                    moved = turn(values[number], 2 * level + 1, 1)
                    ends[number] = jnp.where(here, moved, ends[number])
                sum_x = sum_x + jnp.where(limit_x > level, values[0], 0.0)
                sum_y = sum_y + jnp.where(limit_y > level, values[1], 0.0)
            px[place], py[place] = sum_x, sum_y
            for number in range(3):
                edges[number, place] = ends[number]

    plane = surf[...] + px[...] - turn(px[...], 1, 1) + py[...] - turn(py[...], 1, 0)
    planes[3] = plane
    odd_lane = lax.rem(lane, 2) == 1

    def put(target, values, start, place, count):
        moved = turn(values, place - start, 1)
        return jnp.where((lane >= place) & (lane < place + count), moved, target)

    def fill(ref, eastward):
        if eastward:
            ref[:, :lanes] = jnp.where(odd_lane, turn(edges[1], 1, 1), edges[0])
        else:
            ref[:, :lanes] = jnp.where(odd_lane, edges[0], turn(edges[1], -1, 1))
        start = lanes - WIDE if eastward else 0
        tile = edges[2]
        for values, place in (
            (deep, DEPTH_AT), (planes[1], STORE_AT), (plane, SOURCE_AT), (rows_out[1], STRIP_AT)
        ):
            tile = put(tile, values, start, place, WIDE)
        ref[:, lanes:] = put(tile, planes[2], lanes - 1, DIFF_AT, 1)

    even = lax.rem(lax.axis_index("lon"), 2) == 0

    @pl.when(even)
    def _():
        fill(message_0, True)
        fill(message_1, False)

    @pl.when(jnp.logical_not(even))
    def _():
        fill(message_0, False)
        fill(message_1, True)


def received(got_0, got_1):
    even = lax.rem(lax.axis_index("lon"), 2) == 0
    one, two = got_0[...], got_1[...]
    return jnp.where(even, two, one), jnp.where(even, one, two)


def stitch_kernel(
    got_0, got_1, planes, rows_in, edges,
    wide, face_west, message_a, message_b,
):
    rows, lanes = planes.shape[1:]
    from_west, from_east = received(got_0, got_1)
    lane = iota((rows, lanes), 1)
    left_tile, right_tile = from_west[:, lanes:], from_east[:, lanes:]

    def side(place):
        right = turn(right_tile, -place, 1)
        left = turn(left_tile, lanes - WIDE - place, 1)
        return jnp.where(lane < WIDE, right, jnp.where(lane >= lanes - WIDE, left, 0.0))

    deep, deep_side = planes[0], side(DEPTH_AT)
    store, store_side = planes[1], side(STORE_AT)
    plane, plane_side = planes[3], side(SOURCE_AT)
    strip = side(STRIP_AT)
    level = lax.shift_right_logical(lane, 1).astype(jnp.float32)
    even_lane = lax.rem(lane, 2) == 0

    def flux(values, bound):
        used = even_lane & (level < bound)
        return jnp.sum(jnp.where(used, values, 0.0), axis=1, keepdims=True)

    flux_east = flux(edges[0], jnp.minimum(deep[:, lanes - 1 :], deep_side[:, 0:1]))
    flux_west = flux(from_west[:, :lanes], jnp.minimum(deep_side[:, lanes - 1 :], deep[:, 0:1]))
    first, last = lane == 0, lane == lanes - 1
    plane = plane + jnp.where(last, flux_east, 0.0) - jnp.where(first, flux_west, 0.0)
    plane_side = plane_side - jnp.where(first, flux_east, 0.0) + jnp.where(last, flux_west, 0.0)
    both = ((deep, deep_side), (store, store_side), (plane, plane_side), (rows_in[1], strip))
    for number, (one, two) in enumerate(both):
        wide[number, :, :lanes] = one
        wide[number, :, lanes:] = two
    faces = planes[2]
    face_west[...] = jnp.where(first, turn(left_tile, -DIFF_AT, 1), turn(faces, 1, 1))

    small_lane = iota((PAD, lanes), 1)

    def fill(ref, up):
        start = rows - PAD if up else 0
        base = 0 if up else 3
        groups = [two[start : start + PAD] for _, two in both[:3]]
        groups = groups + [strip[i : i + PAD] for i in range(0, LEVEL_ROWS, PAD)]
        packed = jnp.zeros((PAD, lanes), jnp.float32)
        for number, item in enumerate(groups):
            place = 2 * WIDE * number
            here = (small_lane >= place) & (small_lane < place + 2 * WIDE)
            packed = jnp.where(here, turn(item, place + WIDE, 1), packed)
        for number, (one, _) in enumerate(both[:3]):
            ref[number * PAD : (number + 1) * PAD] = one[start : start + PAD]
        ref[RAW_AT:PAIR_AT] = rows_in[base + 1, :LEVEL_ROWS]
        ref[PAIR_AT:HALO_ROWS] = rows_in[base, :LEVEL_ROWS]
        ref[HALO_ROWS:SIDES_AT] = rows_in[base + 2, :LEVEL_ROWS]
        ref[SIDES_AT:] = packed
        if up:
            ref[PAIR_AT - 1 : PAIR_AT] = faces[rows - 1 :]

    even = lax.rem(lax.axis_index("lat"), 2) == 0

    @pl.when(even)
    def _():
        fill(message_a, True)
        fill(message_b, False)

    @pl.when(jnp.logical_not(even))
    def _():
        fill(message_a, False)
        fill(message_b, True)


def shifted(values):
    return turn(values, -1, 1), turn(values, 1, 1), turn(values, -1, 0), turn(values, 1, 0)


def face_planes(planes, limits, weights):
    deep, face = planes[0], planes[2]
    lane, row = iota(deep.shape, 1), iota(deep.shape, 0)
    rows, lanes = deep.shape
    edges = (lane == lanes - 1, lane == 0, row == rows - 1, row == 0)
    for number, (edge, values) in enumerate(zip(edges, shifted(deep))):
        limits[number] = jnp.where(edge, 0.0, jnp.minimum(deep, values))
    weights[0] = turn(face, 1, 1)
    weights[1] = turn(face, 1, 0)


def level_faces(level, place, planes, limits, weights):
    height = level.astype(jnp.float32)
    face = planes[2, place]
    return (
        height < planes[0, place],
        jnp.where(height < limits[0, place], face, 0.0),
        jnp.where(height < limits[1, place], weights[0, place], 0.0),
        jnp.where(height < limits[2, place], face, 0.0),
        jnp.where(height < limits[3, place], weights[1, place], 0.0),
    )


def smooth(ref, level, tile, tiles, faces):
    wet, face_east, face_west, face_north, face_south = faces
    start = tile * PAD
    item = ref[level, start : start + PAD]
    if tile + 1 < tiles:
        above = ref[level, start + 1 : start + 1 + PAD]
    else:
        above = turn(item, -1, 0)
    below = ref[level, start - 1 : start - 1 + PAD] if tile else turn(item, 1, 0)
    change = face_north * (above - item) + face_south * (below - item)
    change = change + face_east * (turn(item, -1, 1) - item)
    change = change + face_west * (turn(item, 1, 1) - item)
    return item, jnp.where(wet, item, 0.0) + change


def inner_kernel(
    planes, east, north, tracer, east_out, north_out, tracer_out, limits, weights
):
    levels, rows, lanes = tracer.shape
    tiles = rows // PAD
    face_planes(planes, limits, weights)
    for first in range(0, tiles, TILES):

        def step(group, carry):
            for t in range(GROUP):
                level = group * GROUP + t
                for tile in range(first, first + TILES):
                    place = slice(tile * PAD, (tile + 1) * PAD)
                    faces = level_faces(level, place, planes, limits, weights)
                    one, new_one = smooth(east, level, tile, tiles, faces)
                    two, new_two = smooth(north, level, tile, tiles, faces)
                    spin = jnp.where(faces[0], planes[4, place], 0.0)
                    east_out[level, place] = new_one - spin * two
                    north_out[level, place] = new_two + spin * one
                    tracer_out[level, place] = smooth(tracer, level, tile, tiles, faces)[1]
            return carry

        lax.fori_loop(0, levels // GROUP, step, 0)


def rim_kernel(
    got_0, got_1, wide, planes, face_west, edges, east, north, tracer,
    east_out, north_out, tracer_out, limits, faces,
    sides,
):
    levels, rows, lanes = east.shape
    from_west, from_east = received(got_0, got_1)
    lane = iota((rows, lanes), 1)
    deep, beside = wide[0, :, :lanes], wide[0, :, lanes:]
    level_of = lax.shift_right_logical(lane, 1).astype(jnp.float32)
    odd_lane = lax.rem(lane, 2) == 1
    limits[0] = deep
    limits[1] = jnp.minimum(deep, jnp.where(lane == lanes - 1, beside[:, 0:1], turn(deep, -1, 1)))
    limits[2] = jnp.minimum(deep, jnp.where(lane == 0, beside[:, lanes - 1 :], turn(deep, 1, 1)))
    limits[3] = jnp.minimum(deep, turn(deep, -1, 0))
    limits[4] = jnp.minimum(deep, turn(deep, 1, 0))
    faces[0] = planes[2]
    faces[1] = face_west[...]
    faces[2] = planes[2]
    faces[3] = turn(planes[2], 1, 0)
    bound_east = jnp.minimum(deep[:, lanes - 1 :], beside[:, 0:1])
    bound_west = jnp.minimum(deep[:, 0:1], beside[:, lanes - 1 :])
    weight = jnp.where(odd_lane, face_west[:, 0:1], planes[2, :, lanes - 1 :])
    weight = jnp.where(level_of < jnp.where(odd_lane, bound_west, bound_east), weight, 0.0)
    halos = (
        jnp.where(odd_lane, turn(from_west[:, :lanes], 1, 1), turn(from_east[:, :lanes], -1, 1)),
        jnp.where(odd_lane, from_west[:, :lanes], from_east[:, :lanes]),
        jnp.where(odd_lane, turn(from_west[:, lanes:], 1, 1), turn(from_east[:, lanes:], -1, 1)),
    )
    for number in range(3):
        sides[number] = turn(weight * (halos[number] - edges[number]), -1, 1)
    small_lane = iota((PAD, lanes), 1)
    rim = (small_lane == 0) | (small_lane == lanes - 1)
    tiles = rows // PAD
    pairs = ((east, east_out), (north, north_out), (tracer, tracer_out))
    for first in range(0, tiles, TILES):
        chunk = range(first, first + TILES)

        def step(group, rims):
            for t in range(GROUP):
                level = group * GROUP + t
                for number, tile in enumerate(chunk):
                    place = slice(tile * PAD, (tile + 1) * PAD)
                    for index, (source, target) in enumerate(pairs):
                        part = turn(rims[3 * number + index], -2 * t, 1)
                        target[level, place] = source[level, place] + jnp.where(rim, part, 0.0)
            return tuple(turn(item, -2 * GROUP, 1) for item in rims)

        lax.fori_loop(
            0, levels // GROUP, step,
            tuple(
                sides[number, tile * PAD : (tile + 1) * PAD] for tile in chunk for number in range(3)
            ),
        )


def basis_kernel(
    thickness, got_a, got_b, wide, rows_in, tracer_in, limits_in, faces_in,
    gram, basis, fixes, tracer, limits, faces,
    halo,
):
    rows, lanes = wide.shape[1], wide.shape[2] // 2
    lat = lax.axis_index("lat")
    even = lax.rem(lat, 2) == 0
    at_top = lat == lax.axis_size("lat") - 1
    at_bottom = lat == 0

    one, two = got_a[...], got_b[...]
    small_lane = iota((PAD, lanes), 1)
    near_side = (small_lane < WIDE) | (small_lane >= lanes - WIDE)

    def tiles_of(values, number):
        start = number * PAD
        first = values[start : start + PAD]
        if number < SIDE_GROUPS:
            second = turn(values[SIDES_AT:], -2 * WIDE * number - WIDE, 1)
            second = jnp.where(near_side, second, 0.0)
        else:
            start = start + LEVEL_ROWS
            second = values[start : start + PAD]
        return first, second

    groups = range(HALO_ROWS // PAD)
    above = jnp.where(even, one, two)

    @pl.when(at_top)
    def _():
        back = lanes - 1 - small_lane
        for number in groups:
            for tile, values in enumerate(tiles_of(above, number)):
                values = jnp.take_along_axis(values, back, axis=1)
                if number < 3:
                    values = jnp.concatenate(
                        [values[i : i + 1] for i in range(PAD - 1, -1, -1)], axis=0
                    )
                halo[0, number * PAD : (number + 1) * PAD, tile * lanes : (tile + 1) * lanes] = values

    @pl.when(jnp.logical_not(at_top))
    def _():
        for number in groups:
            for tile, values in enumerate(tiles_of(above, number)):
                halo[0, number * PAD : (number + 1) * PAD, tile * lanes : (tile + 1) * lanes] = values

    below = jnp.where(at_bottom, 0.0, jnp.where(even, two, one))
    for number in groups:
        for tile, values in enumerate(tiles_of(below, number)):
            halo[1, number * PAD : (number + 1) * PAD, tile * lanes : (tile + 1) * lanes] = values

    def whole(number):
        place = slice(number * PAD, (number + 1) * PAD)
        return jnp.concatenate([halo[1, place], wide[number], halo[0, place]], axis=0)

    deep, store, plane = whole(0), whole(1), whole(2)
    full = deep.shape
    row = iota(full, 0)
    core_end = PAD + rows
    level = iota((LEVEL_ROWS, full[1]), 0).astype(jnp.float32)
    bound = jnp.minimum(deep[core_end - 1 : core_end], deep[core_end : core_end + 1])
    edge = wide[3, :LEVEL_ROWS] - jnp.where(at_top, halo[0, RAW_AT:PAIR_AT], 0.0)
    flux = jnp.sum(jnp.where(level < bound, edge, 0.0), axis=0, keepdims=True)
    plane = plane + jnp.where(row == core_end - 1, flux, 0.0) - jnp.where(row == core_end, flux, 0.0)
    bound = jnp.minimum(deep[PAD - 1 : PAD], deep[PAD : PAD + 1])
    flux = jnp.sum(jnp.where(level < bound, halo[1, RAW_AT:PAIR_AT], 0.0), axis=0, keepdims=True)
    plane = plane + jnp.where(row == PAD - 1, flux, 0.0) - jnp.where(row == PAD, flux, 0.0)

    place = iota((PAD, lanes), 1)
    table = jnp.zeros((PAD, lanes), jnp.float32)
    for number in range(thickness.shape[0]):
        table = table + jnp.where(place > number, thickness[number], 0.0)

    def column(bound):
        index = bound.astype(jnp.int32)
        return jnp.concatenate(
            [
                jnp.concatenate(
                    [
                        jnp.take_along_axis(
                            table, index[i : i + PAD, j : j + lanes], axis=1
                        )
                        for j in range(0, full[1], lanes)
                    ],
                    axis=1,
                )
                for i in range(0, full[0], PAD)
            ],
            axis=0,
        )

    beside, _, above, _ = shifted(deep)
    to_east = column(jnp.minimum(deep, beside))
    to_north = column(jnp.minimum(deep, above))
    to_north = jnp.where(at_top & (row == core_end - 1), 2.0, 1.0) * to_north
    to_west, to_south = turn(to_east, 1, 1), turn(to_north, 1, 0)
    diag = store + to_east + to_west + to_north + to_south
    there = diag > 0.0
    inverse = jnp.where(there, 1.0 / jnp.where(there, diag, 1.0), 0.0)

    def operate(values):
        east_side, west_side, north_side, south_side = shifted(values)
        total = (
            store * values + to_east * (values - east_side) + to_west * (values - west_side)
        )
        return total + to_north * (values - north_side) + to_south * (values - south_side)

    vectors, images = [plane * inverse], []
    for number in range(4):
        images.append(operate(vectors[-1]))
        if number < 3:
            vectors.append(images[-1] * inverse - SHIFTS[number] * vectors[-1])
    for number in range(4):
        basis[number] = vectors[number]

    def core(values):
        return values[PAD:core_end, :lanes]

    sums = []
    for i in range(4):
        for j in range(i, 4):
            sums.append(core(vectors[i]) * core(images[j]))
    for i in range(4):
        sums.append(core(vectors[i]) * core(plane))
    sums = [jnp.sum(item, axis=0, keepdims=True) for item in sums]
    sums = sums + [jnp.zeros((1, lanes), jnp.float32)] * (16 - len(sums))
    sums = jnp.sum(jnp.concatenate(sums, axis=0), axis=1, keepdims=True)
    same = iota((16, lanes), 0) == iota((16, lanes), 1)
    line = jnp.sum(jnp.where(same, sums, 0.0), axis=0, keepdims=True)
    gram[...] = jnp.broadcast_to(line, gram.shape)

    level = level[:, :lanes]
    top_face = faces_in[2, rows - 1 :] + jnp.where(at_top, halo[0, PAIR_AT - 1 : PAIR_AT, :lanes], 0.0)
    low_face = halo[1, PAIR_AT - 1 : PAIR_AT, :lanes]
    for side, line, weight in ((0, core_end - 1, top_face), (1, PAD, low_face)):
        other = line + 1 - 2 * side
        bound = jnp.minimum(deep[line : line + 1], deep[other : other + 1])[:, :lanes]
        limits[3 + side, line - PAD : line - PAD + 1] = bound
        faces[2 + side, line - PAD : line - PAD + 1] = weight
        outer = (
            halo[side, PAIR_AT:, :lanes],
            halo[side, RAW_AT:PAIR_AT, :lanes],
            halo[side, PAIR_AT:, lanes:],
        )
        for number in range(3):
            inner = rows_in[3 * side + number, :LEVEL_ROWS]
            fixes[3 * side + number] = jnp.where(
                level < bound, weight * (outer[number] - inner), 0.0
            )
    for number in range(tracer.shape[0]):
        last = tracer_in[number, rows - 1 : rows] + fixes[2, number : number + 1]
        first = tracer_in[number, 0:1] + fixes[5, number : number + 1]
        tracer[number, rows - 1 : rows] = last
        tracer[number, 0:1] = first


def solve(line):
    entry = [jnp.broadcast_to(line[:, i : i + 1], line.shape) for i in range(14)]
    system = [[None] * 5 for _ in range(4)]
    for i in range(4):
        for j in range(i, 4):
            system[i][j] = entry.pop(0)
    for i in range(4):
        system[i][4] = entry.pop(0)
    factor, part = {}, []
    for k in range(4):
        pivot = system[k][k]
        usable = pivot > 0.0
        scale = jnp.where(usable, 1.0 / jnp.where(usable, pivot, 1.0), 0.0)
        part.append(system[k][4] * scale)
        for i in range(k + 1, 4):
            factor[i, k] = system[k][i] * scale
            for j in range(i, 5):
                system[i][j] = system[i][j] - factor[i, k] * system[k][j]
    for k in range(2, -1, -1):
        for i in range(k + 1, 4):
            part[k] = part[k] - factor[i, k] * part[i]
    return part


def final_kernel(
    thickness, totals, basis, planes_in, limits, faces, fixes, east, north, tracer,
    tracer_hbm, east_hbm, north_hbm, surface,
    planes, work, east_out, north_out, sems, tracer_sem,
):
    levels, rows, lanes = east.shape
    size = levels // OUT_PARTS
    core_end = PAD + rows
    outs = ((east_out, east_hbm), (north_out, north_hbm))

    def part_copy(number, part):
        place = pl.ds(part * size, size)
        source, target = outs[number]
        return pltpu.make_async_copy(source.at[place], target.at[place], sems.at[number, part])

    tracer_copy = pltpu.make_async_copy(tracer, tracer_hbm, tracer_sem)
    tracer_copy.start()
    at_top = lax.axis_index("lat") == lax.axis_size("lat") - 1
    parts = solve(jnp.sum(totals[...], axis=0, keepdims=True))
    tall = (rows + 2 * PAD, lanes)
    lane, row = iota(tall, 1), iota(tall, 0)

    def combine(start):
        total = parts[0] * basis[0, :, start : start + lanes]
        for number in range(1, 4):
            total = total + parts[number] * basis[number, :, start : start + lanes]
        return total

    inner, outer = combine(0), combine(lanes)
    surface[...] = planes_in[1] * inner[PAD:core_end]

    def to_east(first, second):
        return jnp.where(lane[: first.shape[0]] == lanes - 1, turn(second, -1, 1), turn(first, -1, 1))

    def to_west(first, second):
        return jnp.where(lane[: first.shape[0]] == 0, turn(second, 1, 1), turn(first, 1, 1))

    end = slice(core_end, core_end + PAD)
    fold = at_top & (row[:PAD] == 0)

    def slopes(first, second):
        along = to_east(first, second)
        across = turn(first, -1, 0)
        along_end = jnp.where(fold, to_west(first[end], second[end]), along[end])
        across_end = jnp.where(fold, turn(first, 1, 0)[end], across[end])
        along = jnp.concatenate([along[:core_end], along_end], axis=0)
        across = jnp.concatenate([across[:core_end], across_end], axis=0)
        return along - first, across - first

    inner_x, inner_y = slopes(inner, outer)
    outer_x, outer_y = slopes(outer, inner)
    core = slice(PAD, core_end)
    spin = planes_in[4]
    planes[0] = inner_x[core] - spin * inner_y[core]
    planes[1] = inner_y[core] + spin * inner_x[core]
    for start, first, second in ((2, inner_x, outer_x), (6, inner_y, outer_y)):
        work[...] = first
        own = first[core]
        sides = (
            to_east(own, second[core]), to_west(own, second[core]),
            work[PAD + 1 : core_end + 1], work[PAD - 1 : core_end - 1],
        )
        for number, item in enumerate(sides):
            planes[start + number] = faces[number] * (own - item)

    line = iota((PAD, lanes), 0)
    first_line, last_line = line == 0, line == PAD - 1

    def part_step(part, carry):
        for tile in range(rows // PAD):
            place = slice(tile * PAD, (tile + 1) * PAD)
            bounds = [limits[number, place] for number in range(5)]
            own = [planes[number, place] for number in range(10)]
            for t in range(size):
                level = part * size + t
                height = level.astype(jnp.float32)
                open_sides = [height < bound for bound in bounds]
                for out, values, base, start, number in (
                    (east_out, east, 0, 2, 0), (north_out, north, 1, 6, 1)
                ):
                    change = jnp.where(open_sides[0], own[base], 0.0)
                    for side in range(4):
                        change = change - jnp.where(open_sides[1 + side], own[start + side], 0.0)
                    result = values[level, place] + thickness[level] * change
                    if tile == 0:
                        fix = fixes[3 + number, pl.ds(level, 1), :]
                        result = result + jnp.where(first_line, fix, 0.0)
                    if tile == rows // PAD - 1:
                        fix = fixes[number, pl.ds(level, 1), :]
                        result = result + jnp.where(last_line, fix, 0.0)
                    out[level, place] = result
        part_copy(0, part).start()
        part_copy(1, part).start()
        return carry

    lax.fori_loop(0, OUT_PARTS, part_step, 0)
    tracer_copy.wait()
    for part in range(OUT_PARTS):
        part_copy(0, part).wait()
        part_copy(1, part).wait()


def swaps(lats, lons, odd):
    pairs = []
    for lat in range(lats):
        for lon in range(lons):
            other = lat + 1 if lat % 2 == odd else lat - 1
            if other < 0:
                pairs.append((lon, (lon ^ 1) % lons))
            elif other == lats:
                pairs.append((lat * lons + lon, lat * lons + lons - 1 - lon))
            else:
                pairs.append((lat * lons + lon, other * lons + lon))
    return pairs


def lon_swaps(lons, odd):
    return [(lon, (lon + (1 if lon % 2 == odd else -1)) % lons) for lon in range(lons)]


def local(
    tracer_cot, east_cot, north_cot, surface_cot, depth_levels, diffusivity, coriolis, storage,
    thickness,
):
    levels, rows, lanes = tracer_cot.shape
    lats, lons = lax.axis_size("lat"), lax.axis_size("lon")
    far = lambda value: pltpu.with_memory_space_constraint(value, pltpu.HBM)
    near = lambda value: pltpu.with_memory_space_constraint(value, pltpu.VMEM)
    floats = lambda *shape: pltpu.HBM(shape, jnp.float32)
    scratch = lambda *shape: pltpu.VMEM(shape, jnp.float32)
    scalars = pl.BlockSpec(memory_space=pltpu.SMEM)
    in_hbm = pl.BlockSpec(memory_space=pltpu.HBM)
    in_vmem = pl.BlockSpec(memory_space=pltpu.VMEM)
    params = pltpu.CompilerParams(vmem_limit_bytes=VMEM_BYTES)
    cost = lambda work: pl.CostEstimate(
        flops=work * levels * rows * lanes, bytes_accessed=8 * levels * rows * lanes,
        transcendentals=0,
    )
    plane, pair, field = (rows, lanes), (rows, 2 * lanes), (levels, rows, lanes)
    full = (rows + 2 * PAD, 2 * lanes)
    message, strips = (MESSAGE_ROWS, lanes), (2, HALO_ROWS, 2 * lanes)

    message_0, message_1, planes, edge_rows, edges, east, north, tracer = pl.pallas_call(
        pack_kernel,
        in_specs=[in_hbm] * 8,
        out_specs=[in_vmem] * 8,
        out_shape=[
            scratch(*pair), scratch(*pair), scratch(5, *plane), scratch(6, *plane),
            scratch(3, *plane), scratch(*field), scratch(*field), scratch(*field),
        ],
        scratch_shapes=[
            pltpu.VMEM(plane, jnp.int32), scratch(*plane), scratch(*plane), scratch(*plane),
            scratch(2, *plane), pltpu.SemaphoreType.DMA((3, PARTS)), pltpu.SemaphoreType.DMA((5,)),
        ],
        compiler_params=params,
        name="pack",
    )(
        *[
            far(item)
            for item in (
                east_cot, north_cot, tracer_cot, depth_levels, storage, surface_cot, diffusivity,
                coriolis,
            )
        ]
    )

    got_1 = lax.ppermute(message_1, "lon", lon_swaps(lons, 1))
    got_0 = lax.ppermute(message_0, "lon", lon_swaps(lons, 0))

    east_part, north_part, tracer_part = pl.pallas_call(
        inner_kernel,
        in_specs=[in_vmem] * 4,
        out_specs=[in_vmem] * 3,
        out_shape=[scratch(*field)] * 3,
        scratch_shapes=[scratch(4, *plane), scratch(2, *plane)],
        compiler_params=params,
        cost_estimate=cost(60),
        name="inner",
    )(near(planes), near(east), near(north), near(tracer))

    edges, east_part = lax.optimization_barrier((edges, east_part))
    got_0, got_1 = near(got_0), near(got_1)
    wide, face_west, message_a, message_b = pl.pallas_call(
        stitch_kernel,
        in_specs=[in_vmem] * 5,
        out_specs=[in_vmem] * 4,
        out_shape=[scratch(4, *pair), scratch(*plane), scratch(*message), scratch(*message)],
        compiler_params=params,
        name="stitch",
    )(got_0, got_1, near(planes), near(edge_rows), near(edges))

    got_b = lax.ppermute(message_b, BOTH, swaps(lats, lons, 1))
    got_a = lax.ppermute(message_a, BOTH, swaps(lats, lons, 0))

    east_part, north_part, tracer_part, limits, faces = pl.pallas_call(
        rim_kernel,
        in_specs=[in_vmem] * 9,
        out_specs=[in_vmem] * 5,
        out_shape=[scratch(*field)] * 3 + [scratch(5, *plane), scratch(4, *plane)],
        scratch_shapes=[scratch(3, *plane)],
        input_output_aliases={6: 0, 7: 1, 8: 2},
        compiler_params=params,
        cost_estimate=cost(10),
        name="rim",
    )(
        got_0, got_1, near(wide), near(planes), near(face_west), near(edges), near(east_part),
        near(north_part), near(tracer_part),
    )

    wide, east_part = lax.optimization_barrier((wide, east_part))
    gram, basis, fixes, tracer_part, limits, faces = pl.pallas_call(
        basis_kernel,
        in_specs=[scalars] + [in_vmem] * 7,
        out_specs=[in_vmem] * 6,
        out_shape=[
            scratch(lats * lons, lanes), scratch(4, *full), scratch(6, LEVEL_ROWS, lanes),
            scratch(*field), scratch(5, *plane), scratch(4, *plane),
        ],
        scratch_shapes=[scratch(*strips)],
        input_output_aliases={5: 3, 6: 4, 7: 5},
        compiler_params=params,
        name="basis",
    )(
        thickness, near(got_a), near(got_b), near(wide), near(edge_rows), near(tracer_part),
        near(limits), near(faces),
    )

    totals = lax.all_to_all(gram, BOTH, 0, 0, tiled=True)

    tracer_adj, east_adj, north_adj, surface_adj = pl.pallas_call(
        final_kernel,
        in_specs=[scalars] + [in_vmem] * 9,
        out_specs=[in_hbm] * 3 + [in_vmem],
        out_shape=[floats(*field)] * 3 + [jax.ShapeDtypeStruct(plane, jnp.float32)],
        scratch_shapes=[
            scratch(10, *plane), scratch(rows + 2 * PAD, lanes), scratch(*field), scratch(*field),
            pltpu.SemaphoreType.DMA((2, OUT_PARTS)), pltpu.SemaphoreType.DMA,
        ],
        compiler_params=params,
        name="final",
    )(
        thickness, near(totals), near(basis), near(planes), near(limits), near(faces), near(fixes),
        near(east_part), near(north_part), near(tracer_part),
    )
    return tracer_adj, east_adj, north_adj, surface_adj


def solution(mesh):
    field, plane = P(None, "lat", "lon"), P("lat", "lon")
    return jax.shard_map(
        local,
        mesh=mesh,
        in_specs=(field, field, field, plane, plane, plane, plane, plane, P()),
        out_specs=(field, field, field, plane),
        check_vma=False,
    )
```

```python
import jax
import jax.numpy as jnp
from jax import lax
from jax.experimental import pallas as pl
from jax.experimental.pallas import tpu as pltpu
from jax.sharding import PartitionSpec as P

WIDE = 6
PAD = 8
SHIFTS = (1.0, 0.3, 1.7)
PARTS = 5
OUT_PARTS = 5
LANES = 128
GROUP = 5
TILES = 8
BOTH = ("lat", "lon")
VMEM_BYTES = 32 * 1024 * 1024

DEPTH_AT, STORE_AT, SOURCE_AT, STRIP_AT, DIFF_AT = 100, 106, 112, 118, 124
LEVEL_ROWS = 56
RAW_AT = 3 * PAD
PAIR_AT = RAW_AT + LEVEL_ROWS
HALO_ROWS = PAIR_AT + LEVEL_ROWS
SIDES_AT = HALO_ROWS + LEVEL_ROWS
MESSAGE_ROWS = SIDES_AT + PAD
SIDE_GROUPS = PAIR_AT // PAD


def iota(shape, dim):
    return lax.broadcasted_iota(jnp.int32, shape, dim)


def turn(values, shift, dim):
    return pltpu.roll(values, shift % values.shape[dim], dim)


def pack_kernel(
    east_in, north_in, tracer_in, depth_in, storage_in, surf_in, diff_in, spin_in,
    message_0, message_1, planes, rows_out, edges, east, north, tracer,
    depth, surf, px, py, bounds, field_sems, plane_sems,
):
    levels, rows, lanes = east.shape
    size = levels // PARTS
    sources, fields = (east_in, north_in, tracer_in), (east, north, tracer)

    def part_copy(number, part):
        place = pl.ds(part * size, size)
        return pltpu.make_async_copy(
            sources[number].at[place], fields[number].at[place], field_sems.at[number, part]
        )

    moves = [
        pltpu.make_async_copy(source, target, plane_sems.at[number])
        for number, (source, target) in enumerate(
            (
                (depth_in, depth), (storage_in, planes.at[1]), (surf_in, surf),
                (diff_in, planes.at[2]), (spin_in, planes.at[4]),
            )
        )
    ]
    for move in moves:
        move.start()
    for part in range(PARTS):
        for number in range(3):
            part_copy(number, part).start(priority=min(part, 1))
    rows_out[:, levels - levels % PAD :] = jnp.zeros((6, rows - levels + levels % PAD, lanes), jnp.float32)
    px[...] = jnp.zeros((rows, lanes), jnp.float32)
    py[...] = jnp.zeros((rows, lanes), jnp.float32)
    edges[...] = jnp.zeros((3, rows, lanes), jnp.float32)
    for move in moves:
        move.wait()
    lane = iota((rows, lanes), 1)
    row = iota((rows, lanes), 0)
    deep = depth[...].astype(jnp.float32)
    planes[0] = deep
    bounds[0] = jnp.where(lane == lanes - 1, 0.0, jnp.minimum(deep, turn(deep, -1, 1)))
    bounds[1] = jnp.where(row == rows - 1, 0.0, jnp.minimum(deep, turn(deep, -1, 0)))
    pair_lane = lax.shift_right_logical(iota((PAD, lanes), 1), 1)

    for part in range(PARTS):
        for number in range(3):
            part_copy(number, part).wait()
        for t in range(size):
            level = part * size + t
            for number, ref in enumerate(fields):
                rows_out[number, level : level + 1, :] = ref[level, rows - 1 : rows, :]
                rows_out[3 + number, level : level + 1, :] = ref[level, 0:1, :]
        for tile in range(rows // PAD):
            place = slice(tile * PAD, (tile + 1) * PAD)
            sum_x, sum_y = px[place], py[place]
            limit_x, limit_y = bounds[0, place], bounds[1, place]
            ends = [edges[number, place] for number in range(3)]
            for t in range(size):
                level = part * size + t
                here = pair_lane == level
                values = [ref[level, place] for ref in fields]
                for number in range(3):
                    moved = turn(values[number], 2 * level + 1, 1)
                    ends[number] = jnp.where(here, moved, ends[number])
                sum_x = sum_x + jnp.where(limit_x > level, values[0], 0.0)
                sum_y = sum_y + jnp.where(limit_y > level, values[1], 0.0)
            px[place], py[place] = sum_x, sum_y
            for number in range(3):
                edges[number, place] = ends[number]

    plane = surf[...] + px[...] - turn(px[...], 1, 1) + py[...] - turn(py[...], 1, 0)
    planes[3] = plane
    odd_lane = lax.rem(lane, 2) == 1

    def put(target, values, start, place, count):
        moved = turn(values, place - start, 1)
        return jnp.where((lane >= place) & (lane < place + count), moved, target)

    half = rows // 2

    def fill(ref, eastward):
        if eastward:
            tile = jnp.where(odd_lane, turn(edges[1], 1, 1), edges[0])
            ref[rows:] = jnp.where(odd_lane[half:], turn(edges[2, half:], 1, 1), edges[2, :half])
        else:
            tile = jnp.where(odd_lane, edges[0], turn(edges[1], -1, 1))
            ref[rows:] = jnp.where(odd_lane[half:], edges[2, :half], turn(edges[2, half:], -1, 1))
        start = lanes - WIDE if eastward else 0
        for values, place in (
            (deep, DEPTH_AT), (planes[1], STORE_AT), (plane, SOURCE_AT), (rows_out[1], STRIP_AT)
        ):
            tile = put(tile, values, start, place, WIDE)
        ref[:rows] = put(tile, planes[2], lanes - 1, DIFF_AT, 1)

    odd = lax.rem(lax.axis_index("lon"), 2) == 1

    @pl.when(odd)
    def _():
        fill(message_0, True)
        fill(message_1, False)

    @pl.when(jnp.logical_not(odd))
    def _():
        fill(message_0, False)
        fill(message_1, True)


def received(got_0, got_1):
    odd = lax.rem(lax.axis_index("lon"), 2) == 1
    one, two = got_0[...], got_1[...]
    return jnp.where(odd, two, one), jnp.where(odd, one, two)


def stitch_kernel(
    got_0, got_1, planes, rows_in, edges,
    wide, face_west, message_a, message_b,
):
    rows, lanes = planes.shape[1:]
    from_west, from_east = received(got_0, got_1)
    lane = iota((rows, lanes), 1)
    left_tile, right_tile = from_west[:rows], from_east[:rows]

    def side(place):
        right = turn(right_tile, -place, 1)
        left = turn(left_tile, lanes - WIDE - place, 1)
        return jnp.where(lane < WIDE, right, jnp.where(lane >= lanes - WIDE, left, 0.0))

    deep, deep_side = planes[0], side(DEPTH_AT)
    store, store_side = planes[1], side(STORE_AT)
    plane, plane_side = planes[3], side(SOURCE_AT)
    strip = side(STRIP_AT)
    level = lax.shift_right_logical(lane, 1).astype(jnp.float32)
    even_lane = lax.rem(lane, 2) == 0

    def flux(values, bound):
        used = even_lane & (level < bound)
        return jnp.sum(jnp.where(used, values, 0.0), axis=1, keepdims=True)

    flux_east = flux(edges[0], jnp.minimum(deep[:, lanes - 1 :], deep_side[:, 0:1]))
    flux_west = flux(left_tile, jnp.minimum(deep_side[:, lanes - 1 :], deep[:, 0:1]))
    first, last = lane == 0, lane == lanes - 1
    plane = plane + jnp.where(last, flux_east, 0.0) - jnp.where(first, flux_west, 0.0)
    plane_side = plane_side - jnp.where(first, flux_east, 0.0) + jnp.where(last, flux_west, 0.0)
    both = ((deep, deep_side), (store, store_side), (plane, plane_side), (rows_in[1], strip))
    for number, (one, two) in enumerate(both):
        wide[number, :, :lanes] = one
        wide[number, :, lanes:] = two
    faces = planes[2]
    face_west[...] = jnp.where(first, turn(left_tile, -DIFF_AT, 1), turn(faces, 1, 1))

    small_lane = iota((PAD, lanes), 1)

    def fill(ref, up):
        start = rows - PAD if up else 0
        base = 0 if up else 3
        groups = [two[start : start + PAD] for _, two in both[:3]]
        groups = groups + [strip[i : i + PAD] for i in range(0, LEVEL_ROWS, PAD)]
        packed = jnp.zeros((PAD, lanes), jnp.float32)
        for number, item in enumerate(groups):
            place = 2 * WIDE * number
            here = (small_lane >= place) & (small_lane < place + 2 * WIDE)
            packed = jnp.where(here, turn(item, place + WIDE, 1), packed)
        for number, (one, _) in enumerate(both[:3]):
            ref[number * PAD : (number + 1) * PAD] = one[start : start + PAD]
        ref[RAW_AT:PAIR_AT] = rows_in[base + 1, :LEVEL_ROWS]
        ref[PAIR_AT:HALO_ROWS] = rows_in[base, :LEVEL_ROWS]
        ref[HALO_ROWS:SIDES_AT] = rows_in[base + 2, :LEVEL_ROWS]
        ref[SIDES_AT:] = packed
        if up:
            ref[PAIR_AT - 1 : PAIR_AT] = faces[rows - 1 :]

    even = lax.rem(lax.axis_index("lat"), 2) == 0

    @pl.when(even)
    def _():
        fill(message_a, True)
        fill(message_b, False)

    @pl.when(jnp.logical_not(even))
    def _():
        fill(message_a, False)
        fill(message_b, True)


def shifted(values):
    return turn(values, -1, 1), turn(values, 1, 1), turn(values, -1, 0), turn(values, 1, 0)


def face_planes(planes, limits, weights):
    deep, face = planes[0], planes[2]
    lane, row = iota(deep.shape, 1), iota(deep.shape, 0)
    rows, lanes = deep.shape
    edges = (lane == lanes - 1, lane == 0, row == rows - 1, row == 0)
    for number, (edge, values) in enumerate(zip(edges, shifted(deep))):
        limits[number] = jnp.where(edge, 0.0, jnp.minimum(deep, values))
    weights[0] = turn(face, 1, 1)
    weights[1] = turn(face, 1, 0)


def level_faces(level, place, planes, limits, weights):
    height = level.astype(jnp.float32)
    face = planes[2, place]
    return (
        height < planes[0, place],
        jnp.where(height < limits[0, place], face, 0.0),
        jnp.where(height < limits[1, place], weights[0, place], 0.0),
        jnp.where(height < limits[2, place], face, 0.0),
        jnp.where(height < limits[3, place], weights[1, place], 0.0),
    )


def smooth(ref, level, tile, tiles, faces):
    wet, face_east, face_west, face_north, face_south = faces
    start = tile * PAD
    item = ref[level, start : start + PAD]
    if tile + 1 < tiles:
        above = ref[level, start + 1 : start + 1 + PAD]
    else:
        above = turn(item, -1, 0)
    below = ref[level, start - 1 : start - 1 + PAD] if tile else turn(item, 1, 0)
    change = face_north * (above - item) + face_south * (below - item)
    change = change + face_east * (turn(item, -1, 1) - item)
    change = change + face_west * (turn(item, 1, 1) - item)
    return item, jnp.where(wet, item, 0.0) + change


def inner_kernel(
    planes, east, north, tracer, east_out, north_out, tracer_out, limits, weights
):
    levels, rows, lanes = tracer.shape
    tiles = rows // PAD
    face_planes(planes, limits, weights)
    for first in range(0, tiles, TILES):

        def step(group, carry):
            for t in range(GROUP):
                level = group * GROUP + t
                for tile in range(first, first + TILES):
                    place = slice(tile * PAD, (tile + 1) * PAD)
                    faces = level_faces(level, place, planes, limits, weights)
                    one, new_one = smooth(east, level, tile, tiles, faces)
                    two, new_two = smooth(north, level, tile, tiles, faces)
                    spin = jnp.where(faces[0], planes[4, place], 0.0)
                    east_out[level, place] = new_one - spin * two
                    north_out[level, place] = new_two + spin * one
                    tracer_out[level, place] = smooth(tracer, level, tile, tiles, faces)[1]
            return carry

        lax.fori_loop(0, levels // GROUP, step, 0)


def rim_kernel(
    got_0, got_1, wide, planes, face_west, edges, east, north, tracer,
    east_out, north_out, tracer_out, limits, faces,
    sides,
):
    levels, rows, lanes = east.shape
    from_west, from_east = received(got_0, got_1)
    lane = iota((rows, lanes), 1)
    deep, beside = wide[0, :, :lanes], wide[0, :, lanes:]
    level_of = lax.shift_right_logical(lane, 1).astype(jnp.float32)
    odd_lane = lax.rem(lane, 2) == 1
    limits[0] = deep
    limits[1] = jnp.minimum(deep, jnp.where(lane == lanes - 1, beside[:, 0:1], turn(deep, -1, 1)))
    limits[2] = jnp.minimum(deep, jnp.where(lane == 0, beside[:, lanes - 1 :], turn(deep, 1, 1)))
    limits[3] = jnp.minimum(deep, turn(deep, -1, 0))
    limits[4] = jnp.minimum(deep, turn(deep, 1, 0))
    faces[0] = planes[2]
    faces[1] = face_west[...]
    faces[2] = planes[2]
    faces[3] = turn(planes[2], 1, 0)
    bound_east = jnp.minimum(deep[:, lanes - 1 :], beside[:, 0:1])
    bound_west = jnp.minimum(deep[:, 0:1], beside[:, lanes - 1 :])
    weight = jnp.where(odd_lane, face_west[:, 0:1], planes[2, :, lanes - 1 :])
    weight = jnp.where(level_of < jnp.where(odd_lane, bound_west, bound_east), weight, 0.0)
    left, right = from_west[:rows], from_east[:rows]
    left_half, right_half = from_west[rows:], from_east[rows:]
    half = odd_lane[: rows // 2]
    halos = (
        jnp.where(odd_lane, turn(left, 1, 1), turn(right, -1, 1)),
        jnp.where(odd_lane, left, right),
        jnp.concatenate(
            [
                jnp.where(half, turn(left_half, 1, 1), turn(right_half, -1, 1)),
                jnp.where(half, left_half, right_half),
            ],
            axis=0,
        ),
    )
    for number in range(3):
        sides[number] = turn(weight * (halos[number] - edges[number]), -1, 1)
    small_lane = iota((PAD, lanes), 1)
    rim = (small_lane == 0) | (small_lane == lanes - 1)
    tiles = rows // PAD
    pairs = ((east, east_out), (north, north_out), (tracer, tracer_out))
    for first in range(0, tiles, TILES):
        chunk = range(first, first + TILES)

        def step(group, rims):
            for t in range(GROUP):
                level = group * GROUP + t
                for number, tile in enumerate(chunk):
                    place = slice(tile * PAD, (tile + 1) * PAD)
                    for index, (source, target) in enumerate(pairs):
                        part = turn(rims[3 * number + index], -2 * t, 1)
                        target[level, place] = source[level, place] + jnp.where(rim, part, 0.0)
            return tuple(turn(item, -2 * GROUP, 1) for item in rims)

        lax.fori_loop(
            0, levels // GROUP, step,
            tuple(
                sides[number, tile * PAD : (tile + 1) * PAD] for tile in chunk for number in range(3)
            ),
        )


def basis_kernel(
    thickness, got_a, got_b, wide, rows_in, tracer_in, limits_in, faces_in,
    gram, basis, fixes, tracer, limits, faces,
    halo,
):
    rows, lanes = wide.shape[1], wide.shape[2] // 2
    lat = lax.axis_index("lat")
    even = lax.rem(lat, 2) == 0
    at_top = lat == lax.axis_size("lat") - 1
    at_bottom = lat == 0

    one, two = got_a[...], got_b[...]
    small_lane = iota((PAD, lanes), 1)
    near_side = (small_lane < WIDE) | (small_lane >= lanes - WIDE)

    def tiles_of(values, number):
        start = number * PAD
        first = values[start : start + PAD]
        if number < SIDE_GROUPS:
            second = turn(values[SIDES_AT:], -2 * WIDE * number - WIDE, 1)
            second = jnp.where(near_side, second, 0.0)
        else:
            start = start + LEVEL_ROWS
            second = values[start : start + PAD]
        return first, second

    groups = range(HALO_ROWS // PAD)
    above = jnp.where(even, one, two)

    @pl.when(at_top)
    def _():
        back = lanes - 1 - small_lane
        for number in groups:
            for tile, values in enumerate(tiles_of(above, number)):
                values = jnp.take_along_axis(values, back, axis=1)
                if number < 3:
                    values = jnp.concatenate(
                        [values[i : i + 1] for i in range(PAD - 1, -1, -1)], axis=0
                    )
                halo[0, number * PAD : (number + 1) * PAD, tile * lanes : (tile + 1) * lanes] = values

    @pl.when(jnp.logical_not(at_top))
    def _():
        for number in groups:
            for tile, values in enumerate(tiles_of(above, number)):
                halo[0, number * PAD : (number + 1) * PAD, tile * lanes : (tile + 1) * lanes] = values

    below = jnp.where(at_bottom, 0.0, jnp.where(even, two, one))
    for number in groups:
        for tile, values in enumerate(tiles_of(below, number)):
            halo[1, number * PAD : (number + 1) * PAD, tile * lanes : (tile + 1) * lanes] = values

    def whole(number):
        place = slice(number * PAD, (number + 1) * PAD)
        return jnp.concatenate([halo[1, place], wide[number], halo[0, place]], axis=0)

    deep, store, plane = whole(0), whole(1), whole(2)
    full = deep.shape
    row = iota(full, 0)
    core_end = PAD + rows
    level = iota((LEVEL_ROWS, full[1]), 0).astype(jnp.float32)
    bound = jnp.minimum(deep[core_end - 1 : core_end], deep[core_end : core_end + 1])
    edge = wide[3, :LEVEL_ROWS] - jnp.where(at_top, halo[0, RAW_AT:PAIR_AT], 0.0)
    flux = jnp.sum(jnp.where(level < bound, edge, 0.0), axis=0, keepdims=True)
    plane = plane + jnp.where(row == core_end - 1, flux, 0.0) - jnp.where(row == core_end, flux, 0.0)
    bound = jnp.minimum(deep[PAD - 1 : PAD], deep[PAD : PAD + 1])
    flux = jnp.sum(jnp.where(level < bound, halo[1, RAW_AT:PAIR_AT], 0.0), axis=0, keepdims=True)
    plane = plane + jnp.where(row == PAD - 1, flux, 0.0) - jnp.where(row == PAD, flux, 0.0)

    place = iota((PAD, lanes), 1)
    table = jnp.zeros((PAD, lanes), jnp.float32)
    for number in range(thickness.shape[0]):
        table = table + jnp.where(place > number, thickness[number], 0.0)

    def column(bound):
        index = bound.astype(jnp.int32)
        return jnp.concatenate(
            [
                jnp.concatenate(
                    [
                        jnp.take_along_axis(
                            table, index[i : i + PAD, j : j + lanes], axis=1
                        )
                        for j in range(0, full[1], lanes)
                    ],
                    axis=1,
                )
                for i in range(0, full[0], PAD)
            ],
            axis=0,
        )

    beside, _, above, _ = shifted(deep)
    to_east = column(jnp.minimum(deep, beside))
    to_north = column(jnp.minimum(deep, above))
    to_north = jnp.where(at_top & (row == core_end - 1), 2.0, 1.0) * to_north
    to_west, to_south = turn(to_east, 1, 1), turn(to_north, 1, 0)
    diag = store + to_east + to_west + to_north + to_south
    there = diag > 0.0
    inverse = jnp.where(there, 1.0 / jnp.where(there, diag, 1.0), 0.0)

    def operate(values):
        east_side, west_side, north_side, south_side = shifted(values)
        total = (
            store * values + to_east * (values - east_side) + to_west * (values - west_side)
        )
        return total + to_north * (values - north_side) + to_south * (values - south_side)

    vectors, images = [plane * inverse], []
    for number in range(4):
        images.append(operate(vectors[-1]))
        if number < 3:
            vectors.append(images[-1] * inverse - SHIFTS[number] * vectors[-1])
    for number in range(4):
        basis[number] = vectors[number]

    def core(values):
        return values[PAD:core_end, :lanes]

    sums = []
    for i in range(4):
        for j in range(i, 4):
            sums.append(core(vectors[i]) * core(images[j]))
    for i in range(4):
        sums.append(core(vectors[i]) * core(plane))
    sums = [jnp.sum(item, axis=0, keepdims=True) for item in sums]
    sums = sums + [jnp.zeros((1, lanes), jnp.float32)] * (16 - len(sums))
    sums = jnp.sum(jnp.concatenate(sums, axis=0), axis=1, keepdims=True)
    same = iota((16, lanes), 0) == iota((16, lanes), 1)
    line = jnp.sum(jnp.where(same, sums, 0.0), axis=0, keepdims=True)
    gram[...] = jnp.broadcast_to(line, gram.shape)

    level = level[:, :lanes]
    top_face = faces_in[2, rows - 1 :] + jnp.where(at_top, halo[0, PAIR_AT - 1 : PAIR_AT, :lanes], 0.0)
    low_face = halo[1, PAIR_AT - 1 : PAIR_AT, :lanes]
    for side, line, weight in ((0, core_end - 1, top_face), (1, PAD, low_face)):
        other = line + 1 - 2 * side
        bound = jnp.minimum(deep[line : line + 1], deep[other : other + 1])[:, :lanes]
        limits[3 + side, line - PAD : line - PAD + 1] = bound
        faces[2 + side, line - PAD : line - PAD + 1] = weight
        outer = (
            halo[side, PAIR_AT:, :lanes],
            halo[side, RAW_AT:PAIR_AT, :lanes],
            halo[side, PAIR_AT:, lanes:],
        )
        for number in range(3):
            inner = rows_in[3 * side + number, :LEVEL_ROWS]
            fixes[3 * side + number] = jnp.where(
                level < bound, weight * (outer[number] - inner), 0.0
            )
    for number in range(tracer.shape[0]):
        last = tracer_in[number, rows - 1 : rows] + fixes[2, number : number + 1]
        first = tracer_in[number, 0:1] + fixes[5, number : number + 1]
        tracer[number, rows - 1 : rows] = last
        tracer[number, 0:1] = first


def solve(line):
    entry = [jnp.broadcast_to(line[:, i : i + 1], line.shape) for i in range(14)]
    system = [[None] * 5 for _ in range(4)]
    for i in range(4):
        for j in range(i, 4):
            system[i][j] = entry.pop(0)
    for i in range(4):
        system[i][4] = entry.pop(0)
    factor, part = {}, []
    for k in range(4):
        pivot = system[k][k]
        usable = pivot > 0.0
        scale = jnp.where(usable, 1.0 / jnp.where(usable, pivot, 1.0), 0.0)
        part.append(system[k][4] * scale)
        for i in range(k + 1, 4):
            factor[i, k] = system[k][i] * scale
            for j in range(i, 5):
                system[i][j] = system[i][j] - factor[i, k] * system[k][j]
    for k in range(2, -1, -1):
        for i in range(k + 1, 4):
            part[k] = part[k] - factor[i, k] * part[i]
    return part


def final_kernel(
    thickness, totals, basis, planes_in, limits, faces, fixes, east, north, tracer,
    tracer_hbm, east_hbm, north_hbm, surface,
    planes, bounds_at, work, east_out, north_out, sems, tracer_sem,
):
    levels, rows, lanes = east.shape
    size = levels // OUT_PARTS
    core_end = PAD + rows
    outs = ((east_out, east_hbm), (north_out, north_hbm))

    def part_copy(number, part):
        place = pl.ds(part * size, size)
        source, target = outs[number]
        return pltpu.make_async_copy(source.at[place], target.at[place], sems.at[number, part])

    tracer_copy = pltpu.make_async_copy(tracer, tracer_hbm, tracer_sem)
    tracer_copy.start()
    at_top = lax.axis_index("lat") == lax.axis_size("lat") - 1
    parts = solve(jnp.sum(totals[...], axis=0, keepdims=True))
    tall = (rows + 2 * PAD, lanes)
    lane, row = iota(tall, 1), iota(tall, 0)

    def combine(start):
        total = parts[0] * basis[0, :, start : start + lanes]
        for number in range(1, 4):
            total = total + parts[number] * basis[number, :, start : start + lanes]
        return total

    inner, outer = combine(0), combine(lanes)
    surface[...] = planes_in[1] * inner[PAD:core_end]

    def to_east(first, second):
        return jnp.where(lane[: first.shape[0]] == lanes - 1, turn(second, -1, 1), turn(first, -1, 1))

    def to_west(first, second):
        return jnp.where(lane[: first.shape[0]] == 0, turn(second, 1, 1), turn(first, 1, 1))

    end = slice(core_end, core_end + PAD)
    fold = at_top & (row[:PAD] == 0)

    def slopes(first, second):
        along = to_east(first, second)
        across = turn(first, -1, 0)
        along_end = jnp.where(fold, to_west(first[end], second[end]), along[end])
        across_end = jnp.where(fold, turn(first, 1, 0)[end], across[end])
        along = jnp.concatenate([along[:core_end], along_end], axis=0)
        across = jnp.concatenate([across[:core_end], across_end], axis=0)
        return along - first, across - first

    inner_x, inner_y = slopes(inner, outer)
    outer_x, outer_y = slopes(outer, inner)
    core = slice(PAD, core_end)
    spin = planes_in[4]
    planes[0] = inner_x[core] - spin * inner_y[core]
    planes[1] = inner_y[core] + spin * inner_x[core]
    for start, first, second in ((2, inner_x, outer_x), (6, inner_y, outer_y)):
        work[...] = first
        own = first[core]
        sides = (
            to_east(own, second[core]), to_west(own, second[core]),
            work[PAD + 1 : core_end + 1], work[PAD - 1 : core_end - 1],
        )
        for number, item in enumerate(sides):
            planes[start + number] = faces[number] * (own - item)

    for tile in range(rows // PAD):
        place = slice(tile * PAD, (tile + 1) * PAD)
        keys = [limits[1 + number, place] for number in range(4)]
        sides_of = [[planes[start + number, place] for number in range(4)] for start in (2, 6)]
        for one, two in ((0, 1), (2, 3), (0, 2), (1, 3), (1, 2)):
            swap = keys[one] > keys[two]
            keys[one], keys[two] = (
                jnp.minimum(keys[one], keys[two]), jnp.maximum(keys[one], keys[two])
            )
            for item in sides_of:
                item[one], item[two] = (
                    jnp.where(swap, item[two], item[one]),
                    jnp.where(swap, item[one], item[two]),
                )
        for number in range(4):
            bounds_at[number, place] = keys[number]
            planes[2 + number, place] = sides_of[0][number]
            planes[6 + number, place] = sides_of[1][number]

    line = iota((PAD, lanes), 0)
    first_line, last_line = line == 0, line == PAD - 1

    def part_step(part, carry):
        for tile in range(rows // PAD):
            place = slice(tile * PAD, (tile + 1) * PAD)
            keys = [bounds_at[number, place] for number in range(4)] + [limits[0, place]]
            keys = [jnp.maximum(key, 0.0) for key in keys]
            sums = []
            for start in (0, 1):
                line_of = [planes[start, place]]
                for number in range(3, -1, -1):
                    line_of.append(line_of[-1] - planes[2 + 4 * start + number, place])
                sums.append(line_of)
            for t in range(size):
                level = part * size + t
                height = level.astype(jnp.float32)
                changes = [0.0, 0.0]
                for side in range(5):
                    open_side = height < keys[4 - side]
                    changes = [
                        jnp.where(open_side, sums[number][side], changes[number])
                        for number in range(2)
                    ]
                for out, values, number in ((east_out, east, 0), (north_out, north, 1)):
                    change = changes[number]
                    result = values[level, place] + thickness[level] * change
                    if tile == 0:
                        fix = fixes[3 + number, pl.ds(level, 1), :]
                        result = result + jnp.where(first_line, fix, 0.0)
                    if tile == rows // PAD - 1:
                        fix = fixes[number, pl.ds(level, 1), :]
                        result = result + jnp.where(last_line, fix, 0.0)
                    out[level, place] = result
        part_copy(0, part).start()
        part_copy(1, part).start()
        return carry

    lax.fori_loop(0, OUT_PARTS, part_step, 0)
    tracer_copy.wait()
    for part in range(OUT_PARTS):
        part_copy(0, part).wait()
        part_copy(1, part).wait()


def swaps(lats, lons, odd):
    pairs = []
    for lat in range(lats):
        for lon in range(lons):
            other = lat + 1 if lat % 2 == odd else lat - 1
            if other < 0:
                pairs.append((lon, (lon ^ 1) % lons))
            elif other == lats:
                pairs.append((lat * lons + lon, lat * lons + lons - 1 - lon))
            else:
                pairs.append((lat * lons + lon, other * lons + lon))
    return pairs


def lon_swaps(lons, odd):
    return [(lon, (lon + (1 if lon % 2 == odd else -1)) % lons) for lon in range(lons)]


def local(
    tracer_cot, east_cot, north_cot, surface_cot, depth_levels, diffusivity, coriolis, storage,
    thickness,
):
    levels, rows, lanes = tracer_cot.shape
    lats, lons = lax.axis_size("lat"), lax.axis_size("lon")
    far = lambda value: pltpu.with_memory_space_constraint(value, pltpu.HBM)
    near = lambda value: pltpu.with_memory_space_constraint(value, pltpu.VMEM)
    floats = lambda *shape: pltpu.HBM(shape, jnp.float32)
    scratch = lambda *shape: pltpu.VMEM(shape, jnp.float32)
    scalars = pl.BlockSpec(memory_space=pltpu.SMEM)
    in_hbm = pl.BlockSpec(memory_space=pltpu.HBM)
    in_vmem = pl.BlockSpec(memory_space=pltpu.VMEM)
    params = pltpu.CompilerParams(vmem_limit_bytes=VMEM_BYTES)
    cost = lambda work: pl.CostEstimate(
        flops=work * levels * rows * lanes, bytes_accessed=8 * levels * rows * lanes,
        transcendentals=0,
    )
    plane, pair, field = (rows, lanes), (rows, 2 * lanes), (levels, rows, lanes)
    columns = (rows + rows // 2, lanes)
    full = (rows + 2 * PAD, 2 * lanes)
    message, strips = (MESSAGE_ROWS, lanes), (2, HALO_ROWS, 2 * lanes)

    message_0, message_1, planes, edge_rows, edges, east, north, tracer = pl.pallas_call(
        pack_kernel,
        in_specs=[in_hbm] * 8,
        out_specs=[in_vmem] * 8,
        out_shape=[
            scratch(*columns), scratch(*columns), scratch(5, *plane), scratch(6, *plane),
            scratch(3, *plane), scratch(*field), scratch(*field), scratch(*field),
        ],
        scratch_shapes=[
            pltpu.VMEM(plane, jnp.int32), scratch(*plane), scratch(*plane), scratch(*plane),
            scratch(2, *plane), pltpu.SemaphoreType.DMA((3, PARTS)), pltpu.SemaphoreType.DMA((5,)),
        ],
        compiler_params=params,
        name="pack",
    )(
        *[
            far(item)
            for item in (
                east_cot, north_cot, tracer_cot, depth_levels, storage, surface_cot, diffusivity,
                coriolis,
            )
        ]
    )

    got_1 = lax.ppermute(message_1, "lon", lon_swaps(lons, 0))
    got_0 = lax.ppermute(message_0, "lon", lon_swaps(lons, 1))

    east_part, north_part, tracer_part = pl.pallas_call(
        inner_kernel,
        in_specs=[in_vmem] * 4,
        out_specs=[in_vmem] * 3,
        out_shape=[scratch(*field)] * 3,
        scratch_shapes=[scratch(4, *plane), scratch(2, *plane)],
        compiler_params=params,
        cost_estimate=cost(60),
        name="inner",
    )(near(planes), near(east), near(north), near(tracer))

    edges, east_part = lax.optimization_barrier((edges, east_part))
    got_0, got_1 = near(got_0), near(got_1)
    wide, face_west, message_a, message_b = pl.pallas_call(
        stitch_kernel,
        in_specs=[in_vmem] * 5,
        out_specs=[in_vmem] * 4,
        out_shape=[scratch(4, *pair), scratch(*plane), scratch(*message), scratch(*message)],
        compiler_params=params,
        name="stitch",
    )(got_0, got_1, near(planes), near(edge_rows), near(edges))

    got_b = lax.ppermute(message_b, BOTH, swaps(lats, lons, 1))
    got_a = lax.ppermute(message_a, BOTH, swaps(lats, lons, 0))

    east_part, north_part, tracer_part, limits, faces = pl.pallas_call(
        rim_kernel,
        in_specs=[in_vmem] * 9,
        out_specs=[in_vmem] * 5,
        out_shape=[scratch(*field)] * 3 + [scratch(5, *plane), scratch(4, *plane)],
        scratch_shapes=[scratch(3, *plane)],
        input_output_aliases={6: 0, 7: 1, 8: 2},
        compiler_params=params,
        cost_estimate=cost(10),
        name="rim",
    )(
        got_0, got_1, near(wide), near(planes), near(face_west), near(edges), near(east_part),
        near(north_part), near(tracer_part),
    )

    wide, east_part = lax.optimization_barrier((wide, east_part))
    gram, basis, fixes, tracer_part, limits, faces = pl.pallas_call(
        basis_kernel,
        in_specs=[scalars] + [in_vmem] * 7,
        out_specs=[in_vmem] * 6,
        out_shape=[
            scratch(lats * lons, lanes), scratch(4, *full), scratch(6, LEVEL_ROWS, lanes),
            scratch(*field), scratch(5, *plane), scratch(4, *plane),
        ],
        scratch_shapes=[scratch(*strips)],
        input_output_aliases={5: 3, 6: 4, 7: 5},
        compiler_params=params,
        name="basis",
    )(
        thickness, near(got_a), near(got_b), near(wide), near(edge_rows), near(tracer_part),
        near(limits), near(faces),
    )

    totals = lax.all_to_all(gram, BOTH, 0, 0, tiled=True)

    tracer_adj, east_adj, north_adj, surface_adj = pl.pallas_call(
        final_kernel,
        in_specs=[scalars] + [in_vmem] * 9,
        out_specs=[in_hbm] * 3 + [in_vmem],
        out_shape=[floats(*field)] * 3 + [jax.ShapeDtypeStruct(plane, jnp.float32)],
        scratch_shapes=[
            scratch(10, *plane), scratch(4, *plane), scratch(rows + 2 * PAD, lanes), scratch(*field), scratch(*field),
            pltpu.SemaphoreType.DMA((2, OUT_PARTS)), pltpu.SemaphoreType.DMA,
        ],
        compiler_params=params,
        name="final",
    )(
        thickness, near(totals), near(basis), near(planes), near(limits), near(faces), near(fixes),
        near(east_part), near(north_part), near(tracer_part),
    )
    return tracer_adj, east_adj, north_adj, surface_adj


def solution(mesh):
    field, plane = P(None, "lat", "lon"), P("lat", "lon")
    return jax.shard_map(
        local,
        mesh=mesh,
        in_specs=(field, field, field, plane, plane, plane, plane, plane, P()),
        out_specs=(field, field, field, plane),
        check_vma=False,
    )
```

```python
import jax
import jax.numpy as jnp
from jax import lax
from jax.experimental import pallas as pl
from jax.experimental.pallas import tpu as pltpu
from jax.sharding import PartitionSpec as P

WIDE = 6
PAD = 8
SHIFTS = (1.0, 0.3, 1.7)
PARTS = 5
OUT_PARTS = 5
LANES = 128
GROUP = 5
TILES = 8
BOTH = ("lat", "lon")
VMEM_BYTES = 32 * 1024 * 1024

DEPTH_AT, STORE_AT, SOURCE_AT, STRIP_AT, DIFF_AT = 100, 106, 112, 118, 124
LEVEL_ROWS = 56
RAW_AT = 3 * PAD
PAIR_AT = RAW_AT + LEVEL_ROWS
HALO_ROWS = PAIR_AT + LEVEL_ROWS
SIDES_AT = HALO_ROWS + LEVEL_ROWS
MESSAGE_ROWS = SIDES_AT + PAD
SIDE_GROUPS = PAIR_AT // PAD


def iota(shape, dim):
    return lax.broadcasted_iota(jnp.int32, shape, dim)


def turn(values, shift, dim):
    return pltpu.roll(values, shift % values.shape[dim], dim)


def pack_kernel(
    east_in, north_in, tracer_in, depth_in, storage_in, surf_in, diff_in, spin_in,
    message_0, message_1, planes, rows_out, edges, east, north, tracer,
    depth, surf, px, py, bounds, field_sems, plane_sems,
):
    levels, rows, lanes = east.shape
    size = levels // PARTS
    sources, fields = (east_in, north_in, tracer_in), (east, north, tracer)

    def part_copy(number, part):
        place = pl.ds(part * size, size)
        return pltpu.make_async_copy(
            sources[number].at[place], fields[number].at[place], field_sems.at[number, part]
        )

    moves = [
        pltpu.make_async_copy(source, target, plane_sems.at[number])
        for number, (source, target) in enumerate(
            (
                (depth_in, depth), (storage_in, planes.at[1]), (surf_in, surf),
                (diff_in, planes.at[2]), (spin_in, planes.at[4]),
            )
        )
    ]
    for move in moves:
        move.start()
    for part in range(PARTS):
        for number in range(3):
            part_copy(number, part).start(priority=min(part, 1))
    rows_out[:, levels - levels % PAD :] = jnp.zeros((6, rows - levels + levels % PAD, lanes), jnp.float32)
    px[...] = jnp.zeros((rows, lanes), jnp.float32)
    py[...] = jnp.zeros((rows, lanes), jnp.float32)
    edges[...] = jnp.zeros((3, rows, lanes), jnp.float32)
    for move in moves:
        move.wait()
    lane = iota((rows, lanes), 1)
    row = iota((rows, lanes), 0)
    deep = depth[...].astype(jnp.float32)
    planes[0] = deep
    bounds[0] = jnp.where(lane == lanes - 1, 0.0, jnp.minimum(deep, turn(deep, -1, 1)))
    bounds[1] = jnp.where(row == rows - 1, 0.0, jnp.minimum(deep, turn(deep, -1, 0)))
    pair_lane = lax.shift_right_logical(iota((PAD, lanes), 1), 1)

    for part in range(PARTS):
        for number in range(3):
            part_copy(number, part).wait()
        for t in range(size):
            level = part * size + t
            for number, ref in enumerate(fields):
                rows_out[number, level : level + 1, :] = ref[level, rows - 1 : rows, :]
                rows_out[3 + number, level : level + 1, :] = ref[level, 0:1, :]
        for tile in range(rows // PAD):
            place = slice(tile * PAD, (tile + 1) * PAD)
            sum_x, sum_y = px[place], py[place]
            limit_x, limit_y = bounds[0, place], bounds[1, place]
            ends = [edges[number, place] for number in range(3)]
            for t in range(size):
                level = part * size + t
                here = pair_lane == level
                values = [ref[level, place] for ref in fields]
                for number in range(3):
                    moved = turn(values[number], 2 * level + 1, 1)
                    ends[number] = jnp.where(here, moved, ends[number])
                sum_x = sum_x + jnp.where(limit_x > level, values[0], 0.0)
                sum_y = sum_y + jnp.where(limit_y > level, values[1], 0.0)
            px[place], py[place] = sum_x, sum_y
            for number in range(3):
                edges[number, place] = ends[number]

    plane = surf[...] + px[...] - turn(px[...], 1, 1) + py[...] - turn(py[...], 1, 0)
    planes[3] = plane
    odd_lane = lax.rem(lane, 2) == 1

    def put(target, values, start, place, count):
        moved = turn(values, place - start, 1)
        return jnp.where((lane >= place) & (lane < place + count), moved, target)

    half = rows // 2

    def fill(ref, eastward):
        if eastward:
            tile = jnp.where(odd_lane, turn(edges[1], 1, 1), edges[0])
            ref[rows:] = jnp.where(odd_lane[half:], turn(edges[2, half:], 1, 1), edges[2, :half])
        else:
            tile = jnp.where(odd_lane, edges[0], turn(edges[1], -1, 1))
            ref[rows:] = jnp.where(odd_lane[half:], edges[2, :half], turn(edges[2, half:], -1, 1))
        start = lanes - WIDE if eastward else 0
        for values, place in (
            (deep, DEPTH_AT), (planes[1], STORE_AT), (plane, SOURCE_AT), (rows_out[1], STRIP_AT)
        ):
            tile = put(tile, values, start, place, WIDE)
        ref[:rows] = put(tile, planes[2], lanes - 1, DIFF_AT, 1)

    odd = lax.rem(lax.axis_index("lon"), 2) == 1

    @pl.when(odd)
    def _():
        fill(message_0, True)
        fill(message_1, False)

    @pl.when(jnp.logical_not(odd))
    def _():
        fill(message_0, False)
        fill(message_1, True)


def received(got_0, got_1):
    odd = lax.rem(lax.axis_index("lon"), 2) == 1
    one, two = got_0[...], got_1[...]
    return jnp.where(odd, two, one), jnp.where(odd, one, two)


def stitch_kernel(
    got_0, got_1, planes, rows_in, edges,
    wide, face_west, message_a, message_b,
):
    rows, lanes = planes.shape[1:]
    from_west, from_east = received(got_0, got_1)
    lane = iota((rows, lanes), 1)
    left_tile, right_tile = from_west[:rows], from_east[:rows]

    def side(place):
        right = turn(right_tile, -place, 1)
        left = turn(left_tile, lanes - WIDE - place, 1)
        return jnp.where(lane < WIDE, right, jnp.where(lane >= lanes - WIDE, left, 0.0))

    deep, deep_side = planes[0], side(DEPTH_AT)
    store, store_side = planes[1], side(STORE_AT)
    plane, plane_side = planes[3], side(SOURCE_AT)
    strip = side(STRIP_AT)
    level = lax.shift_right_logical(lane, 1).astype(jnp.float32)
    even_lane = lax.rem(lane, 2) == 0

    def flux(values, bound):
        used = even_lane & (level < bound)
        return jnp.sum(jnp.where(used, values, 0.0), axis=1, keepdims=True)

    flux_east = flux(edges[0], jnp.minimum(deep[:, lanes - 1 :], deep_side[:, 0:1]))
    flux_west = flux(left_tile, jnp.minimum(deep_side[:, lanes - 1 :], deep[:, 0:1]))
    first, last = lane == 0, lane == lanes - 1
    plane = plane + jnp.where(last, flux_east, 0.0) - jnp.where(first, flux_west, 0.0)
    plane_side = plane_side - jnp.where(first, flux_east, 0.0) + jnp.where(last, flux_west, 0.0)
    both = ((deep, deep_side), (store, store_side), (plane, plane_side), (rows_in[1], strip))
    for number, (one, two) in enumerate(both):
        wide[number, :, :lanes] = one
        wide[number, :, lanes:] = two
    faces = planes[2]
    face_west[...] = jnp.where(first, turn(left_tile, -DIFF_AT, 1), turn(faces, 1, 1))

    small_lane = iota((PAD, lanes), 1)

    def fill(ref, up):
        start = rows - PAD if up else 0
        base = 0 if up else 3
        groups = [two[start : start + PAD] for _, two in both[:3]]
        groups = groups + [strip[i : i + PAD] for i in range(0, LEVEL_ROWS, PAD)]
        packed = jnp.zeros((PAD, lanes), jnp.float32)
        for number, item in enumerate(groups):
            place = 2 * WIDE * number
            here = (small_lane >= place) & (small_lane < place + 2 * WIDE)
            packed = jnp.where(here, turn(item, place + WIDE, 1), packed)
        for number, (one, _) in enumerate(both[:3]):
            ref[number * PAD : (number + 1) * PAD] = one[start : start + PAD]
        ref[RAW_AT:PAIR_AT] = rows_in[base + 1, :LEVEL_ROWS]
        ref[PAIR_AT:HALO_ROWS] = rows_in[base, :LEVEL_ROWS]
        ref[HALO_ROWS:SIDES_AT] = rows_in[base + 2, :LEVEL_ROWS]
        ref[SIDES_AT:] = packed
        if up:
            ref[PAIR_AT - 1 : PAIR_AT] = faces[rows - 1 :]

    even = lax.rem(lax.axis_index("lat"), 2) == 0

    @pl.when(even)
    def _():
        fill(message_a, True)
        fill(message_b, False)

    @pl.when(jnp.logical_not(even))
    def _():
        fill(message_a, False)
        fill(message_b, True)


def shifted(values):
    return turn(values, -1, 1), turn(values, 1, 1), turn(values, -1, 0), turn(values, 1, 0)


def face_planes(planes, limits, weights):
    deep, face = planes[0], planes[2]
    lane, row = iota(deep.shape, 1), iota(deep.shape, 0)
    rows, lanes = deep.shape
    edges = (lane == lanes - 1, lane == 0, row == rows - 1, row == 0)
    for number, (edge, values) in enumerate(zip(edges, shifted(deep))):
        limits[number] = jnp.where(edge, 0.0, jnp.minimum(deep, values))
    weights[0] = turn(face, 1, 1)
    weights[1] = turn(face, 1, 0)


def level_faces(level, place, planes, limits, weights):
    height = level.astype(jnp.float32)
    face = planes[2, place]
    return (
        height < planes[0, place],
        jnp.where(height < limits[0, place], face, 0.0),
        jnp.where(height < limits[1, place], weights[0, place], 0.0),
        jnp.where(height < limits[2, place], face, 0.0),
        jnp.where(height < limits[3, place], weights[1, place], 0.0),
    )


def smooth(ref, level, tile, tiles, faces):
    wet, face_east, face_west, face_north, face_south = faces
    start = tile * PAD
    item = ref[level, start : start + PAD]
    if tile + 1 < tiles:
        above = ref[level, start + 1 : start + 1 + PAD]
    else:
        above = turn(item, -1, 0)
    below = ref[level, start - 1 : start - 1 + PAD] if tile else turn(item, 1, 0)
    change = face_north * (above - item) + face_south * (below - item)
    change = change + face_east * (turn(item, -1, 1) - item)
    change = change + face_west * (turn(item, 1, 1) - item)
    return item, jnp.where(wet, item, 0.0) + change


def inner_kernel(
    planes, east, north, tracer, east_out, north_out, tracer_out, limits, weights
):
    levels, rows, lanes = tracer.shape
    tiles = rows // PAD
    face_planes(planes, limits, weights)
    for first in range(0, tiles, TILES):

        def step(group, carry):
            for t in range(GROUP):
                level = group * GROUP + t
                for tile in range(first, first + TILES):
                    place = slice(tile * PAD, (tile + 1) * PAD)
                    faces = level_faces(level, place, planes, limits, weights)
                    one, new_one = smooth(east, level, tile, tiles, faces)
                    two, new_two = smooth(north, level, tile, tiles, faces)
                    spin = jnp.where(faces[0], planes[4, place], 0.0)
                    east_out[level, place] = new_one - spin * two
                    north_out[level, place] = new_two + spin * one
                    tracer_out[level, place] = smooth(tracer, level, tile, tiles, faces)[1]
            return carry

        lax.fori_loop(0, levels // GROUP, step, 0)


def rim_kernel(
    thickness, got_0, got_1, wide, planes, face_west, edges, east, north, tracer,
    east_out, north_out, tracer_out, limits, faces, depths,
    sides,
):
    levels, rows, lanes = east.shape
    from_west, from_east = received(got_0, got_1)
    lane = iota((rows, lanes), 1)
    deep, beside = wide[0, :, :lanes], wide[0, :, lanes:]
    level_of = lax.shift_right_logical(lane, 1).astype(jnp.float32)
    odd_lane = lax.rem(lane, 2) == 1
    place = iota((PAD, lanes), 1)
    table = jnp.zeros((PAD, lanes), jnp.float32)
    for number in range(levels):
        table = table + jnp.where(place > number, thickness[number], 0.0)
    depths[...] = table
    limits[0] = deep
    limits[1] = jnp.minimum(deep, jnp.where(lane == lanes - 1, beside[:, 0:1], turn(deep, -1, 1)))
    limits[2] = jnp.minimum(deep, jnp.where(lane == 0, beside[:, lanes - 1 :], turn(deep, 1, 1)))
    limits[3] = jnp.minimum(deep, turn(deep, -1, 0))
    limits[4] = jnp.minimum(deep, turn(deep, 1, 0))
    faces[0] = planes[2]
    faces[1] = face_west[...]
    faces[2] = planes[2]
    faces[3] = turn(planes[2], 1, 0)
    bound_east = jnp.minimum(deep[:, lanes - 1 :], beside[:, 0:1])
    bound_west = jnp.minimum(deep[:, 0:1], beside[:, lanes - 1 :])
    weight = jnp.where(odd_lane, face_west[:, 0:1], planes[2, :, lanes - 1 :])
    weight = jnp.where(level_of < jnp.where(odd_lane, bound_west, bound_east), weight, 0.0)
    left, right = from_west[:rows], from_east[:rows]
    left_half, right_half = from_west[rows:], from_east[rows:]
    half = odd_lane[: rows // 2]
    halos = (
        jnp.where(odd_lane, turn(left, 1, 1), turn(right, -1, 1)),
        jnp.where(odd_lane, left, right),
        jnp.concatenate(
            [
                jnp.where(half, turn(left_half, 1, 1), turn(right_half, -1, 1)),
                jnp.where(half, left_half, right_half),
            ],
            axis=0,
        ),
    )
    for number in range(3):
        sides[number] = turn(weight * (halos[number] - edges[number]), -1, 1)
    small_lane = iota((PAD, lanes), 1)
    rim = (small_lane == 0) | (small_lane == lanes - 1)
    tiles = rows // PAD
    pairs = ((east, east_out), (north, north_out), (tracer, tracer_out))
    for first in range(0, tiles, TILES):
        chunk = range(first, first + TILES)

        def step(group, rims):
            for t in range(GROUP):
                level = group * GROUP + t
                for number, tile in enumerate(chunk):
                    place = slice(tile * PAD, (tile + 1) * PAD)
                    for index, (source, target) in enumerate(pairs):
                        part = turn(rims[3 * number + index], -2 * t, 1)
                        target[level, place] = source[level, place] + jnp.where(rim, part, 0.0)
            return tuple(turn(item, -2 * GROUP, 1) for item in rims)

        lax.fori_loop(
            0, levels // GROUP, step,
            tuple(
                sides[number, tile * PAD : (tile + 1) * PAD] for tile in chunk for number in range(3)
            ),
        )


def basis_kernel(
    depths, got_a, got_b, wide, rows_in, tracer_in, limits_in, faces_in,
    gram, basis, fixes, tracer, limits, faces,
    halo, work,
):
    rows, lanes = wide.shape[1], wide.shape[2] // 2
    lat = lax.axis_index("lat")
    even = lax.rem(lat, 2) == 0
    at_top = lat == lax.axis_size("lat") - 1
    at_bottom = lat == 0

    one, two = got_a[...], got_b[...]
    small_lane = iota((PAD, lanes), 1)
    near_side = (small_lane < WIDE) | (small_lane >= lanes - WIDE)

    def tiles_of(values, number):
        start = number * PAD
        first = values[start : start + PAD]
        if number < SIDE_GROUPS:
            second = turn(values[SIDES_AT:], -2 * WIDE * number - WIDE, 1)
            second = jnp.where(near_side, second, 0.0)
        else:
            start = start + LEVEL_ROWS
            second = values[start : start + PAD]
        return first, second

    groups = range(HALO_ROWS // PAD)
    above = jnp.where(even, one, two)

    @pl.when(at_top)
    def _():
        back = lanes - 1 - small_lane
        for number in groups:
            for tile, values in enumerate(tiles_of(above, number)):
                values = jnp.take_along_axis(values, back, axis=1)
                if number < 3:
                    values = jnp.concatenate(
                        [values[i : i + 1] for i in range(PAD - 1, -1, -1)], axis=0
                    )
                halo[0, number * PAD : (number + 1) * PAD, tile * lanes : (tile + 1) * lanes] = values

    @pl.when(jnp.logical_not(at_top))
    def _():
        for number in groups:
            for tile, values in enumerate(tiles_of(above, number)):
                halo[0, number * PAD : (number + 1) * PAD, tile * lanes : (tile + 1) * lanes] = values

    below = jnp.where(at_bottom, 0.0, jnp.where(even, two, one))
    for number in groups:
        for tile, values in enumerate(tiles_of(below, number)):
            halo[1, number * PAD : (number + 1) * PAD, tile * lanes : (tile + 1) * lanes] = values

    def whole(number):
        place = slice(number * PAD, (number + 1) * PAD)
        return jnp.concatenate([halo[1, place], wide[number], halo[0, place]], axis=0)

    deep, store, plane = whole(0), whole(1), whole(2)
    full = deep.shape
    row = iota(full, 0)
    core_end = PAD + rows
    level = iota((LEVEL_ROWS, full[1]), 0).astype(jnp.float32)
    bound = jnp.minimum(deep[core_end - 1 : core_end], deep[core_end : core_end + 1])
    edge = wide[3, :LEVEL_ROWS] - jnp.where(at_top, halo[0, RAW_AT:PAIR_AT], 0.0)
    flux = jnp.sum(jnp.where(level < bound, edge, 0.0), axis=0, keepdims=True)
    plane = plane + jnp.where(row == core_end - 1, flux, 0.0) - jnp.where(row == core_end, flux, 0.0)
    bound = jnp.minimum(deep[PAD - 1 : PAD], deep[PAD : PAD + 1])
    flux = jnp.sum(jnp.where(level < bound, halo[1, RAW_AT:PAIR_AT], 0.0), axis=0, keepdims=True)
    plane = plane + jnp.where(row == PAD - 1, flux, 0.0) - jnp.where(row == PAD, flux, 0.0)

    table = depths[...]

    def column(bound):
        index = bound.astype(jnp.int32)
        return jnp.concatenate(
            [
                jnp.concatenate(
                    [
                        jnp.take_along_axis(
                            table, index[i : i + PAD, j : j + lanes], axis=1
                        )
                        for j in range(0, full[1], lanes)
                    ],
                    axis=1,
                )
                for i in range(0, full[0], PAD)
            ],
            axis=0,
        )

    beside, _, above, _ = shifted(deep)
    to_east = column(jnp.minimum(deep, beside))
    to_north = column(jnp.minimum(deep, above))
    to_north = jnp.where(at_top & (row == core_end - 1), 2.0, 1.0) * to_north
    to_west, to_south = turn(to_east, 1, 1), turn(to_north, 1, 0)
    diag = store + to_east + to_west + to_north + to_south
    there = diag > 0.0
    inverse = jnp.where(there, 1.0 / jnp.where(there, diag, 1.0), 0.0)

    def operate(values):
        for tile in range(2):
            work[tile, PAD : PAD + full[0]] = values[:, tile * lanes : (tile + 1) * lanes]
        north_side, south_side = [
            jnp.concatenate([work[tile, start : start + full[0]] for tile in range(2)], axis=1)
            for start in (PAD + 1, PAD - 1)
        ]
        east_side, west_side = turn(values, -1, 1), turn(values, 1, 1)
        total = (
            store * values + to_east * (values - east_side) + to_west * (values - west_side)
        )
        return total + to_north * (values - north_side) + to_south * (values - south_side)

    for start in (0, PAD + full[0]):
        work[:, start : start + PAD] = jnp.zeros((2, PAD, lanes), jnp.float32)
    vectors, images = [plane * inverse], []
    for number in range(4):
        images.append(operate(vectors[-1]))
        if number < 3:
            vectors.append(images[-1] * inverse - SHIFTS[number] * vectors[-1])
    for number in range(4):
        basis[number] = vectors[number]

    def core(values):
        return values[PAD:core_end, :lanes]

    sums = []
    for i in range(4):
        for j in range(i, 4):
            sums.append(core(vectors[i]) * core(images[j]))
    for i in range(4):
        sums.append(core(vectors[i]) * core(plane))
    sums = [jnp.sum(item, axis=0, keepdims=True) for item in sums]
    sums = sums + [jnp.zeros((1, lanes), jnp.float32)] * (16 - len(sums))
    sums = jnp.sum(jnp.concatenate(sums, axis=0), axis=1, keepdims=True)
    same = iota((16, lanes), 0) == iota((16, lanes), 1)
    line = jnp.sum(jnp.where(same, sums, 0.0), axis=0, keepdims=True)
    gram[...] = jnp.broadcast_to(line, gram.shape)

    level = level[:, :lanes]
    top_face = faces_in[2, rows - 1 :] + jnp.where(at_top, halo[0, PAIR_AT - 1 : PAIR_AT, :lanes], 0.0)
    low_face = halo[1, PAIR_AT - 1 : PAIR_AT, :lanes]
    for side, line, weight in ((0, core_end - 1, top_face), (1, PAD, low_face)):
        other = line + 1 - 2 * side
        bound = jnp.minimum(deep[line : line + 1], deep[other : other + 1])[:, :lanes]
        limits[3 + side, line - PAD : line - PAD + 1] = bound
        faces[2 + side, line - PAD : line - PAD + 1] = weight
        outer = (
            halo[side, PAIR_AT:, :lanes],
            halo[side, RAW_AT:PAIR_AT, :lanes],
            halo[side, PAIR_AT:, lanes:],
        )
        for number in range(3):
            inner = rows_in[3 * side + number, :LEVEL_ROWS]
            fixes[3 * side + number] = jnp.where(
                level < bound, weight * (outer[number] - inner), 0.0
            )
    for number in range(tracer.shape[0]):
        last = tracer_in[number, rows - 1 : rows] + fixes[2, number : number + 1]
        first = tracer_in[number, 0:1] + fixes[5, number : number + 1]
        tracer[number, rows - 1 : rows] = last
        tracer[number, 0:1] = first


def solve(line):
    entry = [jnp.broadcast_to(line[:, i : i + 1], line.shape) for i in range(14)]
    system = [[None] * 5 for _ in range(4)]
    for i in range(4):
        for j in range(i, 4):
            system[i][j] = entry.pop(0)
    for i in range(4):
        system[i][4] = entry.pop(0)
    factor, part = {}, []
    for k in range(4):
        pivot = system[k][k]
        usable = pivot > 0.0
        scale = jnp.where(usable, 1.0 / jnp.where(usable, pivot, 1.0), 0.0)
        part.append(system[k][4] * scale)
        for i in range(k + 1, 4):
            factor[i, k] = system[k][i] * scale
            for j in range(i, 5):
                system[i][j] = system[i][j] - factor[i, k] * system[k][j]
    for k in range(2, -1, -1):
        for i in range(k + 1, 4):
            part[k] = part[k] - factor[i, k] * part[i]
    return part


def final_kernel(
    thickness, totals, basis, planes_in, limits, faces, fixes, east, north, tracer,
    tracer_hbm, east_hbm, north_hbm, surface,
    planes, bounds_at, work, east_out, north_out, sems, tracer_sem,
):
    levels, rows, lanes = east.shape
    size = levels // OUT_PARTS
    core_end = PAD + rows
    outs = ((east_out, east_hbm), (north_out, north_hbm))

    def part_copy(number, part):
        place = pl.ds(part * size, size)
        source, target = outs[number]
        return pltpu.make_async_copy(source.at[place], target.at[place], sems.at[number, part])

    tracer_copy = pltpu.make_async_copy(tracer, tracer_hbm, tracer_sem)
    tracer_copy.start()
    at_top = lax.axis_index("lat") == lax.axis_size("lat") - 1
    parts = solve(jnp.sum(totals[...], axis=0, keepdims=True))
    tall = (rows + 2 * PAD, lanes)
    lane, row = iota(tall, 1), iota(tall, 0)

    def combine(start):
        total = parts[0] * basis[0, :, start : start + lanes]
        for number in range(1, 4):
            total = total + parts[number] * basis[number, :, start : start + lanes]
        return total

    inner, outer = combine(0), combine(lanes)
    surface[...] = planes_in[1] * inner[PAD:core_end]

    def to_east(first, second):
        return jnp.where(lane[: first.shape[0]] == lanes - 1, turn(second, -1, 1), turn(first, -1, 1))

    def to_west(first, second):
        return jnp.where(lane[: first.shape[0]] == 0, turn(second, 1, 1), turn(first, 1, 1))

    end = slice(core_end, core_end + PAD)
    fold = at_top & (row[:PAD] == 0)

    def slopes(first, second):
        along = to_east(first, second)
        across = turn(first, -1, 0)
        along_end = jnp.where(fold, to_west(first[end], second[end]), along[end])
        across_end = jnp.where(fold, turn(first, 1, 0)[end], across[end])
        along = jnp.concatenate([along[:core_end], along_end], axis=0)
        across = jnp.concatenate([across[:core_end], across_end], axis=0)
        return along - first, across - first

    inner_x, inner_y = slopes(inner, outer)
    outer_x, outer_y = slopes(outer, inner)
    core = slice(PAD, core_end)
    spin = planes_in[4]
    planes[0] = inner_x[core] - spin * inner_y[core]
    planes[1] = inner_y[core] + spin * inner_x[core]
    for start, first, second in ((2, inner_x, outer_x), (6, inner_y, outer_y)):
        work[...] = first
        own = first[core]
        sides = (
            to_east(own, second[core]), to_west(own, second[core]),
            work[PAD + 1 : core_end + 1], work[PAD - 1 : core_end - 1],
        )
        for number, item in enumerate(sides):
            planes[start + number] = faces[number] * (own - item)

    for tile in range(rows // PAD):
        place = slice(tile * PAD, (tile + 1) * PAD)
        keys = [limits[1 + number, place] for number in range(4)]
        sides_of = [[planes[start + number, place] for number in range(4)] for start in (2, 6)]
        for one, two in ((0, 1), (2, 3), (0, 2), (1, 3), (1, 2)):
            swap = keys[one] > keys[two]
            keys[one], keys[two] = (
                jnp.minimum(keys[one], keys[two]), jnp.maximum(keys[one], keys[two])
            )
            for item in sides_of:
                item[one], item[two] = (
                    jnp.where(swap, item[two], item[one]),
                    jnp.where(swap, item[one], item[two]),
                )
        for number in range(4):
            bounds_at[number, place] = keys[number]
            planes[2 + number, place] = sides_of[0][number]
            planes[6 + number, place] = sides_of[1][number]

    line = iota((PAD, lanes), 0)
    first_line, last_line = line == 0, line == PAD - 1

    def part_step(part, carry):
        for tile in range(rows // PAD):
            place = slice(tile * PAD, (tile + 1) * PAD)
            keys = [bounds_at[number, place] for number in range(4)] + [limits[0, place]]
            keys = [jnp.maximum(key, 0.0) for key in keys]
            sums = []
            for start in (0, 1):
                line_of = [planes[start, place]]
                for number in range(3, -1, -1):
                    line_of.append(line_of[-1] - planes[2 + 4 * start + number, place])
                sums.append(line_of)
            for t in range(size):
                level = part * size + t
                height = level.astype(jnp.float32)
                changes = [0.0, 0.0]
                for side in range(5):
                    open_side = height < keys[4 - side]
                    changes = [
                        jnp.where(open_side, sums[number][side], changes[number])
                        for number in range(2)
                    ]
                for out, values, number in ((east_out, east, 0), (north_out, north, 1)):
                    change = changes[number]
                    result = values[level, place] + thickness[level] * change
                    if tile == 0:
                        fix = fixes[3 + number, pl.ds(level, 1), :]
                        result = result + jnp.where(first_line, fix, 0.0)
                    if tile == rows // PAD - 1:
                        fix = fixes[number, pl.ds(level, 1), :]
                        result = result + jnp.where(last_line, fix, 0.0)
                    out[level, place] = result
        part_copy(0, part).start()
        part_copy(1, part).start()
        return carry

    lax.fori_loop(0, OUT_PARTS, part_step, 0)
    tracer_copy.wait()
    for part in range(OUT_PARTS):
        part_copy(0, part).wait()
        part_copy(1, part).wait()


def swaps(lats, lons, odd):
    pairs = []
    for lat in range(lats):
        for lon in range(lons):
            other = lat + 1 if lat % 2 == odd else lat - 1
            if other < 0:
                pairs.append((lon, (lon ^ 1) % lons))
            elif other == lats:
                pairs.append((lat * lons + lon, lat * lons + lons - 1 - lon))
            else:
                pairs.append((lat * lons + lon, other * lons + lon))
    return pairs


def lon_swaps(lons, odd):
    return [(lon, (lon + (1 if lon % 2 == odd else -1)) % lons) for lon in range(lons)]


def local(
    tracer_cot, east_cot, north_cot, surface_cot, depth_levels, diffusivity, coriolis, storage,
    thickness,
):
    levels, rows, lanes = tracer_cot.shape
    lats, lons = lax.axis_size("lat"), lax.axis_size("lon")
    far = lambda value: pltpu.with_memory_space_constraint(value, pltpu.HBM)
    near = lambda value: pltpu.with_memory_space_constraint(value, pltpu.VMEM)
    floats = lambda *shape: pltpu.HBM(shape, jnp.float32)
    scratch = lambda *shape: pltpu.VMEM(shape, jnp.float32)
    scalars = pl.BlockSpec(memory_space=pltpu.SMEM)
    in_hbm = pl.BlockSpec(memory_space=pltpu.HBM)
    in_vmem = pl.BlockSpec(memory_space=pltpu.VMEM)
    params = pltpu.CompilerParams(vmem_limit_bytes=VMEM_BYTES)
    cost = lambda work: pl.CostEstimate(
        flops=work * levels * rows * lanes, bytes_accessed=8 * levels * rows * lanes,
        transcendentals=0,
    )
    plane, pair, field = (rows, lanes), (rows, 2 * lanes), (levels, rows, lanes)
    columns = (rows + rows // 2, lanes)
    full = (rows + 2 * PAD, 2 * lanes)
    message, strips = (MESSAGE_ROWS, lanes), (2, HALO_ROWS, 2 * lanes)

    message_0, message_1, planes, edge_rows, edges, east, north, tracer = pl.pallas_call(
        pack_kernel,
        in_specs=[in_hbm] * 8,
        out_specs=[in_vmem] * 8,
        out_shape=[
            scratch(*columns), scratch(*columns), scratch(5, *plane), scratch(6, *plane),
            scratch(3, *plane), scratch(*field), scratch(*field), scratch(*field),
        ],
        scratch_shapes=[
            pltpu.VMEM(plane, jnp.int32), scratch(*plane), scratch(*plane), scratch(*plane),
            scratch(2, *plane), pltpu.SemaphoreType.DMA((3, PARTS)), pltpu.SemaphoreType.DMA((5,)),
        ],
        compiler_params=params,
        name="pack",
    )(
        *[
            far(item)
            for item in (
                east_cot, north_cot, tracer_cot, depth_levels, storage, surface_cot, diffusivity,
                coriolis,
            )
        ]
    )

    got_1 = lax.ppermute(message_1, "lon", lon_swaps(lons, 0))
    got_0 = lax.ppermute(message_0, "lon", lon_swaps(lons, 1))

    east_part, north_part, tracer_part = pl.pallas_call(
        inner_kernel,
        in_specs=[in_vmem] * 4,
        out_specs=[in_vmem] * 3,
        out_shape=[scratch(*field)] * 3,
        scratch_shapes=[scratch(4, *plane), scratch(2, *plane)],
        compiler_params=params,
        cost_estimate=cost(60),
        name="inner",
    )(near(planes), near(east), near(north), near(tracer))

    edges, east_part = lax.optimization_barrier((edges, east_part))
    got_0, got_1 = near(got_0), near(got_1)
    wide, face_west, message_a, message_b = pl.pallas_call(
        stitch_kernel,
        in_specs=[in_vmem] * 5,
        out_specs=[in_vmem] * 4,
        out_shape=[scratch(4, *pair), scratch(*plane), scratch(*message), scratch(*message)],
        compiler_params=params,
        name="stitch",
    )(got_0, got_1, near(planes), near(edge_rows), near(edges))

    got_b = lax.ppermute(message_b, BOTH, swaps(lats, lons, 1))
    got_a = lax.ppermute(message_a, BOTH, swaps(lats, lons, 0))

    east_part, north_part, tracer_part, limits, faces, depths = pl.pallas_call(
        rim_kernel,
        in_specs=[scalars] + [in_vmem] * 9,
        out_specs=[in_vmem] * 6,
        out_shape=[scratch(*field)] * 3
        + [scratch(5, *plane), scratch(4, *plane), scratch(PAD, lanes)],
        scratch_shapes=[scratch(3, *plane)],
        input_output_aliases={7: 0, 8: 1, 9: 2},
        compiler_params=params,
        cost_estimate=cost(10),
        name="rim",
    )(
        thickness, got_0, got_1, near(wide), near(planes), near(face_west), near(edges), near(east_part),
        near(north_part), near(tracer_part),
    )

    wide, east_part = lax.optimization_barrier((wide, east_part))
    gram, basis, fixes, tracer_part, limits, faces = pl.pallas_call(
        basis_kernel,
        in_specs=[in_vmem] * 8,
        out_specs=[in_vmem] * 6,
        out_shape=[
            scratch(lats * lons, lanes), scratch(4, *full), scratch(6, LEVEL_ROWS, lanes),
            scratch(*field), scratch(5, *plane), scratch(4, *plane),
        ],
        scratch_shapes=[scratch(*strips), scratch(2, rows + 4 * PAD, lanes)],
        input_output_aliases={5: 3, 6: 4, 7: 5},
        compiler_params=params,
        name="basis",
    )(
        near(depths), near(got_a), near(got_b), near(wide), near(edge_rows), near(tracer_part),
        near(limits), near(faces),
    )

    totals = lax.all_to_all(gram, BOTH, 0, 0, tiled=True)

    tracer_adj, east_adj, north_adj, surface_adj = pl.pallas_call(
        final_kernel,
        in_specs=[scalars] + [in_vmem] * 9,
        out_specs=[in_hbm] * 3 + [in_vmem],
        out_shape=[floats(*field)] * 3 + [jax.ShapeDtypeStruct(plane, jnp.float32)],
        scratch_shapes=[
            scratch(10, *plane), scratch(4, *plane), scratch(rows + 2 * PAD, lanes), scratch(*field), scratch(*field),
            pltpu.SemaphoreType.DMA((2, OUT_PARTS)), pltpu.SemaphoreType.DMA,
        ],
        compiler_params=params,
        name="final",
    )(
        thickness, near(totals), near(basis), near(planes), near(limits), near(faces), near(fixes),
        near(east_part), near(north_part), near(tracer_part),
    )
    return tracer_adj, east_adj, north_adj, surface_adj


def solution(mesh):
    field, plane = P(None, "lat", "lon"), P("lat", "lon")
    return jax.shard_map(
        local,
        mesh=mesh,
        in_specs=(field, field, field, plane, plane, plane, plane, plane, P()),
        out_specs=(field, field, field, plane),
        check_vma=False,
    )
```

```python
import jax
import jax.numpy as jnp
from jax import lax
from jax.experimental import pallas as pl
from jax.experimental.pallas import tpu as pltpu
from jax.sharding import PartitionSpec as P

WIDE = 6
PAD = 8
SHIFTS = (1.0, 0.3, 1.7)
PARTS = 5
OUT_PARTS = 5
LANES = 128
GROUP = 5
TILES = 8
BOTH = ("lat", "lon")
VMEM_BYTES = 32 * 1024 * 1024

DEPTH_AT, STORE_AT, SOURCE_AT, STRIP_AT, DIFF_AT = 100, 106, 112, 118, 124
LEVEL_ROWS = 56
RAW_AT = 3 * PAD
PAIR_AT = RAW_AT + LEVEL_ROWS
HALO_ROWS = PAIR_AT + LEVEL_ROWS
SIDES_AT = HALO_ROWS + LEVEL_ROWS
MESSAGE_ROWS = SIDES_AT + PAD
SIDE_GROUPS = PAIR_AT // PAD


def iota(shape, dim):
    return lax.broadcasted_iota(jnp.int32, shape, dim)


def turn(values, shift, dim):
    return pltpu.roll(values, shift % values.shape[dim], dim)


def pack_kernel(
    east_in, north_in, tracer_in, depth_in, storage_in, surf_in, diff_in, spin_in,
    message_0, message_1, planes, rows_out, edges, east, north, tracer,
    depth, surf, px, py, bounds, field_sems, plane_sems,
):
    levels, rows, lanes = east.shape
    size = levels // PARTS
    sources, fields = (east_in, north_in, tracer_in), (east, north, tracer)

    def part_copy(number, part):
        place = pl.ds(part * size, size)
        return pltpu.make_async_copy(
            sources[number].at[place], fields[number].at[place], field_sems.at[number, part]
        )

    moves = [
        pltpu.make_async_copy(source, target, plane_sems.at[number])
        for number, (source, target) in enumerate(
            (
                (depth_in, depth), (storage_in, planes.at[1]), (surf_in, surf),
                (diff_in, planes.at[2]), (spin_in, planes.at[4]),
            )
        )
    ]
    for move in moves:
        move.start()
    for part in range(PARTS):
        for number in range(3):
            part_copy(number, part).start(priority=min(part, 1))
    rows_out[:, levels - levels % PAD :] = jnp.zeros((6, rows - levels + levels % PAD, lanes), jnp.float32)
    px[...] = jnp.zeros((rows, lanes), jnp.float32)
    py[...] = jnp.zeros((rows, lanes), jnp.float32)
    edges[...] = jnp.zeros((3, rows, lanes), jnp.float32)
    for move in moves:
        move.wait()
    lane = iota((rows, lanes), 1)
    row = iota((rows, lanes), 0)
    deep = depth[...].astype(jnp.float32)
    planes[0] = deep
    bounds[0] = jnp.where(lane == lanes - 1, 0.0, jnp.minimum(deep, turn(deep, -1, 1)))
    bounds[1] = jnp.where(row == rows - 1, 0.0, jnp.minimum(deep, turn(deep, -1, 0)))
    pair_lane = lax.shift_right_logical(iota((PAD, lanes), 1), 1)

    for part in range(PARTS):
        for number in range(3):
            part_copy(number, part).wait()
        for t in range(size):
            level = part * size + t
            for number, ref in enumerate(fields):
                rows_out[number, level : level + 1, :] = ref[level, rows - 1 : rows, :]
                rows_out[3 + number, level : level + 1, :] = ref[level, 0:1, :]
        for tile in range(rows // PAD):
            place = slice(tile * PAD, (tile + 1) * PAD)
            sum_x, sum_y = px[place], py[place]
            limit_x, limit_y = bounds[0, place], bounds[1, place]
            ends = [edges[number, place] for number in range(3)]
            for t in range(size):
                level = part * size + t
                here = pair_lane == level
                values = [ref[level, place] for ref in fields]
                for number in range(3):
                    moved = turn(values[number], 2 * level + 1, 1)
                    ends[number] = jnp.where(here, moved, ends[number])
                sum_x = sum_x + jnp.where(limit_x > level, values[0], 0.0)
                sum_y = sum_y + jnp.where(limit_y > level, values[1], 0.0)
            px[place], py[place] = sum_x, sum_y
            for number in range(3):
                edges[number, place] = ends[number]

    plane = surf[...] + px[...] - turn(px[...], 1, 1) + py[...] - turn(py[...], 1, 0)
    planes[3] = plane
    odd_lane = lax.rem(lane, 2) == 1

    def put(target, values, start, place, count):
        moved = turn(values, place - start, 1)
        return jnp.where((lane >= place) & (lane < place + count), moved, target)

    half = rows // 2

    def fill(ref, eastward):
        if eastward:
            tile = jnp.where(odd_lane, turn(edges[1], 1, 1), edges[0])
            ref[rows:] = jnp.where(odd_lane[half:], turn(edges[2, half:], 1, 1), edges[2, :half])
        else:
            tile = jnp.where(odd_lane, edges[0], turn(edges[1], -1, 1))
            ref[rows:] = jnp.where(odd_lane[half:], edges[2, :half], turn(edges[2, half:], -1, 1))
        start = lanes - WIDE if eastward else 0
        for values, place in (
            (deep, DEPTH_AT), (planes[1], STORE_AT), (plane, SOURCE_AT), (rows_out[1], STRIP_AT)
        ):
            tile = put(tile, values, start, place, WIDE)
        ref[:rows] = put(tile, planes[2], lanes - 1, DIFF_AT, 1)

    odd = lax.rem(lax.axis_index("lon"), 2) == 1

    @pl.when(odd)
    def _():
        fill(message_0, True)
        fill(message_1, False)

    @pl.when(jnp.logical_not(odd))
    def _():
        fill(message_0, False)
        fill(message_1, True)


def received(got_0, got_1):
    odd = lax.rem(lax.axis_index("lon"), 2) == 1
    one, two = got_0[...], got_1[...]
    return jnp.where(odd, two, one), jnp.where(odd, one, two)


def stitch_kernel(
    got_0, got_1, planes, rows_in, edges,
    wide, face_west, message_a, message_b,
):
    rows, lanes = planes.shape[1:]
    from_west, from_east = received(got_0, got_1)
    lane = iota((rows, lanes), 1)
    left_tile, right_tile = from_west[:rows], from_east[:rows]

    def side(place):
        right = turn(right_tile, -place, 1)
        left = turn(left_tile, lanes - WIDE - place, 1)
        return jnp.where(lane < WIDE, right, jnp.where(lane >= lanes - WIDE, left, 0.0))

    deep, deep_side = planes[0], side(DEPTH_AT)
    store, store_side = planes[1], side(STORE_AT)
    plane, plane_side = planes[3], side(SOURCE_AT)
    strip = side(STRIP_AT)
    level = lax.shift_right_logical(lane, 1).astype(jnp.float32)
    even_lane = lax.rem(lane, 2) == 0

    def flux(values, bound):
        used = even_lane & (level < bound)
        return jnp.sum(jnp.where(used, values, 0.0), axis=1, keepdims=True)

    flux_east = flux(edges[0], jnp.minimum(deep[:, lanes - 1 :], deep_side[:, 0:1]))
    flux_west = flux(left_tile, jnp.minimum(deep_side[:, lanes - 1 :], deep[:, 0:1]))
    first, last = lane == 0, lane == lanes - 1
    plane = plane + jnp.where(last, flux_east, 0.0) - jnp.where(first, flux_west, 0.0)
    plane_side = plane_side - jnp.where(first, flux_east, 0.0) + jnp.where(last, flux_west, 0.0)
    both = ((deep, deep_side), (store, store_side), (plane, plane_side), (rows_in[1], strip))
    for number, (one, two) in enumerate(both):
        wide[number, :, :lanes] = one
        wide[number, :, lanes:] = two
    faces = planes[2]
    face_west[...] = jnp.where(first, turn(left_tile, -DIFF_AT, 1), turn(faces, 1, 1))

    small_lane = iota((PAD, lanes), 1)

    def fill(ref, up):
        start = rows - PAD if up else 0
        base = 0 if up else 3
        groups = [two[start : start + PAD] for _, two in both[:3]]
        groups = groups + [strip[i : i + PAD] for i in range(0, LEVEL_ROWS, PAD)]
        packed = jnp.zeros((PAD, lanes), jnp.float32)
        for number, item in enumerate(groups):
            place = 2 * WIDE * number
            here = (small_lane >= place) & (small_lane < place + 2 * WIDE)
            packed = jnp.where(here, turn(item, place + WIDE, 1), packed)
        for number, (one, _) in enumerate(both[:3]):
            ref[number * PAD : (number + 1) * PAD] = one[start : start + PAD]
        ref[RAW_AT:PAIR_AT] = rows_in[base + 1, :LEVEL_ROWS]
        ref[PAIR_AT:HALO_ROWS] = rows_in[base, :LEVEL_ROWS]
        ref[HALO_ROWS:SIDES_AT] = rows_in[base + 2, :LEVEL_ROWS]
        ref[SIDES_AT:] = packed
        if up:
            ref[PAIR_AT - 1 : PAIR_AT] = faces[rows - 1 :]

    even = lax.rem(lax.axis_index("lat"), 2) == 0

    @pl.when(even)
    def _():
        fill(message_a, True)
        fill(message_b, False)

    @pl.when(jnp.logical_not(even))
    def _():
        fill(message_a, False)
        fill(message_b, True)


def shifted(values):
    return turn(values, -1, 1), turn(values, 1, 1), turn(values, -1, 0), turn(values, 1, 0)


def face_planes(planes, limits, weights):
    deep, face = planes[0], planes[2]
    lane, row = iota(deep.shape, 1), iota(deep.shape, 0)
    rows, lanes = deep.shape
    edges = (lane == lanes - 1, lane == 0, row == rows - 1, row == 0)
    for number, (edge, values) in enumerate(zip(edges, shifted(deep))):
        limits[number] = jnp.where(edge, 0.0, jnp.minimum(deep, values))
    weights[0] = turn(face, 1, 1)
    weights[1] = turn(face, 1, 0)


def level_faces(level, place, planes, limits, weights):
    height = level.astype(jnp.float32)
    face = planes[2, place]
    return (
        height < planes[0, place],
        jnp.where(height < limits[0, place], face, 0.0),
        jnp.where(height < limits[1, place], weights[0, place], 0.0),
        jnp.where(height < limits[2, place], face, 0.0),
        jnp.where(height < limits[3, place], weights[1, place], 0.0),
    )


def smooth(ref, level, tile, tiles, faces):
    wet, face_east, face_west, face_north, face_south = faces
    start = tile * PAD
    item = ref[level, start : start + PAD]
    if tile + 1 < tiles:
        above = ref[level, start + 1 : start + 1 + PAD]
    else:
        above = turn(item, -1, 0)
    below = ref[level, start - 1 : start - 1 + PAD] if tile else turn(item, 1, 0)
    change = face_north * (above - item) + face_south * (below - item)
    change = change + face_east * (turn(item, -1, 1) - item)
    change = change + face_west * (turn(item, 1, 1) - item)
    return item, jnp.where(wet, item, 0.0) + change


def inner_kernel(
    planes, east, north, tracer, east_out, north_out, tracer_out, limits, weights
):
    levels, rows, lanes = tracer.shape
    tiles = rows // PAD
    face_planes(planes, limits, weights)
    for first in range(0, tiles, TILES):

        def step(group, carry):
            for t in range(GROUP):
                level = group * GROUP + t
                for tile in range(first, first + TILES):
                    place = slice(tile * PAD, (tile + 1) * PAD)
                    faces = level_faces(level, place, planes, limits, weights)
                    one, new_one = smooth(east, level, tile, tiles, faces)
                    two, new_two = smooth(north, level, tile, tiles, faces)
                    spin = jnp.where(faces[0], planes[4, place], 0.0)
                    east_out[level, place] = new_one - spin * two
                    north_out[level, place] = new_two + spin * one
                    tracer_out[level, place] = smooth(tracer, level, tile, tiles, faces)[1]
            return carry

        lax.fori_loop(0, levels // GROUP, step, 0)


def rim_kernel(
    thickness, got_0, got_1, wide, planes, face_west, edges, east, north, tracer,
    east_out, north_out, tracer_out, limits, faces, depths,
    sides,
):
    levels, rows, lanes = east.shape
    from_west, from_east = received(got_0, got_1)
    lane = iota((rows, lanes), 1)
    deep, beside = wide[0, :, :lanes], wide[0, :, lanes:]
    level_of = lax.shift_right_logical(lane, 1).astype(jnp.float32)
    odd_lane = lax.rem(lane, 2) == 1
    place = iota((PAD, lanes), 1)
    table = jnp.zeros((PAD, lanes), jnp.float32)
    for number in range(levels):
        table = table + jnp.where(place > number, thickness[number], 0.0)
    depths[...] = table
    limits[0] = deep
    limits[1] = jnp.minimum(deep, jnp.where(lane == lanes - 1, beside[:, 0:1], turn(deep, -1, 1)))
    limits[2] = jnp.minimum(deep, jnp.where(lane == 0, beside[:, lanes - 1 :], turn(deep, 1, 1)))
    limits[3] = jnp.minimum(deep, turn(deep, -1, 0))
    limits[4] = jnp.minimum(deep, turn(deep, 1, 0))
    faces[0] = planes[2]
    faces[1] = face_west[...]
    faces[2] = planes[2]
    faces[3] = turn(planes[2], 1, 0)
    bound_east = jnp.minimum(deep[:, lanes - 1 :], beside[:, 0:1])
    bound_west = jnp.minimum(deep[:, 0:1], beside[:, lanes - 1 :])
    weight = jnp.where(odd_lane, face_west[:, 0:1], planes[2, :, lanes - 1 :])
    weight = jnp.where(level_of < jnp.where(odd_lane, bound_west, bound_east), weight, 0.0)
    left, right = from_west[:rows], from_east[:rows]
    left_half, right_half = from_west[rows:], from_east[rows:]
    half = odd_lane[: rows // 2]
    halos = (
        jnp.where(odd_lane, turn(left, 1, 1), turn(right, -1, 1)),
        jnp.where(odd_lane, left, right),
        jnp.concatenate(
            [
                jnp.where(half, turn(left_half, 1, 1), turn(right_half, -1, 1)),
                jnp.where(half, left_half, right_half),
            ],
            axis=0,
        ),
    )
    for number in range(3):
        sides[number] = turn(weight * (halos[number] - edges[number]), -1, 1)
    small_lane = iota((PAD, lanes), 1)
    rim = (small_lane == 0) | (small_lane == lanes - 1)
    tiles = rows // PAD
    pairs = ((east, east_out), (north, north_out), (tracer, tracer_out))
    for first in range(0, tiles, TILES):
        chunk = range(first, first + TILES)

        def step(group, rims):
            for t in range(GROUP):
                level = group * GROUP + t
                for number, tile in enumerate(chunk):
                    place = slice(tile * PAD, (tile + 1) * PAD)
                    for index, (source, target) in enumerate(pairs):
                        part = turn(rims[3 * number + index], -2 * t, 1)
                        target[level, place] = source[level, place] + jnp.where(rim, part, 0.0)
            return tuple(turn(item, -2 * GROUP, 1) for item in rims)

        lax.fori_loop(
            0, levels // GROUP, step,
            tuple(
                sides[number, tile * PAD : (tile + 1) * PAD] for tile in chunk for number in range(3)
            ),
        )


def basis_kernel(
    depths, got_a, got_b, wide, rows_in, tracer_in, limits_in, faces_in,
    gram, basis, fixes, tracer, limits, faces,
    halo, work,
):
    rows, lanes = wide.shape[1], wide.shape[2] // 2
    lat = lax.axis_index("lat")
    even = lax.rem(lat, 2) == 0
    at_top = lat == lax.axis_size("lat") - 1
    at_bottom = lat == 0

    one, two = got_a[...], got_b[...]
    small_lane = iota((PAD, lanes), 1)
    near_side = (small_lane < WIDE) | (small_lane >= lanes - WIDE)

    def tiles_of(values, number):
        start = number * PAD
        first = values[start : start + PAD]
        if number < SIDE_GROUPS:
            second = turn(values[SIDES_AT:], -2 * WIDE * number - WIDE, 1)
            second = jnp.where(near_side, second, 0.0)
        else:
            start = start + LEVEL_ROWS
            second = values[start : start + PAD]
        return first, second

    groups = range(HALO_ROWS // PAD)
    above = jnp.where(even, one, two)

    @pl.when(at_top)
    def _():
        back = lanes - 1 - small_lane
        for number in groups:
            for tile, values in enumerate(tiles_of(above, number)):
                values = jnp.take_along_axis(values, back, axis=1)
                if number < 3:
                    values = jnp.concatenate(
                        [values[i : i + 1] for i in range(PAD - 1, -1, -1)], axis=0
                    )
                halo[0, number * PAD : (number + 1) * PAD, tile * lanes : (tile + 1) * lanes] = values

    @pl.when(jnp.logical_not(at_top))
    def _():
        for number in groups:
            for tile, values in enumerate(tiles_of(above, number)):
                halo[0, number * PAD : (number + 1) * PAD, tile * lanes : (tile + 1) * lanes] = values

    below = jnp.where(at_bottom, 0.0, jnp.where(even, two, one))
    for number in groups:
        for tile, values in enumerate(tiles_of(below, number)):
            halo[1, number * PAD : (number + 1) * PAD, tile * lanes : (tile + 1) * lanes] = values

    def whole(number):
        place = slice(number * PAD, (number + 1) * PAD)
        return jnp.concatenate([halo[1, place], wide[number], halo[0, place]], axis=0)

    deep, store, plane = whole(0), whole(1), whole(2)
    full = deep.shape
    row = iota(full, 0)
    core_end = PAD + rows
    level = iota((LEVEL_ROWS, full[1]), 0).astype(jnp.float32)
    bound = jnp.minimum(deep[core_end - 1 : core_end], deep[core_end : core_end + 1])
    edge = wide[3, :LEVEL_ROWS] - jnp.where(at_top, halo[0, RAW_AT:PAIR_AT], 0.0)
    flux = jnp.sum(jnp.where(level < bound, edge, 0.0), axis=0, keepdims=True)
    plane = plane + jnp.where(row == core_end - 1, flux, 0.0) - jnp.where(row == core_end, flux, 0.0)
    bound = jnp.minimum(deep[PAD - 1 : PAD], deep[PAD : PAD + 1])
    flux = jnp.sum(jnp.where(level < bound, halo[1, RAW_AT:PAIR_AT], 0.0), axis=0, keepdims=True)
    plane = plane + jnp.where(row == PAD - 1, flux, 0.0) - jnp.where(row == PAD, flux, 0.0)

    table = depths[...]

    def column(bound):
        index = bound.astype(jnp.int32)
        return jnp.concatenate(
            [
                jnp.concatenate(
                    [
                        jnp.take_along_axis(
                            table, index[i : i + PAD, j : j + lanes], axis=1
                        )
                        for j in range(0, full[1], lanes)
                    ],
                    axis=1,
                )
                for i in range(0, full[0], PAD)
            ],
            axis=0,
        )

    beside, _, above, _ = shifted(deep)
    to_east = column(jnp.minimum(deep, beside))
    to_north = column(jnp.minimum(deep, above))
    to_north = jnp.where(at_top & (row == core_end - 1), 2.0, 1.0) * to_north
    to_west, to_south = turn(to_east, 1, 1), turn(to_north, 1, 0)
    diag = store + to_east + to_west + to_north + to_south
    there = diag > 0.0
    inverse = jnp.where(there, 1.0 / jnp.where(there, diag, 1.0), 0.0)

    def operate(values):
        for tile in range(2):
            work[tile, PAD : PAD + full[0]] = values[:, tile * lanes : (tile + 1) * lanes]
        north_side, south_side = [
            jnp.concatenate([work[tile, start : start + full[0]] for tile in range(2)], axis=1)
            for start in (PAD + 1, PAD - 1)
        ]
        east_side, west_side = turn(values, -1, 1), turn(values, 1, 1)
        total = (
            store * values + to_east * (values - east_side) + to_west * (values - west_side)
        )
        return total + to_north * (values - north_side) + to_south * (values - south_side)

    for start in (0, PAD + full[0]):
        work[:, start : start + PAD] = jnp.zeros((2, PAD, lanes), jnp.float32)
    vectors, images = [plane * inverse], []
    for number in range(4):
        images.append(operate(vectors[-1]))
        if number < 3:
            vectors.append(images[-1] * inverse - SHIFTS[number] * vectors[-1])
    for number in range(4):
        basis[number] = vectors[number]

    def core(values):
        return values[PAD:core_end, :lanes]

    sums = []
    for i in range(4):
        for j in range(i, 4):
            sums.append(core(vectors[i]) * core(images[j]))
    for i in range(4):
        sums.append(core(vectors[i]) * core(plane))
    sums = [jnp.sum(item, axis=0, keepdims=True) for item in sums]
    sums = sums + [jnp.zeros((1, lanes), jnp.float32)] * (16 - len(sums))
    sums = jnp.sum(jnp.concatenate(sums, axis=0), axis=1, keepdims=True)
    same = iota((16, lanes), 0) == iota((16, lanes), 1)
    line = jnp.sum(jnp.where(same, sums, 0.0), axis=0, keepdims=True)
    gram[...] = jnp.broadcast_to(line, gram.shape)

    level = level[:, :lanes]
    top_face = faces_in[2, rows - 1 :] + jnp.where(at_top, halo[0, PAIR_AT - 1 : PAIR_AT, :lanes], 0.0)
    low_face = halo[1, PAIR_AT - 1 : PAIR_AT, :lanes]
    for side, line, weight in ((0, core_end - 1, top_face), (1, PAD, low_face)):
        other = line + 1 - 2 * side
        bound = jnp.minimum(deep[line : line + 1], deep[other : other + 1])[:, :lanes]
        limits[3 + side, line - PAD : line - PAD + 1] = bound
        faces[2 + side, line - PAD : line - PAD + 1] = weight
        outer = (
            halo[side, PAIR_AT:, :lanes],
            halo[side, RAW_AT:PAIR_AT, :lanes],
            halo[side, PAIR_AT:, lanes:],
        )
        for number in range(3):
            inner = rows_in[3 * side + number, :LEVEL_ROWS]
            fixes[3 * side + number] = jnp.where(
                level < bound, weight * (outer[number] - inner), 0.0
            )
    for number in range(tracer.shape[0]):
        last = tracer_in[number, rows - 1 : rows] + fixes[2, number : number + 1]
        first = tracer_in[number, 0:1] + fixes[5, number : number + 1]
        tracer[number, rows - 1 : rows] = last
        tracer[number, 0:1] = first


def solve(line):
    entry = [jnp.broadcast_to(line[:, i : i + 1], line.shape) for i in range(14)]
    system = [[None] * 5 for _ in range(4)]
    for i in range(4):
        for j in range(i, 4):
            system[i][j] = entry.pop(0)
    for i in range(4):
        system[i][4] = entry.pop(0)
    factor, part = {}, []
    for k in range(4):
        pivot = system[k][k]
        usable = pivot > 0.0
        scale = jnp.where(usable, 1.0 / jnp.where(usable, pivot, 1.0), 0.0)
        part.append(system[k][4] * scale)
        for i in range(k + 1, 4):
            factor[i, k] = system[k][i] * scale
            for j in range(i, 5):
                system[i][j] = system[i][j] - factor[i, k] * system[k][j]
    for k in range(2, -1, -1):
        for i in range(k + 1, 4):
            part[k] = part[k] - factor[i, k] * part[i]
    return part


def final_kernel(
    thickness, totals, basis, planes_in, limits, faces, fixes, east, north, tracer,
    tracer_hbm, east_hbm, north_hbm, surface,
    planes, bounds_at, work, east_out, north_out, sems, tracer_sem,
):
    levels, rows, lanes = east.shape
    size = levels // OUT_PARTS
    core_end = PAD + rows
    outs = ((east_out, east_hbm), (north_out, north_hbm))

    def part_copy(number, part):
        place = pl.ds(part * size, size)
        source, target = outs[number]
        return pltpu.make_async_copy(source.at[place], target.at[place], sems.at[number, part])

    tracer_copy = pltpu.make_async_copy(tracer, tracer_hbm, tracer_sem)
    tracer_copy.start()
    at_top = lax.axis_index("lat") == lax.axis_size("lat") - 1
    parts = solve(jnp.sum(totals[...], axis=0, keepdims=True))
    tall = (rows + 2 * PAD, lanes)
    lane, row = iota(tall, 1), iota(tall, 0)

    def combine(start):
        total = parts[0] * basis[0, :, start : start + lanes]
        for number in range(1, 4):
            total = total + parts[number] * basis[number, :, start : start + lanes]
        return total

    inner, outer = combine(0), combine(lanes)
    surface[...] = planes_in[1] * inner[PAD:core_end]

    def to_east(first, second):
        return jnp.where(lane[: first.shape[0]] == lanes - 1, turn(second, -1, 1), turn(first, -1, 1))

    def to_west(first, second):
        return jnp.where(lane[: first.shape[0]] == 0, turn(second, 1, 1), turn(first, 1, 1))

    end = slice(core_end, core_end + PAD)
    fold = at_top & (row[:PAD] == 0)

    def slopes(first, second):
        along = to_east(first, second)
        work[: rows + 2 * PAD] = first
        across = work[1 : rows + 2 * PAD + 1]
        along_end = jnp.where(fold, to_west(first[end], second[end]), along[end])
        across_end = jnp.where(fold, work[core_end - 1 : core_end + PAD - 1], across[end])
        along = jnp.concatenate([along[:core_end], along_end], axis=0)
        across = jnp.concatenate([across[:core_end], across_end], axis=0)
        return along - first, across - first

    work[rows + 2 * PAD :] = jnp.zeros((PAD, lanes), jnp.float32)
    inner_x, inner_y = slopes(inner, outer)
    outer_x, outer_y = slopes(outer, inner)
    core = slice(PAD, core_end)
    spin = planes_in[4]
    planes[0] = inner_x[core] - spin * inner_y[core]
    planes[1] = inner_y[core] + spin * inner_x[core]
    for start, first, second in ((2, inner_x, outer_x), (6, inner_y, outer_y)):
        work[: rows + 2 * PAD] = first
        own = first[core]
        sides = (
            to_east(own, second[core]), to_west(own, second[core]),
            work[PAD + 1 : core_end + 1], work[PAD - 1 : core_end - 1],
        )
        for number, item in enumerate(sides):
            planes[start + number] = faces[number] * (own - item)

    for tile in range(rows // PAD):
        place = slice(tile * PAD, (tile + 1) * PAD)
        keys = [limits[1 + number, place] for number in range(4)]
        sides_of = [[planes[start + number, place] for number in range(4)] for start in (2, 6)]
        for one, two in ((0, 1), (2, 3), (0, 2), (1, 3), (1, 2)):
            swap = keys[one] > keys[two]
            keys[one], keys[two] = (
                jnp.minimum(keys[one], keys[two]), jnp.maximum(keys[one], keys[two])
            )
            for item in sides_of:
                item[one], item[two] = (
                    jnp.where(swap, item[two], item[one]),
                    jnp.where(swap, item[one], item[two]),
                )
        for number in range(4):
            bounds_at[number, place] = keys[number]
            planes[2 + number, place] = sides_of[0][number]
            planes[6 + number, place] = sides_of[1][number]

    line = iota((PAD, lanes), 0)
    first_line, last_line = line == 0, line == PAD - 1

    def part_step(part, carry):
        for tile in range(rows // PAD):
            place = slice(tile * PAD, (tile + 1) * PAD)
            keys = [bounds_at[number, place] for number in range(4)] + [limits[0, place]]
            keys = [jnp.maximum(key, 0.0) for key in keys]
            sums = []
            for start in (0, 1):
                line_of = [planes[start, place]]
                for number in range(3, -1, -1):
                    line_of.append(line_of[-1] - planes[2 + 4 * start + number, place])
                sums.append(line_of)
            for t in range(size):
                level = part * size + t
                height = level.astype(jnp.float32)
                changes = [0.0, 0.0]
                for side in range(5):
                    open_side = height < keys[4 - side]
                    changes = [
                        jnp.where(open_side, sums[number][side], changes[number])
                        for number in range(2)
                    ]
                for out, values, number in ((east_out, east, 0), (north_out, north, 1)):
                    change = changes[number]
                    result = values[level, place] + thickness[level] * change
                    if tile == 0:
                        fix = fixes[3 + number, pl.ds(level, 1), :]
                        result = result + jnp.where(first_line, fix, 0.0)
                    if tile == rows // PAD - 1:
                        fix = fixes[number, pl.ds(level, 1), :]
                        result = result + jnp.where(last_line, fix, 0.0)
                    out[level, place] = result
        part_copy(0, part).start()
        part_copy(1, part).start()
        return carry

    lax.fori_loop(0, OUT_PARTS, part_step, 0)
    tracer_copy.wait()
    for part in range(OUT_PARTS):
        part_copy(0, part).wait()
        part_copy(1, part).wait()


def swaps(lats, lons, odd):
    pairs = []
    for lat in range(lats):
        for lon in range(lons):
            other = lat + 1 if lat % 2 == odd else lat - 1
            if other < 0:
                pairs.append((lon, (lon ^ 1) % lons))
            elif other == lats:
                pairs.append((lat * lons + lon, lat * lons + lons - 1 - lon))
            else:
                pairs.append((lat * lons + lon, other * lons + lon))
    return pairs


def lon_swaps(lons, odd):
    return [(lon, (lon + (1 if lon % 2 == odd else -1)) % lons) for lon in range(lons)]


def local(
    tracer_cot, east_cot, north_cot, surface_cot, depth_levels, diffusivity, coriolis, storage,
    thickness,
):
    levels, rows, lanes = tracer_cot.shape
    lats, lons = lax.axis_size("lat"), lax.axis_size("lon")
    far = lambda value: pltpu.with_memory_space_constraint(value, pltpu.HBM)
    near = lambda value: pltpu.with_memory_space_constraint(value, pltpu.VMEM)
    floats = lambda *shape: pltpu.HBM(shape, jnp.float32)
    scratch = lambda *shape: pltpu.VMEM(shape, jnp.float32)
    scalars = pl.BlockSpec(memory_space=pltpu.SMEM)
    in_hbm = pl.BlockSpec(memory_space=pltpu.HBM)
    in_vmem = pl.BlockSpec(memory_space=pltpu.VMEM)
    params = pltpu.CompilerParams(vmem_limit_bytes=VMEM_BYTES)
    cost = lambda work: pl.CostEstimate(
        flops=work * levels * rows * lanes, bytes_accessed=8 * levels * rows * lanes,
        transcendentals=0,
    )
    plane, pair, field = (rows, lanes), (rows, 2 * lanes), (levels, rows, lanes)
    columns = (rows + rows // 2, lanes)
    full = (rows + 2 * PAD, 2 * lanes)
    message, strips = (MESSAGE_ROWS, lanes), (2, HALO_ROWS, 2 * lanes)

    message_0, message_1, planes, edge_rows, edges, east, north, tracer = pl.pallas_call(
        pack_kernel,
        in_specs=[in_hbm] * 8,
        out_specs=[in_vmem] * 8,
        out_shape=[
            scratch(*columns), scratch(*columns), scratch(5, *plane), scratch(6, *plane),
            scratch(3, *plane), scratch(*field), scratch(*field), scratch(*field),
        ],
        scratch_shapes=[
            pltpu.VMEM(plane, jnp.int32), scratch(*plane), scratch(*plane), scratch(*plane),
            scratch(2, *plane), pltpu.SemaphoreType.DMA((3, PARTS)), pltpu.SemaphoreType.DMA((5,)),
        ],
        compiler_params=params,
        name="pack",
    )(
        *[
            far(item)
            for item in (
                east_cot, north_cot, tracer_cot, depth_levels, storage, surface_cot, diffusivity,
                coriolis,
            )
        ]
    )

    got_1 = lax.ppermute(message_1, "lon", lon_swaps(lons, 0))
    got_0 = lax.ppermute(message_0, "lon", lon_swaps(lons, 1))

    east_part, north_part, tracer_part = pl.pallas_call(
        inner_kernel,
        in_specs=[in_vmem] * 4,
        out_specs=[in_vmem] * 3,
        out_shape=[scratch(*field)] * 3,
        scratch_shapes=[scratch(4, *plane), scratch(2, *plane)],
        compiler_params=params,
        cost_estimate=cost(60),
        name="inner",
    )(near(planes), near(east), near(north), near(tracer))

    edges, east_part = lax.optimization_barrier((edges, east_part))
    got_0, got_1 = near(got_0), near(got_1)
    wide, face_west, message_a, message_b = pl.pallas_call(
        stitch_kernel,
        in_specs=[in_vmem] * 5,
        out_specs=[in_vmem] * 4,
        out_shape=[scratch(4, *pair), scratch(*plane), scratch(*message), scratch(*message)],
        compiler_params=params,
        name="stitch",
    )(got_0, got_1, near(planes), near(edge_rows), near(edges))

    got_b = lax.ppermute(message_b, BOTH, swaps(lats, lons, 1))
    got_a = lax.ppermute(message_a, BOTH, swaps(lats, lons, 0))

    east_part, north_part, tracer_part, limits, faces, depths = pl.pallas_call(
        rim_kernel,
        in_specs=[scalars] + [in_vmem] * 9,
        out_specs=[in_vmem] * 6,
        out_shape=[scratch(*field)] * 3
        + [scratch(5, *plane), scratch(4, *plane), scratch(PAD, lanes)],
        scratch_shapes=[scratch(3, *plane)],
        input_output_aliases={7: 0, 8: 1, 9: 2},
        compiler_params=params,
        cost_estimate=cost(10),
        name="rim",
    )(
        thickness, got_0, got_1, near(wide), near(planes), near(face_west), near(edges), near(east_part),
        near(north_part), near(tracer_part),
    )

    wide, east_part = lax.optimization_barrier((wide, east_part))
    gram, basis, fixes, tracer_part, limits, faces = pl.pallas_call(
        basis_kernel,
        in_specs=[in_vmem] * 8,
        out_specs=[in_vmem] * 6,
        out_shape=[
            scratch(lats * lons, lanes), scratch(4, *full), scratch(6, LEVEL_ROWS, lanes),
            scratch(*field), scratch(5, *plane), scratch(4, *plane),
        ],
        scratch_shapes=[scratch(*strips), scratch(2, rows + 4 * PAD, lanes)],
        input_output_aliases={5: 3, 6: 4, 7: 5},
        compiler_params=params,
        name="basis",
    )(
        near(depths), near(got_a), near(got_b), near(wide), near(edge_rows), near(tracer_part),
        near(limits), near(faces),
    )

    totals = lax.all_to_all(gram, BOTH, 0, 0, tiled=True)

    tracer_adj, east_adj, north_adj, surface_adj = pl.pallas_call(
        final_kernel,
        in_specs=[scalars] + [in_vmem] * 9,
        out_specs=[in_hbm] * 3 + [in_vmem],
        out_shape=[floats(*field)] * 3 + [jax.ShapeDtypeStruct(plane, jnp.float32)],
        scratch_shapes=[
            scratch(10, *plane), scratch(4, *plane), scratch(rows + 3 * PAD, lanes), scratch(*field), scratch(*field),
            pltpu.SemaphoreType.DMA((2, OUT_PARTS)), pltpu.SemaphoreType.DMA,
        ],
        compiler_params=params,
        name="final",
    )(
        thickness, near(totals), near(basis), near(planes), near(limits), near(faces), near(fixes),
        near(east_part), near(north_part), near(tracer_part),
    )
    return tracer_adj, east_adj, north_adj, surface_adj


def solution(mesh):
    field, plane = P(None, "lat", "lon"), P("lat", "lon")
    return jax.shard_map(
        local,
        mesh=mesh,
        in_specs=(field, field, field, plane, plane, plane, plane, plane, P()),
        out_specs=(field, field, field, plane),
        check_vma=False,
    )
```
